256 devices in a mesh: gx: 8 (over y, core), gy: 32 (over x, z).
Axes of the slice: x: 4, y: 4, z: 8, core: 2. Of those that a mesh axis runs over, the one named last changes fastest.
Arguments:
- forcing_field: float32 [64, 1024, 1024], P(None, 'gy', 'gx'), may hold values from -6 to 6
- innovations: float32 [524288, 64], P(('gx', 'gy')), may hold values from -6 to 6
- owner_device: int32 [524288, 1], P(('gx', 'gy')), may hold values from 0 to 255; in each aligned block of 2048 rows (0 to 2047, 2048 to 4095, ...) at most 16 rows name the same one
- column_index: int32 [524288], P(('gx', 'gy')), may hold values from 0 to 4095
- obs_weight: float32 [64, 64], replicated, may hold values from -0.75 to 0.75
- vert_inverse: float32 [64, 64], replicated, may hold values from -0.3 to 1.3
- vert_basis: float32 [64, 64], replicated, may hold values from -0.3 to 1.3
- vert_eigen: float32 [64], replicated, may hold values from 0.002 to 2
Outputs:
- pressure_adjoint: float32 [64, 1024, 1024], P(None, 'gy', 'gx')
The draws below stay inside these ranges and needn't reach their ends.
Inputs may be any that keep to these rules, and one draw needn't show every extreme that they name: `owner_device`: the rows of one device name any one owner at most 16 times.
All inputs are finite; a program needn't handle non-finite values.
Results may differ from the reference program's by a relative error of at most 0.00011.
Values sent between devices are 32-bit elements; how exact they have to be, the bound alone decides.
A program may use at most 64 MiB of HBM per device.

```python
import math
import jax
import jax.numpy as jnp
import numpy as np
from jax import lax

NX = 1024
NY = 1024
NZ = 64
ROWS_DEV = 2048
COLS_DEV = 4096
ROWS = 524288
CAP = 16
N_GX = 8
N_GY = 32
DEVICES = 256


def basis_like(key):
    noise = jax.random.truncated_normal(key, -3.0, 3.0, (NZ, NZ), jnp.float32)
    return jnp.eye(NZ, dtype=jnp.float32) + 0.6 * noise / 8.0


def draw_vert_inverse(key, part):
    key = jax.random.fold_in(key, 11)
    return basis_like(key)


def draw_vert_basis(key, part):
    key = jax.random.fold_in(key, 23)
    return basis_like(key)


def draw_vert_eigen(key, part):
    key = jax.random.fold_in(key, 37)
    value_key, place_key = jax.random.split(key)
    logs = jax.random.uniform(value_key, (NZ,), jnp.float32, jnp.log(0.0021), jnp.log(0.006))
    values = jnp.exp(logs)
    ranking = jax.random.permutation(place_key, NZ)
    levels = jnp.arange(NZ, dtype=jnp.int32)
    values = jnp.where(levels == ranking[0], 2.0, values)
    values = jnp.where(levels == ranking[1], 0.002, values)
    return values.astype(jnp.float32)


def touch_ends(entries, own_key, low, high):
    place = [jax.random.randint(jax.random.fold_in(own_key, axis), (), 0, length) for axis, length in enumerate(entries.shape)]
    main_axis = entries.shape.index(max(entries.shape))
    beside = place[:main_axis] + [(place[main_axis] + 1) % entries.shape[main_axis]] + place[main_axis + 1:]
    return entries.at[tuple(place)].set(low).at[tuple(beside)].set(high)


def block_levels(key, extent, cuts, low, top_value):
    def one(position, shards_of):
        heights = jax.random.uniform(jax.random.fold_in(jax.random.fold_in(key, 6), position), (shards_of,), jnp.float32, low / len(cuts), top_value / len(cuts))
        return jnp.repeat(jnp.exp(heights), extent[position] // shards_of).reshape((-1,) + (1,) * (len(extent) - position - 1))

    factor_of = one(*cuts[0])
    for cut in cuts[1:]:
        factor_of = factor_of * one(*cut)
    return factor_of


def shared_out(own_key, own, number, rows, number_of, top, reach, skew):
    order = jax.random.permutation(own_key, number_of)
    heavy_load, common = shares(number_of, rows * top, reach, skew, True), shares(number_of, rows * top, reach, skew, False)
    places = jnp.arange(number_of)

    def named(sizes, offset_by):
        used = int((sizes > 0).sum())
        fixed = max(1, used // 4)
        passed = fixed + (places - fixed + offset_by * (used - fixed)) % max(1, number_of - fixed)
        return jnp.zeros((number_of,), jnp.int32).at[order[jnp.where(places < fixed, places, passed)]].set(jnp.asarray(sizes, jnp.int32))

    sizes = jnp.where(number % 4 == 0, named(heavy_load, number // 4), named(common, number - number // 4 - 1))
    mixed = jax.random.permutation(jax.random.fold_in(own, 3), number_of)
    donor, taker = mixed[0:number_of // 2 * 2:2], mixed[1:number_of // 2 * 2:2]
    slack = jnp.minimum(sizes[donor] - 1, reach - sizes[taker]) // 2
    slack = jnp.where((donor == order[0]) | (taker == order[0]) | (sizes[taker] == 0), 0, jnp.maximum(slack, 0))
    passed = jax.random.randint(jax.random.fold_in(own, 4), (number_of // 2,), 0, 1 << 20) % (slack + 1)
    sizes = sizes.at[donor].add(-passed).at[taker].add(passed)
    items = jnp.searchsorted(jnp.cumsum(sizes), jnp.arange(rows * top), side="right").astype(jnp.int32)
    table = items.reshape(top, rows).T
    table = table[jax.random.permutation(jax.random.fold_in(own, 1), rows)]
    offset_by = jax.random.randint(jax.random.fold_in(own, 2), (rows, 1), 0, top)
    return jnp.take_along_axis(table, (jnp.arange(top)[None, :] + offset_by) % top, axis=1)


def shares(amount, total, most, slope, full):
    portions = [(1 << 20) // math.isqrt(rank ** slope) + 1 for rank in range(1, amount + 1)]
    largest = most if full else min(most, max(-(-total // amount), total * portions[0] // sum(portions)))
    least = 1 if total - largest >= amount - 1 else 0
    counts, spare = [largest] + [least] * (amount - 1), total - largest - least * (amount - 1)
    while spare > 0:
        movable = [i for i in range(1, amount) if counts[i] < largest] or [i for i in range(1, amount) if counts[i] < most]
        whole, budget = sum([portions[i] for i in movable]), spare
        for i in movable:
            addition = min(most - counts[i], max(1, budget * portions[i] // whole), spare)
            counts[i] = counts[i] + addition
            spare = spare - addition
    return np.array(counts)


def normal_values(rng, dims, width, limit, pieces=(), held_as=jnp.bfloat16):
    array = jax.random.normal(rng, dims, jnp.float32) * width
    if len(pieces) > 0:
        array = block_levels(rng, dims, pieces, -0.22, 0.18) * array
    return jnp.clip(array, min=-limit, max=limit).astype(held_as)


def setup_inputs(seed: int = 0) -> dict:
    seeds = jax.random.split(jax.random.key(seed), 9)
    forcing_field = normal_values(seeds[0], (NZ, NY, NX), 1.0, 6.0, ((1, 32), (2, 8)), jnp.float32)
    innovations = normal_values(seeds[1], (ROWS, NZ), 1.0, 6.0, ((0, 256),), jnp.float32)
    owner_device_keys = jax.random.split(jax.random.fold_in(seeds[2], 1), ROWS // ROWS_DEV)
    owner_device_turns = jax.random.permutation(jax.random.fold_in(seeds[2], 3), ROWS // ROWS_DEV)
    owner_device = jax.vmap(lambda own, number: shared_out(jax.random.fold_in(seeds[2], 2), own, number, ROWS_DEV, DEVICES, 1, CAP, 2))(owner_device_keys, owner_device_turns).reshape((ROWS, 1))
    column_index = touch_ends(jax.random.randint(seeds[3], (ROWS,), 0, COLS_DEV), jax.random.fold_in(seeds[3], 1), 0, COLS_DEV - 1).astype(jnp.int32)
    obs_weight = normal_values(seeds[4], (NZ, NZ), NZ ** -0.5, 0.75, (), jnp.float32)
    vert_inverse = draw_vert_inverse(jax.random.fold_in(seeds[8], 71), 0)
    vert_basis = draw_vert_basis(jax.random.fold_in(seeds[8], 71), 0)
    vert_eigen = draw_vert_eigen(jax.random.fold_in(seeds[8], 71), 0)
    return {"forcing_field": forcing_field, "innovations": innovations, "owner_device": owner_device, "column_index": column_index, "obs_weight": obs_weight, "vert_inverse": vert_inverse, "vert_basis": vert_basis, "vert_eigen": vert_eigen}


def cosine_table(length):
    frequency = jnp.arange(length, dtype=jnp.float32)[:, None]
    points = jnp.arange(length, dtype=jnp.float32)[None, :]
    scales = jnp.where(frequency == 0, jnp.sqrt(1.0 / length), jnp.sqrt(2.0 / length))
    return scales * jnp.cos(jnp.pi * frequency * (2.0 * points + 1.0) / (2.0 * length))

def eigen_line(wave_ids, length):
    return 4.0 * jnp.sin(jnp.pi * wave_ids / (2.0 * length)) ** 2

def reference(forcing_field, innovations, owner_device, column_index, obs_weight, vert_inverse, vert_basis, vert_eigen):
    highest = lax.Precision.HIGHEST
    weighted = jnp.dot(innovations, obs_weight, precision=highest, preferred_element_type=jnp.float32)
    cols_x = NX // N_GX
    cols_y = NY // N_GY
    targets = owner_device[:, 0].astype(jnp.int32)
    pos_x = targets // N_GY * cols_x + column_index % cols_x
    pos_y = targets % N_GY * cols_y + column_index // cols_x
    flat_index = (pos_y * NX + pos_x).astype(jnp.int32)
    observed = jax.ops.segment_sum(weighted, flat_index, num_segments=NX * NY)
    observed = observed.T.reshape(NZ, NY, NX)
    forcing_total = forcing_field + observed
    vertical = jnp.einsum('mz,zyx->myx', vert_inverse, forcing_total, precision=highest)
    table_x = cosine_table(NX)
    table_y = cosine_table(NY)
    spectral = jnp.einsum('myx,kx->myk', vertical, table_x, precision=highest)
    spectral = jnp.einsum('myk,ly->mlk', spectral, table_y, precision=highest)
    line_x = eigen_line(jnp.arange(NX, dtype=jnp.float32), NX)
    line_y = eigen_line(jnp.arange(NY, dtype=jnp.float32), NY)
    denominator = vert_eigen[:, None, None] + line_y[None, :, None] + line_x[None, None, :]
    solved = spectral / denominator
    physical = jnp.einsum('mlk,ly->myk', solved, table_y, precision=highest)
    physical = jnp.einsum('myk,kx->myx', physical, table_x, precision=highest)
    return jnp.einsum('zm,myx->zyx', vert_basis, physical, precision=highest)
```

```python
import functools

import jax
import jax.numpy as jnp
import ml_dtypes
import numpy as np
from jax import lax
from jax.experimental import pallas as pl
from jax.experimental.pallas import tpu as pltpu
from jax.sharding import PartitionSpec as P

MESH = pl.DeviceIdType.MESH
F32 = jnp.float32
BF16 = jnp.bfloat16
LANES = 128
Y_CUTS = 2
K_CUTS = 2


def wave_order(length):
    return np.concatenate([np.arange(0, length, 2), np.arange(1, length, 2)])


def split_table(table):
    high = table.astype(np.float32).astype(ml_dtypes.bfloat16)
    low = (table - high.astype(np.float64)).astype(np.float32).astype(ml_dtypes.bfloat16)
    return high, low


def wave_tables(length):
    waves = wave_order(length).astype(np.float64)
    points = np.arange(length, dtype=np.float64)
    scales = np.where(waves == 0, np.sqrt(1.0 / length), np.sqrt(2.0 / length))
    table = scales[:, None] * np.cos(np.pi * waves[:, None] * (2 * points + 1) / (2 * length))
    line = 4.0 * np.sin(np.pi * waves / (2.0 * length)) ** 2
    return split_table(table), split_table(table.T), line.astype(np.float32)


def halves(value):
    high = value.astype(BF16)
    low = (value - high.astype(F32)).astype(BF16)
    return high, low


def dot(left, right):
    return jnp.dot(left, right, preferred_element_type=F32)


def wait_for(ref, sem):
    pltpu.make_async_copy(ref, ref, sem).wait()


def field_kernel(
    n_gx, n_gy, gy_dims, field, vinv, vbas, eigen, c_hi, c_lo, t_hi, t_lo, line_col, line_row, out,
    vert, x_in, x_out, y_in, y_out, z_in, z_out, phys, solved,
    xf_send, xf_recv, yf_send, yf_recv, yb_send, yb_recv, xb_send, xb_recv,
):
    gx = lax.axis_index("gx")
    gy = lax.axis_index("gy")
    n_hi, n_lo = gy_dims
    rows_y = y_in.shape[2]
    levels = phys.shape[0] // rows_y
    own_levels = levels // n_gx
    parts = n_gy // own_levels
    cut = rows_y // Y_CUTS
    length = c_hi.shape[0]

    def gx_peer(step):
        return lax.rem(gx + step, n_gx)

    def gy_peer(step):
        high = lax.rem(gy // n_lo + step // n_lo, n_hi)
        low = lax.rem(gy + step, n_lo)
        return high * n_lo + low

    barrier = pltpu.get_barrier_semaphore()

    def greet_gx(step, carry):
        pl.semaphore_signal(barrier, inc=1, device_id=(gx_peer(step), gy), device_id_type=MESH)
        return carry

    def greet_gy(step, carry):
        pl.semaphore_signal(barrier, inc=1, device_id=(gx, gy_peer(step)), device_id_type=MESH)
        return carry

    lax.fori_loop(1, n_gx, greet_gx, 0)
    lax.fori_loop(1, n_gy, greet_gy, 0)

    def mix_levels(matrix, source, target, y_cut):
        m_hi, m_lo = halves(matrix)
        stack = jnp.concatenate([m_hi, m_hi, m_lo], axis=1)
        for y in range(y_cut * cut, (y_cut + 1) * cut, 2):
            pair = jnp.concatenate(
                [source[pl.ds(y + i, levels, stride=rows_y), :] for i in range(2)], axis=1
            )
            hi, lo = halves(pair)
            mixed = dot(stack, jnp.concatenate([hi, lo, hi], axis=0))
            for i in range(2):
                target[pl.ds(y + i, levels, stride=rows_y), :] = mixed[:, i * LANES : (i + 1) * LANES]

    def send_gx(source, target, send_sem, recv_sem):
        pltpu.make_async_copy(source(gx), target, recv_sem).start()

        def one(step, carry):
            peer = gx_peer(step)
            pltpu.make_async_remote_copy(
                src_ref=source(peer), dst_ref=target, send_sem=send_sem, recv_sem=recv_sem,
                device_id=(peer, gy), device_id_type=MESH,
            ).start()
            return carry

        lax.fori_loop(1, n_gx, one, 0)

    def send_gy(source, target, send_sem, recv_sem):
        pltpu.make_async_copy(source(gy), target, recv_sem).start()

        def one(step, carry):
            peer = gy_peer(step)
            pltpu.make_async_remote_copy(
                src_ref=source(peer), dst_ref=target, send_sem=send_sem, recv_sem=recv_sem,
                device_id=(gx, peer), device_id_type=MESH,
            ).start()
            return carry

        lax.fori_loop(1, n_gy, one, 0)

    def y_span(y_cut):
        return pl.ds(y_cut * cut, cut)

    vert3 = vert.reshape(levels, rows_y, LANES)
    phys3 = phys.reshape(levels, rows_y, LANES)

    for h in range(Y_CUTS):
        mix_levels(vinv[...], field, vert, h)
        if h == 0:
            pl.semaphore_wait(barrier, n_gx - 1 + n_gy - 1)
        send_gx(
            lambda a: vert3.at[pl.ds(a * own_levels, own_levels), y_span(h), :],
            x_in.at[gx, :, y_span(h), :],
            xf_send.at[h], xf_recv.at[h],
        )

    wide = 2 * LANES

    def transform_x(h, k):
        lines = jnp.concatenate(
            [x_in[a, :, y_span(h), :].reshape(own_levels * cut, LANES) for a in range(n_gx)], axis=1
        )
        hi, lo = halves(lines)
        for block in range(parts * LANES // wide):
            cols = pl.ds(k * parts * LANES + block * wide, wide)
            res = dot(hi, t_hi[:, cols]) + dot(lo, t_hi[:, cols]) + dot(hi, t_lo[:, cols])
            for i in range(2):
                x_out[k, :, block * 2 + i, y_span(h), :] = res[:, i * LANES : (i + 1) * LANES].reshape(
                    own_levels, cut, LANES
                )
        send_gy(
            lambda b: x_out.at[k, b // parts, lax.rem(b, parts), y_span(h), :],
            y_in.at[k, gy, y_span(h), :],
            yf_send.at[k, h], yf_recv.at[k, h],
        )

    for k in range(K_CUTS):
        for h in range(Y_CUTS):
            if k == 0:
                wait_for(x_in.at[:, :, y_span(h), :], xf_recv.at[h])
            transform_x(h, k)

    level = gx * own_levels + gy // parts
    part = lax.rem(gy, parts)

    def transform_y(k):
        hi, lo = halves(y_in[k].reshape(length, LANES))
        both = jnp.concatenate([hi, lo], axis=1)
        line = line_row[pl.ds(k * parts + part, 1), :] + eigen[level]
        for block in range(length // wide):
            rows = pl.ds(block * wide, wide)
            res = dot(c_hi[rows, :], both)
            res = res[:, :LANES] + res[:, LANES:] + dot(c_lo[rows, :], hi)
            res = res / (line_col[rows, :] + line)
            s_hi, s_lo = halves(res)
            solved[rows, :LANES] = s_hi
            solved[rows, LANES:] = s_lo
        per = wide // rows_y
        for block in range(length // wide):
            rows = pl.ds(block * wide, wide)
            res = dot(t_hi[rows, :], solved[...])
            res = res[:, :LANES] + res[:, LANES:] + dot(t_lo[rows, :], solved[:, :LANES])
            y_out[k, pl.ds(block * per, per), :, :] = res.reshape(per, rows_y, LANES)

    for k in range(K_CUTS):
        for h in range(Y_CUTS):
            wait_for(y_in.at[k, :, y_span(h), :], yf_recv.at[k, h])
        transform_y(k)
        for h in range(Y_CUTS):
            send_gy(
                lambda b: y_out.at[k, b, y_span(h), :],
                z_in.at[k, gy // parts, part, y_span(h), :],
                yb_send.at[k, h], yb_recv.at[k, h],
            )

    for h in range(Y_CUTS):
        for k in range(K_CUTS):
            wait_for(z_in.at[k, :, :, y_span(h), :], yb_recv.at[k, h])
        lines = jnp.concatenate(
            [
                z_in[k, :, p, y_span(h), :].reshape(own_levels * cut, LANES)
                for k in range(K_CUTS)
                for p in range(parts)
            ],
            axis=1,
        )
        hi, lo = halves(lines)
        for block in range(length // wide):
            cols = pl.ds(block * wide, wide)
            res = dot(hi, c_hi[:, cols]) + dot(lo, c_hi[:, cols]) + dot(hi, c_lo[:, cols])
            for i in range(2):
                z_out[block * 2 + i, :, y_span(h), :] = res[:, i * LANES : (i + 1) * LANES].reshape(
                    own_levels, cut, LANES
                )
        send_gx(
            lambda a: z_out.at[a, :, y_span(h), :],
            phys3.at[pl.ds(gx * own_levels, own_levels), y_span(h), :],
            xb_send.at[h], xb_recv.at[h],
        )

    for h in range(Y_CUTS):
        wait_for(phys3.at[:, y_span(h), :], xb_recv.at[h])
        mix_levels(vbas[...], phys, out, h)

    for h in range(Y_CUTS):
        wait_for(x_in.at[pl.ds(0, n_gx - 1), :, y_span(h), :], xf_send.at[h])
        wait_for(z_out.at[pl.ds(0, n_gx - 1), :, y_span(h), :], xb_send.at[h])
        for k in range(K_CUTS):
            wait_for(y_in.at[k, pl.ds(0, n_gy - 1), y_span(h), :], yf_send.at[k, h])
            wait_for(y_out.at[k, pl.ds(0, n_gy - 1), y_span(h), :], yb_send.at[k, h])


def solve_field(forcing_total, vert_inverse, vert_basis, vert_eigen, gy_dims):
    n_gx = lax.axis_size("gx")
    n_gy = lax.axis_size("gy")
    levels, rows_y, cols_x = forcing_total.shape
    length = cols_x * n_gx
    (c_hi, c_lo), (t_hi, t_lo), line = wave_tables(length)
    own_levels = levels // n_gx
    parts = n_gy // own_levels
    line_col = np.broadcast_to(line[:, None], (length, LANES))
    line_row = line.reshape(K_CUTS * parts, LANES)
    vmem = pl.BlockSpec(memory_space=pltpu.VMEM)
    smem = pl.BlockSpec(memory_space=pltpu.SMEM)
    dma = pltpu.SemaphoreType.DMA
    out = pl.pallas_call(
        functools.partial(field_kernel, n_gx, n_gy, gy_dims),
        out_shape=jax.ShapeDtypeStruct((levels * rows_y, cols_x), F32),
        in_specs=[vmem, vmem, vmem, smem, vmem, vmem, vmem, vmem, vmem, vmem],
        out_specs=vmem,
        scratch_shapes=[
            pltpu.VMEM((levels * rows_y, LANES), F32),
            pltpu.VMEM((n_gx, own_levels, rows_y, LANES), F32),
            pltpu.VMEM((K_CUTS, own_levels, parts, rows_y, LANES), F32),
            pltpu.VMEM((K_CUTS, n_gy, rows_y, LANES), F32),
            pltpu.VMEM((K_CUTS, n_gy, rows_y, LANES), F32),
            pltpu.VMEM((K_CUTS, own_levels, parts, rows_y, LANES), F32),
            pltpu.VMEM((n_gx, own_levels, rows_y, LANES), F32),
            pltpu.VMEM((levels * rows_y, LANES), F32),
            pltpu.VMEM((length, 2 * LANES), BF16),
            dma((Y_CUTS,)), dma((Y_CUTS,)),
            dma((K_CUTS, Y_CUTS)), dma((K_CUTS, Y_CUTS)),
            dma((K_CUTS, Y_CUTS)), dma((K_CUTS, Y_CUTS)),
            dma((Y_CUTS,)), dma((Y_CUTS,)),
        ],
        compiler_params=pltpu.CompilerParams(
            collective_id=0, has_side_effects=True, vmem_limit_bytes=48 * 1024 * 1024
        ),
        name="field_solve",
    )(
        forcing_total.reshape(levels * rows_y, cols_x), vert_inverse, vert_basis, vert_eigen,
        c_hi, c_lo, t_hi, t_lo, line_col, line_row,
    )
    return out.reshape(levels, rows_y, cols_x)


def observed_field(innovations, owner_device, column_index, obs_weight, shape):
    highest = lax.Precision.HIGHEST
    levels, cols_y, cols_x = shape
    groups_x = lax.axis_size("gx")
    groups_y = lax.axis_size("gy")
    devices_all = groups_x * groups_y
    row_total = innovations.shape[0]
    capacity = 2 * row_total // devices_all
    targets = owner_device[:, 0]
    one_hot = (targets[:, None] == jnp.arange(devices_all, dtype=jnp.int32)[None, :]).astype(
        jnp.int32
    )
    rank_in_peer = jnp.sum(jnp.cumsum(one_hot, axis=0) * one_hot, axis=1) - 1
    slot_index = targets * capacity + rank_in_peer
    payload = jnp.dot(innovations, obs_weight, precision=highest, preferred_element_type=F32)
    send_rows = jnp.zeros((devices_all * capacity, levels), F32).at[slot_index].set(payload)
    send_cols = jnp.full((devices_all * capacity,), -1, jnp.int32).at[slot_index].set(column_index)
    send_rows = send_rows.reshape(groups_x, groups_y, capacity, levels)
    send_cols = send_cols.reshape(groups_x, groups_y, capacity)

    def swap(array):
        array = lax.all_to_all(array, "gx", split_axis=0, concat_axis=0, tiled=True)
        return lax.all_to_all(array, "gy", split_axis=1, concat_axis=1, tiled=True)

    flat_rows = swap(send_rows).reshape(devices_all * capacity, levels)
    flat_cols = swap(send_cols).reshape(devices_all * capacity)
    row_valid = flat_cols >= 0
    summed = jax.ops.segment_sum(
        jnp.where(row_valid[:, None], flat_rows, 0.0),
        jnp.where(row_valid, flat_cols, 0),
        num_segments=cols_y * cols_x,
    )
    return summed.reshape(cols_y, cols_x, levels).transpose(2, 0, 1)


def per_device(
    forcing_field, innovations, owner_device, column_index, obs_weight, vert_inverse, vert_basis,
    vert_eigen,
):
    observed = observed_field(
        innovations, owner_device, column_index, obs_weight, forcing_field.shape
    )
    return solve_field(forcing_field + observed, vert_inverse, vert_basis, vert_eigen, (4, 8))


def solution(mesh):
    return jax.shard_map(
        per_device,
        mesh=mesh,
        in_specs=(
            P(None, "gy", "gx"),
            P(("gx", "gy"), None),
            P(("gx", "gy"), None),
            P(("gx", "gy")),
            P(),
            P(),
            P(),
            P(),
        ),
        out_specs=P(None, "gy", "gx"),
        check_vma=False,
    )
```

```python
import functools

import jax
import jax.numpy as jnp
import ml_dtypes
import numpy as np
from jax import lax
from jax.experimental import pallas as pl
from jax.experimental.pallas import tpu as pltpu
from jax.sharding import PartitionSpec as P

MESH = pl.DeviceIdType.MESH
F32 = jnp.float32
BF16 = jnp.bfloat16
LANES = 128
Y_CUTS = 2
K_CUTS = 2
R_CUTS = 3
R_PLANES = 3
TILE = 256


def wave_order(length):
    return np.concatenate([np.arange(0, length, 2), np.arange(1, length, 2)])


def split_table(table):
    high = table.astype(np.float32).astype(ml_dtypes.bfloat16)
    low = (table - high.astype(np.float64)).astype(np.float32).astype(ml_dtypes.bfloat16)
    return high, low


def wave_tables(length):
    waves = wave_order(length).astype(np.float64)
    points = np.arange(length, dtype=np.float64)
    scales = np.where(waves == 0, np.sqrt(1.0 / length), np.sqrt(2.0 / length))
    table = scales[:, None] * np.cos(np.pi * waves[:, None] * (2 * points + 1) / (2 * length))
    line = 4.0 * np.sin(np.pi * waves / (2.0 * length)) ** 2
    return split_table(table), split_table(table.T), line.astype(np.float32)


def halves(value):
    high = value.astype(BF16)
    low = (value - high.astype(F32)).astype(BF16)
    return high, low


def dot(left, right):
    return jnp.dot(left, right, preferred_element_type=F32)


def dot_nt(left, right):
    return lax.dot_general(left, right, (((1,), (1,)), ((), ())), preferred_element_type=F32)


def wait_for(ref, sem):
    pltpu.make_async_copy(ref, ref, sem).wait()


def field_kernel(
    n_gx, n_gy, gy_dims,
    field_hbm, innov, owner, column, weight, vinv, vbas, eigen,
    c_hi_hbm, c_lo_hbm, t_hi_hbm, t_lo_hbm, line_col_hbm, line_row,
    out,
    field, c_hi, c_lo, t_hi, t_lo, line_col,
    hots, expanded, slots, relay, relay_out, got, sums,
    vert, x_in, x_out, y_in, y_out, z_in, z_out, phys, solved,
    load_sem, rx_send, rx_recv, ry_send, ry_recv,
    xf_send, xf_recv, yf_send, yf_recv, yb_send, yb_recv, xb_send, xb_recv,
):
    gx = lax.axis_index("gx")
    gy = lax.axis_index("gy")
    n_hi, n_lo = gy_dims
    rows_y = y_in.shape[2]
    levels = phys.shape[0] // rows_y
    own_levels = levels // n_gx
    parts = n_gy // own_levels
    cut = rows_y // Y_CUTS
    length = c_hi.shape[0]

    def gx_peer(step):
        return lax.rem(gx + step, n_gx)

    def gy_peer(step):
        high = lax.rem(gy // n_lo + step // n_lo, n_hi)
        low = lax.rem(gy + step, n_lo)
        return high * n_lo + low

    loads = [
        pltpu.make_async_copy(source, target, load_sem.at[i])
        for i, (source, target) in enumerate(
            [
                (field_hbm, field), (t_hi_hbm, t_hi), (t_lo_hbm, t_lo), (c_hi_hbm, c_hi),
                (c_lo_hbm, c_lo), (line_col_hbm, line_col),
            ]
        )
    ]
    for load in loads:
        load.start()

    barrier = pltpu.get_barrier_semaphore()

    def greet_gx(step, carry):
        pl.semaphore_signal(barrier, inc=1, device_id=(gx_peer(step), gy), device_id_type=MESH)
        return carry

    def greet_gy(step, carry):
        pl.semaphore_signal(barrier, inc=1, device_id=(gx, gy_peer(step)), device_id_type=MESH)
        return carry

    lax.fori_loop(1, n_gx, greet_gx, 0)
    lax.fori_loop(1, n_gy, greet_gy, 0)

    def mix_levels(matrix, source, target, y_cut):
        m_hi, m_lo = halves(matrix)
        stack = jnp.concatenate([m_hi, m_hi, m_lo], axis=1)
        for y in range(y_cut * cut, (y_cut + 1) * cut, 2):
            pair = jnp.concatenate(
                [source[pl.ds(y + i, levels, stride=rows_y), :] for i in range(2)], axis=1
            )
            hi, lo = halves(pair)
            mixed = dot(stack, jnp.concatenate([hi, lo, hi], axis=0))
            for i in range(2):
                target[pl.ds(y + i, levels, stride=rows_y), :] = mixed[:, i * LANES : (i + 1) * LANES]

    def send_gx(source, target, send_sem, recv_sem):
        pltpu.make_async_copy(source(gx), target, recv_sem).start()

        def one(step, carry):
            peer = gx_peer(step)
            pltpu.make_async_remote_copy(
                src_ref=source(peer), dst_ref=target, send_sem=send_sem, recv_sem=recv_sem,
                device_id=(peer, gy), device_id_type=MESH,
            ).start()
            return carry

        lax.fori_loop(1, n_gx, one, 0)

    def send_gy(source, target, send_sem, recv_sem):
        pltpu.make_async_copy(source(gy), target, recv_sem).start()

        def one(step, carry):
            peer = gy_peer(step)
            pltpu.make_async_remote_copy(
                src_ref=source(peer), dst_ref=target, send_sem=send_sem, recv_sem=recv_sem,
                device_id=(gx, peer), device_id_type=MESH,
            ).start()
            return carry

        lax.fori_loop(1, n_gy, one, 0)

    def y_span(y_cut):
        return pl.ds(y_cut * cut, cut)

    vert3 = vert.reshape(levels, rows_y, LANES)
    phys3 = phys.reshape(levels, rows_y, LANES)
    devices = n_gx * n_gy
    slot_pairs = R_CUTS * R_PLANES - 1
    chunks = owner.shape[0]
    side = lax.broadcasted_iota(jnp.int32, (devices, TILE), 0)

    def number_rows():
        before = jnp.where(
            lax.broadcasted_iota(jnp.int32, (TILE, TILE), 0)
            < lax.broadcasted_iota(jnp.int32, (TILE, TILE), 1),
            1.0, 0.0,
        ).astype(BF16)
        seen = jnp.zeros((devices, 1), F32)
        ranks = []
        for chunk in range(chunks):
            hot = jnp.where(side == owner[chunk : chunk + 1, :], 1.0, 0.0)
            narrow = hot.astype(BF16)
            hots[:, chunk * TILE : (chunk + 1) * TILE] = narrow
            earlier = dot(narrow, before) + seen
            ranks.append(jnp.sum(hot * earlier, axis=0, keepdims=True).astype(jnp.int32))
            seen = seen + jnp.sum(hot, axis=1, keepdims=True)
        return ranks

    def weigh_rows(ranks):
        mixed = lax.dot_general(
            weight[...], vinv[...], (((1,), (1,)), ((), ())),
            precision=lax.Precision.HIGHEST, preferred_element_type=F32,
        )
        w_hi, w_lo = halves(jnp.concatenate([mixed, mixed], axis=1))
        upper = lax.broadcasted_iota(jnp.int32, (LANES, LANES), 1) >= levels
        for chunk in range(chunks):
            rows = slice(chunk * TILE, (chunk + 1) * TILE)
            hi, lo = halves(innov[rows, :])
            rows_m = dot(hi, w_hi) + dot(lo, w_hi) + dot(hi, w_lo)
            odd = (ranks[chunk] & 1).astype(F32)
            keep = []
            for i in range(TILE // LANES):
                turned = jnp.broadcast_to(odd[:, i * LANES : (i + 1) * LANES], (LANES, LANES)).T
                keep.append(jnp.where(upper, turned, 1.0 - turned))
            hi, lo = halves(rows_m * jnp.concatenate(keep, axis=0))
            expanded[rows, :LANES] = hi
            expanded[rows, LANES:] = lo

    def place_codes(ranks):
        wide_side = lax.broadcasted_iota(jnp.int32, (LANES, TILE), 0)
        high = jnp.zeros((devices, LANES), F32)
        low = jnp.zeros((devices, LANES), F32)
        for chunk in range(chunks):
            lane = (ranks[chunk] & 1) * slot_pairs + (ranks[chunk] >> 1)
            code = column[chunk : chunk + 1, :] + 1
            here = wide_side == lane
            hot = hots[:, chunk * TILE : (chunk + 1) * TILE]
            high += dot_nt(hot, jnp.where(here, (code >> 6).astype(F32), 0.0).astype(BF16))
            low += dot_nt(hot, jnp.where(here, (code & 63).astype(F32), 0.0).astype(BF16))
        slots[0] = high * 64.0 + low

    def place_rows(ranks, pair):
        total = jnp.zeros((devices, TILE), F32)
        for chunk in range(chunks):
            mask = jnp.where((ranks[chunk] >> 1) == pair, 1.0, 0.0).astype(BF16)
            hot = hots[:, chunk * TILE : (chunk + 1) * TILE] * mask
            total += dot(hot, expanded[chunk * TILE : (chunk + 1) * TILE, :])
        slots[pair + 1] = total[:, :LANES] + total[:, LANES:]

    ranks = number_rows()
    place_codes(ranks)
    weigh_rows(ranks)
    for r in range(R_CUTS):
        planes = pl.ds(r * R_PLANES, R_PLANES)
        for plane in range(r * R_PLANES, (r + 1) * R_PLANES):
            if plane > 0:
                place_rows(ranks, plane - 1)
        if r == 0:
            pl.semaphore_wait(barrier, n_gx - 1 + n_gy - 1)
        send_gx(
            lambda a: slots.at[planes, pl.ds(a * n_gy, n_gy), :],
            relay.at[planes, gx, :, :],
            rx_send.at[r], rx_recv.at[r],
        )

    def pass_on(r):
        wait_for(relay.at[pl.ds(r * R_PLANES, R_PLANES)], rx_recv.at[r])
        for i in range(R_PLANES):
            plane = relay.at[r * R_PLANES + i].reshape(devices, LANES)
            for b in range(n_gy):
                relay_out[r, b, i, :, :] = plane[pl.ds(b, n_gx, stride=n_gy), :]
        send_gy(
            lambda b: relay_out.at[r, b], got.at[r, gy], ry_send.at[r], ry_recv.at[r]
        )

    pass_on(0)
    loads[0].wait()
    for h in range(Y_CUTS):
        mix_levels(vinv[...], field, vert, h)
    for r in range(1, R_CUTS):
        pass_on(r)

    spots = 4
    area = rows_y * LANES // spots
    place_side = lax.broadcasted_iota(jnp.int32, (area, devices), 0)

    def add_rows(r, codes):
        lefts, rights = [], []
        for i in range(R_PLANES):
            pair = r * R_PLANES + i - 1
            if pair < 0:
                continue
            data = got[r, :, i, :, :].reshape(devices, LANES).T
            hi, lo = halves(data)
            for half in range(2):
                code = codes[half * slot_pairs + pair : half * slot_pairs + pair + 1, :]
                spot, place = code >> 10, code & (area - 1)
                both = jnp.concatenate(
                    [part[half * levels : (half + 1) * levels, :] for part in (hi, lo)], axis=0
                )
                lefts.append(
                    jnp.concatenate(
                        [
                            both * jnp.where(spot == s, 1.0, 0.0).astype(BF16)
                            for s in range(spots)
                        ],
                        axis=0,
                    )
                )
                rights.append(jnp.where(place_side == place, 1.0, 0.0).astype(BF16))
        term = dot_nt(jnp.concatenate(lefts, axis=1), jnp.concatenate(rights, axis=1))
        if r == 0:
            sums[...] = term
        else:
            sums[...] += term

    codes = None
    for r in range(R_CUTS):
        wait_for(got.at[r], ry_recv.at[r])
        if r == 0:
            codes = got[0, :, 0, :, :].reshape(devices, LANES).T.astype(jnp.int32) - 1
        add_rows(r, codes)

    per_spot = rows_y // spots
    for h in range(Y_CUTS):
        for y in range(h * cut, (h + 1) * cut):
            spot, lanes = y // per_spot, slice((y % per_spot) * LANES, (y % per_spot + 1) * LANES)
            top = spot * 2 * levels
            rows = pl.ds(y, levels, stride=rows_y)
            vert[rows, :] = (
                vert[rows, :] + sums[top : top + levels, lanes]
                + sums[top + levels : top + 2 * levels, lanes]
            )
        send_gx(
            lambda a: vert3.at[pl.ds(a * own_levels, own_levels), y_span(h), :],
            x_in.at[gx, :, y_span(h), :],
            xf_send.at[h], xf_recv.at[h],
        )
    for load in loads[1:]:
        load.wait()

    wide = 2 * LANES

    def transform_x(h, k):
        lines = jnp.concatenate(
            [x_in[a, :, y_span(h), :].reshape(own_levels * cut, LANES) for a in range(n_gx)], axis=1
        )
        hi, lo = halves(lines)
        for block in range(parts * LANES // wide):
            cols = pl.ds(k * parts * LANES + block * wide, wide)
            res = dot(hi, t_hi[:, cols]) + dot(lo, t_hi[:, cols]) + dot(hi, t_lo[:, cols])
            for i in range(2):
                x_out[k, :, block * 2 + i, y_span(h), :] = res[:, i * LANES : (i + 1) * LANES].reshape(
                    own_levels, cut, LANES
                )
        send_gy(
            lambda b: x_out.at[k, b // parts, lax.rem(b, parts), y_span(h), :],
            y_in.at[k, gy, y_span(h), :],
            yf_send.at[k, h], yf_recv.at[k, h],
        )

    for k in range(K_CUTS):
        for h in range(Y_CUTS):
            if k == 0:
                wait_for(x_in.at[:, :, y_span(h), :], xf_recv.at[h])
            transform_x(h, k)

    level = gx * own_levels + gy // parts
    part = lax.rem(gy, parts)

    def transform_y(k):
        hi, lo = halves(y_in[k].reshape(length, LANES))
        both = jnp.concatenate([hi, lo], axis=1)
        line = line_row[pl.ds(k * parts + part, 1), :] + eigen[level]
        for block in range(length // wide):
            rows = pl.ds(block * wide, wide)
            res = dot(c_hi[rows, :], both)
            res = res[:, :LANES] + res[:, LANES:] + dot(c_lo[rows, :], hi)
            res = res / (line_col[rows, :] + line)
            s_hi, s_lo = halves(res)
            solved[rows, :LANES] = s_hi
            solved[rows, LANES:] = s_lo
        per = wide // rows_y
        for block in range(length // wide):
            rows = pl.ds(block * wide, wide)
            res = dot(t_hi[rows, :], solved[...])
            res = res[:, :LANES] + res[:, LANES:] + dot(t_lo[rows, :], solved[:, :LANES])
            y_out[k, pl.ds(block * per, per), :, :] = res.reshape(per, rows_y, LANES)

    for k in range(K_CUTS):
        for h in range(Y_CUTS):
            wait_for(y_in.at[k, :, y_span(h), :], yf_recv.at[k, h])
        transform_y(k)
        for h in range(Y_CUTS):
            send_gy(
                lambda b: y_out.at[k, b, y_span(h), :],
                z_in.at[k, gy // parts, part, y_span(h), :],
                yb_send.at[k, h], yb_recv.at[k, h],
            )

    for h in range(Y_CUTS):
        for k in range(K_CUTS):
            wait_for(z_in.at[k, :, :, y_span(h), :], yb_recv.at[k, h])
        lines = jnp.concatenate(
            [
                z_in[k, :, p, y_span(h), :].reshape(own_levels * cut, LANES)
                for k in range(K_CUTS)
                for p in range(parts)
            ],
            axis=1,
        )
        hi, lo = halves(lines)
        for block in range(length // wide):
            cols = pl.ds(block * wide, wide)
            res = dot(hi, c_hi[:, cols]) + dot(lo, c_hi[:, cols]) + dot(hi, c_lo[:, cols])
            for i in range(2):
                z_out[block * 2 + i, :, y_span(h), :] = res[:, i * LANES : (i + 1) * LANES].reshape(
                    own_levels, cut, LANES
                )
        send_gx(
            lambda a: z_out.at[a, :, y_span(h), :],
            phys3.at[pl.ds(gx * own_levels, own_levels), y_span(h), :],
            xb_send.at[h], xb_recv.at[h],
        )

    for h in range(Y_CUTS):
        wait_for(phys3.at[:, y_span(h), :], xb_recv.at[h])
        mix_levels(vbas[...], phys, out, h)

    for r in range(R_CUTS):
        wait_for(relay.at[pl.ds(r * R_PLANES, R_PLANES), pl.ds(0, n_gx - 1)], rx_send.at[r])
        wait_for(got.at[r, pl.ds(0, n_gy - 1)], ry_send.at[r])
    for h in range(Y_CUTS):
        wait_for(x_in.at[pl.ds(0, n_gx - 1), :, y_span(h), :], xf_send.at[h])
        wait_for(z_out.at[pl.ds(0, n_gx - 1), :, y_span(h), :], xb_send.at[h])
        for k in range(K_CUTS):
            wait_for(y_in.at[k, pl.ds(0, n_gy - 1), y_span(h), :], yf_send.at[k, h])
            wait_for(y_out.at[k, pl.ds(0, n_gy - 1), y_span(h), :], yb_send.at[k, h])


def per_device(
    forcing_field, innovations, owner_device, column_index, obs_weight, vert_inverse, vert_basis,
    vert_eigen,
):
    n_gx = lax.axis_size("gx")
    n_gy = lax.axis_size("gy")
    devices = n_gx * n_gy
    levels, rows_y, cols_x = forcing_field.shape
    length = cols_x * n_gx
    (c_hi, c_lo), (t_hi, t_lo), line = wave_tables(length)
    own_levels = levels // n_gx
    parts = n_gy // own_levels
    planes = R_CUTS * R_PLANES
    line_col = np.broadcast_to(line[:, None], (length, LANES))
    line_row = line.reshape(K_CUTS * parts, LANES)
    vmem = pl.BlockSpec(memory_space=pltpu.VMEM)
    smem = pl.BlockSpec(memory_space=pltpu.SMEM)
    hbm = pl.BlockSpec(memory_space=pl.ANY)
    dma = pltpu.SemaphoreType.DMA
    out = pl.pallas_call(
        functools.partial(field_kernel, n_gx, n_gy, (4, 8)),
        out_shape=jax.ShapeDtypeStruct((levels * rows_y, cols_x), F32),
        in_specs=[hbm, vmem, vmem, vmem, vmem, vmem, vmem, smem, hbm, hbm, hbm, hbm, hbm, vmem],
        out_specs=vmem,
        scratch_shapes=[
            pltpu.VMEM((levels * rows_y, LANES), F32),
            pltpu.VMEM((length, length), BF16),
            pltpu.VMEM((length, length), BF16),
            pltpu.VMEM((length, length), BF16),
            pltpu.VMEM((length, length), BF16),
            pltpu.VMEM((length, LANES), F32),
            pltpu.VMEM((devices, innovations.shape[0]), BF16),
            pltpu.VMEM((innovations.shape[0], 2 * LANES), BF16),
            pltpu.VMEM((planes, devices, LANES), F32),
            pltpu.VMEM((planes, n_gx, n_gy, LANES), F32),
            pltpu.VMEM((R_CUTS, n_gy, R_PLANES, n_gx, LANES), F32),
            pltpu.VMEM((R_CUTS, n_gy, R_PLANES, n_gx, LANES), F32),
            pltpu.VMEM((8 * levels, rows_y * cols_x // 4), F32),
            pltpu.VMEM((levels * rows_y, LANES), F32),
            pltpu.VMEM((n_gx, own_levels, rows_y, LANES), F32),
            pltpu.VMEM((K_CUTS, own_levels, parts, rows_y, LANES), F32),
            pltpu.VMEM((K_CUTS, n_gy, rows_y, LANES), F32),
            pltpu.VMEM((K_CUTS, n_gy, rows_y, LANES), F32),
            pltpu.VMEM((K_CUTS, own_levels, parts, rows_y, LANES), F32),
            pltpu.VMEM((n_gx, own_levels, rows_y, LANES), F32),
            pltpu.VMEM((levels * rows_y, LANES), F32),
            pltpu.VMEM((length, 2 * LANES), BF16),
            dma((6,)),
            dma((R_CUTS,)), dma((R_CUTS,)),
            dma((R_CUTS,)), dma((R_CUTS,)),
            dma((Y_CUTS,)), dma((Y_CUTS,)),
            dma((K_CUTS, Y_CUTS)), dma((K_CUTS, Y_CUTS)),
            dma((K_CUTS, Y_CUTS)), dma((K_CUTS, Y_CUTS)),
            dma((Y_CUTS,)), dma((Y_CUTS,)),
        ],
        compiler_params=pltpu.CompilerParams(
            collective_id=0, has_side_effects=True, vmem_limit_bytes=56 * 1024 * 1024
        ),
        name="field_solve",
    )(
        forcing_field.reshape(levels * rows_y, cols_x), innovations,
        owner_device.reshape(-1, TILE), column_index.reshape(-1, TILE), obs_weight,
        vert_inverse, vert_basis, vert_eigen,
        c_hi, c_lo, t_hi, t_lo, line_col, line_row,
    )
    return out.reshape(levels, rows_y, cols_x)


def solution(mesh):
    return jax.shard_map(
        per_device,
        mesh=mesh,
        in_specs=(
            P(None, "gy", "gx"),
            P(("gx", "gy"), None),
            P(("gx", "gy"), None),
            P(("gx", "gy")),
            P(),
            P(),
            P(),
            P(),
        ),
        out_specs=P(None, "gy", "gx"),
        check_vma=False,
    )
```

```python
import functools

import jax
import jax.numpy as jnp
import ml_dtypes
import numpy as np
from jax import lax
from jax.experimental import pallas as pl
from jax.experimental.pallas import tpu as pltpu
from jax.sharding import PartitionSpec as P

MESH = pl.DeviceIdType.MESH
F32 = jnp.float32
BF16 = jnp.bfloat16
LANES = 128
Y_CUTS = 2
R_CUTS = 3
R_PLANES = 3
TILE = 256


def split_table(table):
    high = table.astype(np.float32).astype(ml_dtypes.bfloat16)
    low = (table - high.astype(np.float64)).astype(np.float32).astype(ml_dtypes.bfloat16)
    return high, low


def wave_tables(length):
    waves = np.arange(length, dtype=np.float64)
    scales = np.where(waves == 0, np.sqrt(1.0 / length), np.sqrt(2.0 / length))
    table = scales[:, None] * np.cos(np.pi * waves[:, None] * (2 * waves + 1) / (2 * length))
    line = 4.0 * np.sin(np.pi * waves / (2.0 * length)) ** 2
    return split_table(table), split_table(table.T), line.astype(np.float32)


def halves(value):
    high = value.astype(BF16)
    low = (value - high.astype(F32)).astype(BF16)
    return high, low


def dot(left, right):
    return jnp.dot(left, right, preferred_element_type=F32)


def dot_nt(left, right):
    return lax.dot_general(left, right, (((1,), (1,)), ((), ())), preferred_element_type=F32)


def wait_for(ref, sem):
    pltpu.make_async_copy(ref, ref, sem).wait()


def power(value, doublings):
    for _ in range(doublings):
        value = value * value
    return value


def decay(sigma):
    root = jnp.sqrt(sigma + 0.25 * sigma * sigma)
    return 1.0 / (1.0 + 0.5 * sigma + root), 0.5 / root


def field_kernel(
    n_gx, n_gy, gy_dims,
    field_hbm, innov, owner, column, weight, vinv, vbas, eigen,
    t_hi_hbm, t_lo_hbm, c_hi_hbm, c_lo_hbm, line,
    out,
    field, t_hi, t_lo, c_hi, c_lo,
    hots, expanded, slots, relay, relay_out, got, sums,
    vert, x_in, spec, run, edge_out, edge_in, inflow_out, inflow_in, inflow, z_out, phys,
    load_sem, rx_send, rx_recv, ry_send, ry_recv,
    xf_send, xf_recv, edge_send, edge_recv, flow_send, flow_recv, xb_send, xb_recv,
):
    gx = lax.axis_index("gx")
    gy = lax.axis_index("gy")
    n_hi, n_lo = gy_dims
    rows_y, levels, _ = vert.shape
    own_levels = levels // n_gx
    cut = rows_y // Y_CUTS
    length = t_hi.shape[0]

    def gx_peer(step):
        return lax.rem(gx + step, n_gx)

    def gy_peer(step):
        high = lax.rem(gy // n_lo + step // n_lo, n_hi)
        low = lax.rem(gy + step, n_lo)
        return high * n_lo + low

    loads = [
        pltpu.make_async_copy(source, target, load_sem.at[i])
        for i, (source, target) in enumerate(
            [
                (field_hbm, field), (t_hi_hbm, t_hi), (t_lo_hbm, t_lo), (c_hi_hbm, c_hi),
                (c_lo_hbm, c_lo),
            ]
        )
    ]
    for load in loads:
        load.start()

    barrier = pltpu.get_barrier_semaphore()

    def greet_gx(step, carry):
        pl.semaphore_signal(barrier, inc=1, device_id=(gx_peer(step), gy), device_id_type=MESH)
        return carry

    def greet_gy(step, carry):
        pl.semaphore_signal(barrier, inc=1, device_id=(gx, gy_peer(step)), device_id_type=MESH)
        return carry

    lax.fori_loop(1, n_gx, greet_gx, 0)
    lax.fori_loop(1, n_gy, greet_gy, 0)

    def mix_levels(matrix, read, write, y_cut):
        m_hi, m_lo = halves(matrix)
        stack = jnp.concatenate([m_hi, m_hi, m_lo], axis=1)
        for y in range(y_cut * cut, (y_cut + 1) * cut, 2):
            hi, lo = halves(jnp.concatenate([read(y), read(y + 1)], axis=1))
            mixed = dot(stack, jnp.concatenate([hi, lo, hi], axis=0))
            write(y, mixed[:, :LANES])
            write(y + 1, mixed[:, LANES:])

    def strided(ref, y):
        return ref.at[pl.ds(y, levels, stride=rows_y), :]

    def send_gx(source, target, send_sem, recv_sem):
        pltpu.make_async_copy(source(gx), target, recv_sem).start()

        def one(step, carry):
            peer = gx_peer(step)
            pltpu.make_async_remote_copy(
                src_ref=source(peer), dst_ref=target, send_sem=send_sem, recv_sem=recv_sem,
                device_id=(peer, gy), device_id_type=MESH,
            ).start()
            return carry

        lax.fori_loop(1, n_gx, one, 0)

    def send_gy(source, target, send_sem, recv_sem):
        pltpu.make_async_copy(source(gy), target, recv_sem).start()

        def one(step, carry):
            peer = gy_peer(step)
            pltpu.make_async_remote_copy(
                src_ref=source(peer), dst_ref=target, send_sem=send_sem, recv_sem=recv_sem,
                device_id=(gx, peer), device_id_type=MESH,
            ).start()
            return carry

        lax.fori_loop(1, n_gy, one, 0)

    def y_span(y_cut):
        return pl.ds(y_cut * cut, cut)

    devices = n_gx * n_gy
    slot_pairs = R_CUTS * R_PLANES - 1
    chunks = owner.shape[1] // TILE
    side = lax.broadcasted_iota(jnp.int32, (devices, TILE), 0)

    def number_rows():
        before = jnp.where(
            lax.broadcasted_iota(jnp.int32, (TILE, TILE), 0)
            < lax.broadcasted_iota(jnp.int32, (TILE, TILE), 1),
            1.0, 0.0,
        ).astype(BF16)
        seen = jnp.zeros((devices, 1), F32)
        ranks = []
        for chunk in range(chunks):
            hot = jnp.where(side == owner[:, chunk * TILE : (chunk + 1) * TILE], 1.0, 0.0)
            narrow = hot.astype(BF16)
            hots[:, chunk * TILE : (chunk + 1) * TILE] = narrow
            earlier = dot(narrow, before) + seen
            ranks.append(jnp.sum(hot * earlier, axis=0, keepdims=True).astype(jnp.int32))
            seen = seen + jnp.sum(hot, axis=1, keepdims=True)
        return ranks

    def weigh_rows(ranks):
        mixed = lax.dot_general(
            vinv[...], weight[...], (((1,), (1,)), ((), ())),
            precision=lax.Precision.HIGHEST, preferred_element_type=F32,
        )
        w_hi, w_lo = halves(jnp.concatenate([mixed, mixed], axis=0))
        stack = jnp.concatenate([w_hi, w_hi, w_lo], axis=1)
        upper = lax.broadcasted_iota(jnp.int32, (LANES, TILE), 0) // levels
        for chunk in range(chunks):
            lanes = slice(chunk * TILE, (chunk + 1) * TILE)
            hi, lo = halves(innov[:, lanes])
            rows_m = dot(stack, jnp.concatenate([hi, lo, hi], axis=0))
            hi, lo = halves(jnp.where(upper == (ranks[chunk] & 1), rows_m, 0.0))
            expanded[:LANES, lanes] = hi
            expanded[LANES:, lanes] = lo

    def place_codes(ranks):
        wide_side = lax.broadcasted_iota(jnp.int32, (LANES, TILE), 0)
        high = jnp.zeros((devices, LANES), F32)
        low = jnp.zeros((devices, LANES), F32)
        for chunk in range(chunks):
            lane = (ranks[chunk] & 1) * slot_pairs + (ranks[chunk] >> 1)
            code = column[:, chunk * TILE : (chunk + 1) * TILE] + 1
            here = wide_side == lane
            hot = hots[:, chunk * TILE : (chunk + 1) * TILE]
            high += dot_nt(hot, jnp.where(here, (code >> 6).astype(F32), 0.0).astype(BF16))
            low += dot_nt(hot, jnp.where(here, (code & 63).astype(F32), 0.0).astype(BF16))
        slots[0] = high * 64.0 + low

    def place_rows(ranks, pair):
        total = jnp.zeros((devices, TILE), F32)
        for chunk in range(chunks):
            mask = jnp.where((ranks[chunk] >> 1) == pair, 1.0, 0.0).astype(BF16)
            hot = hots[:, chunk * TILE : (chunk + 1) * TILE] * mask
            total += dot_nt(hot, expanded[:, chunk * TILE : (chunk + 1) * TILE])
        slots[pair + 1] = total[:, :LANES] + total[:, LANES:]

    ranks = number_rows()
    place_codes(ranks)
    weigh_rows(ranks)
    for r in range(R_CUTS):
        planes = pl.ds(r * R_PLANES, R_PLANES)
        for plane in range(r * R_PLANES, (r + 1) * R_PLANES):
            if plane > 0:
                place_rows(ranks, plane - 1)
        if r == 0:
            pl.semaphore_wait(barrier, n_gx - 1 + n_gy - 1)
        send_gx(
            lambda a: slots.at[planes, pl.ds(a * n_gy, n_gy), :],
            relay.at[planes, gx, :, :],
            rx_send.at[r], rx_recv.at[r],
        )

    def pass_on(r):
        wait_for(relay.at[pl.ds(r * R_PLANES, R_PLANES)], rx_recv.at[r])
        for i in range(R_PLANES):
            plane = relay.at[r * R_PLANES + i].reshape(devices, LANES)
            for b in range(n_gy):
                relay_out[r, b, i, :, :] = plane[pl.ds(b, n_gx, stride=n_gy), :]
        send_gy(
            lambda b: relay_out.at[r, b], got.at[r, gy], ry_send.at[r], ry_recv.at[r]
        )

    def set_vert(y, value):
        vert[y] = value

    pass_on(0)
    loads[0].wait()
    for h in range(Y_CUTS):
        mix_levels(vinv[...], lambda y: strided(field, y)[...], set_vert, h)
    for r in range(1, R_CUTS):
        pass_on(r)

    spots = 4
    area = rows_y * LANES // spots
    place_side = lax.broadcasted_iota(jnp.int32, (area, devices), 0)

    def add_rows(r, codes):
        lefts, rights = [], []
        for i in range(R_PLANES):
            pair = r * R_PLANES + i - 1
            if pair < 0:
                continue
            data = got[r, :, i, :, :].reshape(devices, LANES).T
            hi, lo = halves(data)
            for half in range(2):
                code = codes[half * slot_pairs + pair : half * slot_pairs + pair + 1, :]
                spot, place = code >> 10, code & (area - 1)
                both = jnp.concatenate(
                    [part[half * levels : (half + 1) * levels, :] for part in (hi, lo)], axis=0
                )
                lefts.append(
                    jnp.concatenate(
                        [
                            both * jnp.where(spot == s, 1.0, 0.0).astype(BF16)
                            for s in range(spots)
                        ],
                        axis=0,
                    )
                )
                rights.append(jnp.where(place_side == place, 1.0, 0.0).astype(BF16))
        term = dot_nt(jnp.concatenate(lefts, axis=1), jnp.concatenate(rights, axis=1))
        if r == 0:
            sums[...] = term
        else:
            sums[...] += term

    codes = None
    for r in range(R_CUTS):
        wait_for(got.at[r], ry_recv.at[r])
        if r == 0:
            codes = got[0, :, 0, :, :].reshape(devices, LANES).T.astype(jnp.int32) - 1
        add_rows(r, codes)

    per_spot = rows_y // spots
    for h in range(Y_CUTS):
        for y in range(h * cut, (h + 1) * cut):
            spot, lanes = y // per_spot, slice((y % per_spot) * LANES, (y % per_spot + 1) * LANES)
            top = spot * 2 * levels
            vert[y] = (
                vert[y] + sums[top : top + levels, lanes]
                + sums[top + levels : top + 2 * levels, lanes]
            )
        send_gx(
            lambda a: vert.at[y_span(h), pl.ds(a * own_levels, own_levels), :],
            x_in.at[gx, y_span(h)],
            xf_send.at[h], xf_recv.at[h],
        )
    for load in loads[1:]:
        load.wait()

    def times_table(lines, hi_table, lo_table, write):
        hi, lo = halves(lines)
        for block in range(length // TILE):
            cols = pl.ds(block * TILE, TILE)
            write(
                block,
                dot(hi, hi_table[:, cols]) + dot(lo, hi_table[:, cols]) + dot(hi, lo_table[:, cols]),
            )

    def level_sigma(first, count, waves):
        row = lax.broadcasted_iota(jnp.int32, (count, waves.shape[1]), 0)
        sigma = jnp.broadcast_to(waves, row.shape)
        for i in range(count):
            sigma = sigma + jnp.where(row == i, eigen[first + i], 0.0)
        return sigma

    ratio, scale = decay(level_sigma(gx * own_levels, own_levels, line[...]))

    def flat(ref, h):
        return ref[y_span(h)].reshape(cut * own_levels, length)

    ahead = jnp.zeros((own_levels, length), F32)
    for h in range(Y_CUTS):
        wait_for(x_in.at[:, y_span(h)], xf_recv.at[h])
        lines = jnp.concatenate(
            [x_in[a, y_span(h)].reshape(cut * own_levels, LANES) for a in range(n_gx)], axis=1
        )

        def set_spec(block, value):
            spec[y_span(h), :, block * TILE : (block + 1) * TILE] = value.reshape(
                cut, own_levels, TILE
            )

        times_table(lines, t_hi, t_lo, set_spec)
        for y in range(h * cut, (h + 1) * cut):
            ahead = spec[y] + ratio * ahead
            run[y] = ahead
    behind = jnp.zeros((own_levels, length), F32)
    for y in reversed(range(rows_y)):
        behind = ratio * behind
        run[y] += behind
        behind = spec[y] + behind

    groups = own_levels // 2
    for s in range(n_gy):
        top, lanes = s % groups * 2, slice(s // groups * LANES, (s // groups + 1) * LANES)
        edge_out[s, 0:2, :] = ahead[top : top + 2, lanes]
        edge_out[s, 2:4, :] = behind[top : top + 2, lanes]
    send_gy(lambda b: edge_out.at[b], edge_in.at[gy], edge_send, edge_recv)
    part = pl.ds(pl.multiple_of(gy // groups * LANES, LANES), LANES)
    one_ratio, _ = decay(
        level_sigma(gx * own_levels + lax.rem(gy, groups) * 2, 2, line[:, part])
    )
    hop = power(one_ratio, rows_y.bit_length() - 1)
    across = power(hop, n_gy.bit_length() - 1)
    wait_for(edge_in, edge_recv)
    right = jnp.zeros((2, LANES), F32)
    left = jnp.zeros((2, LANES), F32)
    for b in range(n_gy):
        right = edge_in[b, 0:2, :] + hop * right
        left = edge_in[n_gy - 1 - b, 2:4, :] + hop * left
    mirror = 1.0 / (1.0 - across * across)
    right, left = (left + across * right) * mirror, (right + across * left) * mirror
    for b in range(n_gy):
        inflow_out[b, 0:2, :] = right
        inflow_out[n_gy - 1 - b, 2:4, :] = left
        right = edge_in[b, 0:2, :] + hop * right
        left = edge_in[n_gy - 1 - b, 2:4, :] + hop * left
    send_gy(lambda b: inflow_out.at[b], inflow_in.at[gy], flow_send, flow_recv)
    wait_for(inflow_in, flow_recv)
    for s in range(n_gy):
        top, lanes = s % groups * 2, slice(s // groups * LANES, (s // groups + 1) * LANES)
        inflow[0, top : top + 2, lanes] = inflow_in[s, 0:2, :]
        inflow[1, top : top + 2, lanes] = inflow_in[s, 2:4, :]
    ahead = inflow[0]
    for y in range(rows_y):
        ahead = ratio * ahead
        run[y] += ahead
    behind = inflow[1]

    for h in reversed(range(Y_CUTS)):
        for y in reversed(range(h * cut, (h + 1) * cut)):
            behind = ratio * behind
            run[y] = (run[y] + behind) * scale

        def set_lines(block, value):
            for i in range(TILE // LANES):
                z_out[block * 2 + i, y_span(h)] = value[:, i * LANES : (i + 1) * LANES].reshape(
                    cut, own_levels, LANES
                )

        times_table(flat(run, h), c_hi, c_lo, set_lines)
        send_gx(
            lambda a: z_out.at[a, y_span(h)],
            phys.at[y_span(h), pl.ds(gx * own_levels, own_levels), :],
            xb_send.at[h], xb_recv.at[h],
        )

    def set_out(y, value):
        out[pl.ds(y, levels, stride=rows_y), :] = value

    for h in reversed(range(Y_CUTS)):
        wait_for(phys.at[y_span(h)], xb_recv.at[h])
        mix_levels(vbas[...], lambda y: phys[y], set_out, h)

    for r in range(R_CUTS):
        wait_for(relay.at[pl.ds(r * R_PLANES, R_PLANES), pl.ds(0, n_gx - 1)], rx_send.at[r])
        wait_for(got.at[r, pl.ds(0, n_gy - 1)], ry_send.at[r])
    for h in range(Y_CUTS):
        wait_for(x_in.at[pl.ds(0, n_gx - 1), y_span(h)], xf_send.at[h])
        wait_for(z_out.at[pl.ds(0, n_gx - 1), y_span(h)], xb_send.at[h])
    wait_for(edge_in.at[pl.ds(0, n_gy - 1)], edge_send)
    wait_for(inflow_in.at[pl.ds(0, n_gy - 1)], flow_send)


def per_device(
    forcing_field, innovations, owner_device, column_index, obs_weight, vert_inverse, vert_basis,
    vert_eigen,
):
    n_gx = lax.axis_size("gx")
    n_gy = lax.axis_size("gy")
    devices = n_gx * n_gy
    levels, rows_y, cols_x = forcing_field.shape
    row_total = innovations.shape[0]
    length = cols_x * n_gx
    (c_hi, c_lo), (t_hi, t_lo), line = wave_tables(length)
    own_levels = levels // n_gx
    planes = R_CUTS * R_PLANES
    vmem = pl.BlockSpec(memory_space=pltpu.VMEM)
    smem = pl.BlockSpec(memory_space=pltpu.SMEM)
    hbm = pl.BlockSpec(memory_space=pl.ANY)
    dma = pltpu.SemaphoreType.DMA
    out = pl.pallas_call(
        functools.partial(field_kernel, n_gx, n_gy, (4, 8)),
        out_shape=jax.ShapeDtypeStruct((levels * rows_y, cols_x), F32),
        in_specs=[hbm, vmem, vmem, vmem, vmem, vmem, vmem, smem, hbm, hbm, hbm, hbm, vmem],
        out_specs=vmem,
        scratch_shapes=[
            pltpu.VMEM((levels * rows_y, LANES), F32),
            pltpu.VMEM((length, length), BF16),
            pltpu.VMEM((length, length), BF16),
            pltpu.VMEM((length, length), BF16),
            pltpu.VMEM((length, length), BF16),
            pltpu.VMEM((devices, row_total), BF16),
            pltpu.VMEM((2 * LANES, row_total), BF16),
            pltpu.VMEM((planes, devices, LANES), F32),
            pltpu.VMEM((planes, n_gx, n_gy, LANES), F32),
            pltpu.VMEM((R_CUTS, n_gy, R_PLANES, n_gx, LANES), F32),
            pltpu.VMEM((R_CUTS, n_gy, R_PLANES, n_gx, LANES), F32),
            pltpu.VMEM((8 * levels, rows_y * cols_x // 4), F32),
            pltpu.VMEM((rows_y, levels, LANES), F32),
            pltpu.VMEM((n_gx, rows_y, own_levels, LANES), F32),
            pltpu.VMEM((rows_y, own_levels, length), F32),
            pltpu.VMEM((rows_y, own_levels, length), F32),
            pltpu.VMEM((n_gy, 4, LANES), F32),
            pltpu.VMEM((n_gy, 4, LANES), F32),
            pltpu.VMEM((n_gy, 4, LANES), F32),
            pltpu.VMEM((n_gy, 4, LANES), F32),
            pltpu.VMEM((2, own_levels, length), F32),
            pltpu.VMEM((n_gx, rows_y, own_levels, LANES), F32),
            pltpu.VMEM((rows_y, levels, LANES), F32),
            dma((5,)),
            dma((R_CUTS,)), dma((R_CUTS,)),
            dma((R_CUTS,)), dma((R_CUTS,)),
            dma((Y_CUTS,)), dma((Y_CUTS,)),
            dma(()), dma(()),
            dma(()), dma(()),
            dma((Y_CUTS,)), dma((Y_CUTS,)),
        ],
        compiler_params=pltpu.CompilerParams(
            collective_id=0, has_side_effects=True, vmem_limit_bytes=56 * 1024 * 1024
        ),
        name="field_solve",
    )(
        forcing_field.reshape(levels * rows_y, cols_x), innovations.T,
        owner_device.T, column_index.reshape(1, -1), obs_weight,
        vert_inverse, vert_basis, vert_eigen,
        t_hi, t_lo, c_hi, c_lo, line.reshape(1, -1),
    )
    return out.reshape(levels, rows_y, cols_x)


def solution(mesh):
    return jax.shard_map(
        per_device,
        mesh=mesh,
        in_specs=(
            P(None, "gy", "gx"),
            P(("gx", "gy"), None),
            P(("gx", "gy"), None),
            P(("gx", "gy")),
            P(),
            P(),
            P(),
            P(),
        ),
        out_specs=P(None, "gy", "gx"),
        check_vma=False,
    )
```

```python
import functools

import jax
import jax.numpy as jnp
import ml_dtypes
import numpy as np
from jax import lax
from jax.experimental import pallas as pl
from jax.experimental.pallas import tpu as pltpu
from jax.sharding import PartitionSpec as P

MESH = pl.DeviceIdType.MESH
F32 = jnp.float32
BF16 = jnp.bfloat16
LANES = 128
TILE = 256
CUTS = 2
SLOTS = 16
QUADS = 4
PAIRS = SLOTS // QUADS


def split_table(table):
    high = table.astype(np.float32).astype(ml_dtypes.bfloat16)
    low = (table - high.astype(np.float64)).astype(np.float32).astype(ml_dtypes.bfloat16)
    return high, low


def wave_tables(length):
    waves = np.arange(length, dtype=np.float64)
    scales = np.where(waves == 0, np.sqrt(1.0 / length), np.sqrt(2.0 / length))
    table = scales[:, None] * np.cos(np.pi * waves[:, None] * (2 * waves + 1) / (2 * length))
    line = 4.0 * np.sin(np.pi * waves / (2.0 * length)) ** 2
    return split_table(table), split_table(table.T), line.astype(np.float32)


def halves(value):
    high = value.astype(BF16)
    low = (value - high.astype(F32)).astype(BF16)
    return high, low


def dot(left, right):
    return jnp.dot(left, right, preferred_element_type=F32)


def dot_nt(left, right):
    return lax.dot_general(left, right, (((1,), (1,)), ((), ())), preferred_element_type=F32)


def wait_for(ref, sem):
    pltpu.make_async_copy(ref, ref, sem).wait()


def power(value, doublings):
    for _ in range(doublings):
        value = value * value
    return value


def decay(sigma):
    root = jnp.sqrt(sigma + 0.25 * sigma * sigma)
    return 1.0 / (1.0 + 0.5 * sigma + root), 0.5 / root


def field_kernel(
    n_gx, n_gy, gy_dims,
    field_hbm, innov, owner, column, weight, vinv, vbas, eigen,
    t_hi_hbm, t_lo_hbm, c_hi_hbm, c_lo_hbm, line,
    out,
    field, t_hi, t_lo, c_hi, c_lo,
    hots, expanded, slots, got, turned, rows_in, codes_out, codes_in, code_lines, codes, hot_x,
    vert, x_in, spec, run, edge_out, edge_in, flow_out, flow_in, z_out, phys,
    load_sem, cy_send, cy_recv, cx_send, cx_recv, ry_send, ry_recv, rx_send, rx_recv,
    xf_send, xf_recv, edge_send, edge_recv, flow_send, flow_recv, xb_send, xb_recv,
):
    gx = lax.axis_index("gx")
    gy = lax.axis_index("gy")
    n_hi, n_lo = gy_dims
    devices = n_gx * n_gy
    levels = vinv.shape[0]
    own = levels // n_gx
    few = own // CUTS
    steps = vert.shape[1]
    rows_y = 2 * steps
    length = t_hi.shape[0]
    chunks = owner.shape[1] // TILE
    tiles = length // LANES

    def iota(shape, axis):
        return lax.broadcasted_iota(jnp.int32, shape, axis)

    def gx_peer(step):
        return lax.rem(gx + step, n_gx)

    def gy_peer(step):
        high = lax.rem(gy // n_lo + step // n_lo, n_hi)
        low = lax.rem(gy + step, n_lo)
        return high * n_lo + low

    loads = [
        pltpu.make_async_copy(source, target, load_sem.at[i])
        for i, (source, target) in enumerate(
            [
                (field_hbm, field), (t_hi_hbm, t_hi), (t_lo_hbm, t_lo), (c_hi_hbm, c_hi),
                (c_lo_hbm, c_lo),
            ]
        )
    ]
    for load in loads:
        load.start()

    barrier = pltpu.get_barrier_semaphore()

    def greet_gx(step, carry):
        pl.semaphore_signal(barrier, inc=1, device_id=(gx_peer(step), gy), device_id_type=MESH)
        return carry

    def greet_gy(step, carry):
        pl.semaphore_signal(barrier, inc=1, device_id=(gx, gy_peer(step)), device_id_type=MESH)
        return carry

    lax.fori_loop(1, n_gy, greet_gy, 0)
    lax.fori_loop(1, n_gx, greet_gx, 0)

    def send_gx(source, target, send_sem, recv_sem):
        pltpu.make_async_copy(source(gx), target, recv_sem).start()

        def one(step, carry):
            peer = gx_peer(step)
            pltpu.make_async_remote_copy(
                src_ref=source(peer), dst_ref=target, send_sem=send_sem, recv_sem=recv_sem,
                device_id=(peer, gy), device_id_type=MESH,
            ).start()
            return carry

        lax.fori_loop(1, n_gx, one, 0)

    def send_gy(source, target, send_sem, recv_sem):
        pltpu.make_async_copy(source(gy), target, recv_sem).start()

        def one(step, carry):
            peer = gy_peer(step)
            pltpu.make_async_remote_copy(
                src_ref=source(peer), dst_ref=target, send_sem=send_sem, recv_sem=recv_sem,
                device_id=(gx, peer), device_id_type=MESH,
            ).start()
            return carry

        lax.fori_loop(1, n_gy, one, 0)

    def exact(left, right, dims):
        return lax.dot_general(
            left, right, (dims, ((), ())), precision=lax.Precision.HIGHEST,
            preferred_element_type=F32,
        )

    side = iota((devices, TILE), 0)

    def lanes_of(chunk):
        return slice(chunk * TILE, (chunk + 1) * TILE)

    def number_rows():
        before = jnp.where(iota((TILE, TILE), 0) < iota((TILE, TILE), 1), 1.0, 0.0).astype(BF16)
        seen = jnp.zeros((devices, 1), F32)
        ranks = []
        for chunk in range(chunks):
            name = owner[:, lanes_of(chunk)]
            peer = lax.rem(name, n_gy) * n_gx + name // n_gy
            hot = jnp.where(side == peer, 1.0, 0.0)
            narrow = hot.astype(BF16)
            hots[:, lanes_of(chunk)] = narrow
            earlier = dot(narrow, before) + seen
            ranks.append(jnp.sum(hot * earlier, axis=0, keepdims=True).astype(jnp.int32))
            seen = seen + jnp.sum(hot, axis=1, keepdims=True)
        return ranks

    def place_codes(ranks):
        lane_side = iota((LANES, TILE), 0)
        gy_side = iota((n_gy, TILE), 0)
        high = jnp.zeros((n_gy, LANES), F32)
        low = jnp.zeros((n_gy, LANES), F32)
        for chunk in range(chunks):
            name = owner[:, lanes_of(chunk)]
            rank = ranks[chunk]
            lane = (rank // QUADS * n_gx + name // n_gy) * QUADS + rank % QUADS
            code = column[:, lanes_of(chunk)] + 1
            here = lane_side == lane
            hot = jnp.where(gy_side == lax.rem(name, n_gy), 1.0, 0.0).astype(BF16)
            high += dot_nt(hot, jnp.where(here, (code >> 6).astype(F32), 0.0).astype(BF16))
            low += dot_nt(hot, jnp.where(here, (code & 63).astype(F32), 0.0).astype(BF16))
        codes_out[:, 0, :] = high * 64.0 + low

    def weigh_rows(ranks, c):
        place = iota((LANES, levels), 0)
        pick = place // (QUADS * few) * own + c * few + place % few
        chosen = jnp.where(iota((LANES, levels), 1) == pick, 1.0, 0.0)
        mixed = exact(vinv[...], weight[...], ((1,), (1,)))
        w_hi, w_lo = halves(exact(chosen, mixed, ((1,), (0,))))
        stack = jnp.concatenate([w_hi, w_hi, w_lo], axis=1)
        quad = iota((LANES, TILE), 0) // few % QUADS
        for chunk in range(chunks):
            hi, lo = halves(innov[:, lanes_of(chunk)])
            rows_m = dot(stack, jnp.concatenate([hi, lo, hi], axis=0))
            hi, lo = halves(jnp.where(quad == ranks[chunk] % QUADS, rows_m, 0.0))
            expanded[:LANES, lanes_of(chunk)] = hi
            expanded[LANES:, lanes_of(chunk)] = lo

    def place_rows(ranks, c, pair):
        total = jnp.zeros((devices, TILE), F32)
        for chunk in range(chunks):
            mask = jnp.where(ranks[chunk] // QUADS == pair, 1.0, 0.0).astype(BF16)
            total += dot_nt(hots[:, lanes_of(chunk)] * mask, expanded[:, lanes_of(chunk)])
        slots[c, pair] = total[:, :LANES] + total[:, LANES:]

    ranks = number_rows()
    place_codes(ranks)
    for c in range(CUTS):
        weigh_rows(ranks, c)
        for pair in range(PAIRS):
            place_rows(ranks, c, pair)
        if c == 0:
            pl.semaphore_wait(barrier, n_gx - 1 + n_gy - 1)
            send_gy(lambda b: codes_out.at[b], codes_in.at[gy], cy_send, cy_recv)
        send_gy(
            lambda b: slots.at[c, :, pl.ds(b * n_gx, n_gx), :],
            got.at[c, gy], ry_send.at[c], ry_recv.at[c],
        )

    width = 2 * levels
    place = iota((width, levels), 0)
    pick = place // (2 * few) % n_gx * own + place // (width // CUTS) * few + place % few
    chosen = jnp.where(iota((width, levels), 1) == pick, 1.0, 0.0)
    upper = (place // few) % 2

    def mix_lines(matrix, read, write):
        m_hi, m_lo = halves(matrix)
        stack = jnp.concatenate([m_hi, m_hi, m_lo], axis=1)
        for j in range(0, steps, 2):
            hi, lo = halves(jnp.concatenate([read(j), read(j + 1)], axis=1))
            mixed = dot(stack, jnp.concatenate([hi, lo, hi], axis=0))
            write(j, mixed[:, :LANES])
            write(j + 1, mixed[:, LANES:])

    def read_field(j):
        return jnp.concatenate(
            [field[pl.ds(half * steps + j, levels, stride=rows_y), :] for half in range(2)], axis=0
        )

    def write_vert(j, value):
        for c in range(CUTS):
            vert[c, j] = value[c * levels : (c + 1) * levels, :]

    into = exact(chosen, vinv[...], ((1,), (0,)))
    into = jnp.concatenate([jnp.where(upper == half, into, 0.0) for half in range(2)], axis=1)
    loads[0].wait()
    mix_lines(into, read_field, write_vert)
    for c in range(CUTS):
        send_gx(
            lambda a: vert.at[c, :, pl.ds(a * own, own), :],
            x_in.at[c, gx], xf_send.at[c], xf_recv.at[c],
        )

    wait_for(codes_in, cy_recv)
    turned_codes = codes_in[:, 0, :].T
    group = n_gx * QUADS
    code_lines[...] = jnp.concatenate(
        [turned_codes[pair * group : (pair + 1) * group, :] for pair in range(PAIRS)], axis=1
    )
    send_gx(lambda a: code_lines, codes.at[gx], cx_send, cx_recv)
    for load in loads[1:]:
        load.wait()
    wait_for(codes, cx_recv)
    wide = QUADS * LANES
    x_side = iota((2 * LANES, wide), 0)

    def slot_codes(a, block):
        return jnp.concatenate(
            [codes[a, pl.ds(block * QUADS + quad, 1), :] for quad in range(QUADS)], axis=1
        ).astype(jnp.int32) - 1

    def mark_x(block, carry):
        for a in range(n_gx):
            code = slot_codes(a, block)
            spot = (code // (steps * LANES)) * LANES + (code & (LANES - 1))
            spot = jnp.where(code < 0, -1, spot)
            hot_x[block, :, a * wide : (a + 1) * wide] = jnp.where(x_side == spot, 1.0, 0.0).astype(
                BF16
            )
        return carry

    lax.fori_loop(0, n_gx, mark_x, 0)

    def turn(c):
        wait_for(got.at[c], ry_recv.at[c])
        lines = got.at[c].reshape(n_gy * PAIRS * n_gx, LANES)
        for block in range(n_gx):
            flat = jnp.concatenate(
                [
                    lines[pl.ds(pair * n_gx + block, n_gy, stride=PAIRS * n_gx), :]
                    for pair in range(PAIRS)
                ],
                axis=0,
            )
            turned[c, :, block] = flat.T.reshape(n_gx, 2, 2 * few, LANES)
        send_gx(lambda a: turned.at[c, a], rows_in.at[c, gx], rx_send.at[c], rx_recv.at[c])

    lower = iota((2 * few, LANES), 0) < few

    def add_rows(c):
        def one(block, carry):
            total = jnp.zeros((steps * 2 * few, 2 * LANES), F32)
            for a in range(n_gx):
                step_of = (slot_codes(a, block) // LANES) & (steps - 1)
                parts = []
                for quad in range(QUADS):
                    data = rows_in[c, a, block, quad // 2]
                    hi = data.astype(BF16).astype(F32)
                    lo = data - hi
                    if quad % 2 == 0:
                        both = jnp.where(lower, hi, pltpu.roll(lo, few, 0))
                    else:
                        both = jnp.where(lower, pltpu.roll(hi, few, 0), lo)
                    at = step_of[:, quad * LANES : (quad + 1) * LANES]
                    parts.append(
                        jnp.concatenate(
                            [jnp.where(at == j, both, 0.0) for j in range(steps)], axis=0
                        ).astype(BF16)
                    )
                total += dot_nt(
                    jnp.concatenate(parts, axis=1), hot_x[block, :, a * wide : (a + 1) * wide]
                )
            for j in range(steps):
                both = total[j * 2 * few : (j + 1) * 2 * few, :]
                both = both + pltpu.roll(both, few, 0)
                x_in[c, block, j] += jnp.where(lower, both[:, :LANES], both[:, LANES:])
            return carry

        lax.fori_loop(0, n_gx, one, 0)

    def times_table(lines, hi_table, lo_table, write):
        hi, lo = halves(lines)
        for block in range(length // TILE):
            cols = pl.ds(block * TILE, TILE)
            write(
                block,
                dot(hi, hi_table[:, cols]) + dot(lo, hi_table[:, cols]) + dot(hi, lo_table[:, cols]),
            )

    def level_sigma(c, waves):
        row = iota((2 * few, waves.shape[1]), 0) % few
        sigma = jnp.broadcast_to(waves, row.shape)
        for i in range(few):
            sigma = sigma + jnp.where(row == i, eigen[gx * own + c * few + i], 0.0)
        return sigma

    first = iota((2 * few, length), 0) < few

    def swap(value):
        return pltpu.roll(value, few, 0)

    def solver(c, tile):
        return (tile + 2 * c) % n_hi * n_lo + tile

    def forward(c):
        lines = jnp.concatenate(
            [x_in[c, a].reshape(steps * 2 * few, LANES) for a in range(n_gx)], axis=1
        )

        def set_spec(block, value):
            spec[c, :, :, block * TILE : (block + 1) * TILE] = value.reshape(steps, 2 * few, TILE)

        times_table(lines, t_hi, t_lo, set_spec)
        ratio, scale = decay(level_sigma(c, line[...]))
        jump = power(ratio, steps.bit_length() - 1)
        ahead = jnp.zeros((2 * few, length), F32)
        for j in range(steps):
            ahead = spec[c, j] + ratio * ahead
            run[c, j] = ahead
        behind = jnp.zeros((2 * few, length), F32)
        for j in reversed(range(steps)):
            behind = ratio * behind
            run[c, j] += behind
            behind = spec[c, j] + behind
        edges = jnp.where(first, behind + jump * swap(behind), ahead + jump * swap(ahead))
        for tile in range(tiles):
            edge_out[c, tile] = edges[:, tile * LANES : (tile + 1) * LANES]
        for tile in range(tiles):
            target = solver(c, tile)

            @pl.when(gy == target)
            def _():
                pltpu.make_async_copy(edge_out.at[c, tile], edge_in.at[c, gy], edge_recv.at[c]).start()

            @pl.when(gy != target)
            def _():
                pltpu.make_async_remote_copy(
                    src_ref=edge_out.at[c, tile], dst_ref=edge_in.at[c, gy],
                    send_sem=edge_send.at[c], recv_sem=edge_recv.at[c],
                    device_id=(gx, target), device_id_type=MESH,
                ).start()

        return ratio, scale, jump, ahead, behind

    def solve_edges(c):
        tile = lax.rem(gy, n_lo)
        mine = gy // n_lo == lax.rem(tile + 2 * c, n_hi)

        @pl.when(mine)
        def _():
            part = pl.ds(pl.multiple_of(tile * LANES, LANES), LANES)
            ratio, _ = decay(level_sigma(c, line[:, part]))
            hop = power(ratio, rows_y.bit_length() - 1)
            across = power(hop, n_gy.bit_length() - 1)
            wait_for(edge_in.at[c], edge_recv.at[c])
            right = jnp.zeros((2 * few, LANES), F32)
            left = jnp.zeros((2 * few, LANES), F32)
            for b in range(n_gy):
                right = edge_in[c, b] + hop * right
                left = edge_in[c, n_gy - 1 - b] + hop * left
            mirror = 1.0 / (1.0 - across * across)
            right, left = (
                (swap(left) + across * right) * mirror, (swap(right) + across * left) * mirror
            )
            for b in range(n_gy):
                flow_out[c, b, few:, :] = right[few:, :]
                flow_out[c, n_gy - 1 - b, :few, :] = left[:few, :]
                right = edge_in[c, b] + hop * right
                left = edge_in[c, n_gy - 1 - b] + hop * left
            send_gy(
                lambda b: flow_out.at[c, b], flow_in.at[c, tile], flow_send.at[c], flow_recv.at[c]
            )

    def backward(c, ratio, scale, jump, ahead, behind):
        wait_for(flow_in.at[c], flow_recv.at[c])
        flow = jnp.concatenate([flow_in[c, tile] for tile in range(tiles)], axis=1)
        ahead, behind = (
            jnp.where(first, swap(flow), jump * flow + swap(ahead)),
            jnp.where(first, jump * flow + swap(behind), swap(flow)),
        )
        for j in range(steps):
            ahead = ratio * ahead
            run[c, j] += ahead
        for j in reversed(range(steps)):
            behind = ratio * behind
            run[c, j] = (run[c, j] + behind) * scale

        def set_lines(block, value):
            for i in range(TILE // LANES):
                z_out[c, block * 2 + i] = value[:, i * LANES : (i + 1) * LANES].reshape(
                    steps, 2 * few, LANES
                )

        times_table(run[c].reshape(steps * 2 * few, length), c_hi, c_lo, set_lines)
        send_gx(
            lambda a: z_out.at[c, a], phys.at[c, :, pl.ds(gx * own, own), :],
            xb_send.at[c], xb_recv.at[c],
        )

    for c in range(CUTS):
        turn(c)
    kept = []
    for c in range(CUTS):
        wait_for(x_in.at[c], xf_recv.at[c])
        wait_for(rows_in.at[c], rx_recv.at[c])
        add_rows(c)
        kept.append(forward(c))
    for c in range(CUTS):
        solve_edges(c)
    for c in range(CUTS):
        backward(c, *kept[c])

    out_of = exact(vbas[...], chosen, ((1,), (1,)))
    half_of = (iota((levels, width), 1) // few) % 2
    out_of = jnp.concatenate([jnp.where(half_of == half, out_of, 0.0) for half in range(2)], axis=0)

    def read_phys(j):
        return jnp.concatenate([phys[c, j] for c in range(CUTS)], axis=0)

    def write_out(j, value):
        for half in range(2):
            out[pl.ds(half * steps + j, levels, stride=rows_y), :] = value[
                half * levels : (half + 1) * levels, :
            ]

    for c in range(CUTS):
        wait_for(phys.at[c], xb_recv.at[c])
    mix_lines(out_of, read_phys, write_out)

    wait_for(codes_in.at[pl.ds(0, n_gy - 1)], cy_send)
    wait_for(codes.at[pl.ds(0, n_gx - 1)], cx_send)
    for c in range(CUTS):
        wait_for(got.at[c, pl.ds(0, n_gy - 1)], ry_send.at[c])
        wait_for(rows_in.at[c, pl.ds(0, n_gx - 1)], rx_send.at[c])
        wait_for(x_in.at[c, pl.ds(0, n_gx - 1)], xf_send.at[c])
        wait_for(z_out.at[c, pl.ds(0, n_gx - 1)], xb_send.at[c])
        mine = gy // n_lo == lax.rem(lax.rem(gy, n_lo) + 2 * c, n_hi)

        @pl.when(mine)
        def _():
            wait_for(edge_out.at[c, pl.ds(0, tiles - 1)], edge_send.at[c])
            wait_for(flow_out.at[c, pl.ds(0, n_gy - 1)], flow_send.at[c])

        @pl.when(jnp.logical_not(mine))
        def _():
            wait_for(edge_out.at[c], edge_send.at[c])


def per_device(
    forcing_field, innovations, owner_device, column_index, obs_weight, vert_inverse, vert_basis,
    vert_eigen,
):
    n_gx = lax.axis_size("gx")
    n_gy = lax.axis_size("gy")
    devices = n_gx * n_gy
    levels, rows_y, cols_x = forcing_field.shape
    row_total = innovations.shape[0]
    length = cols_x * n_gx
    (c_hi, c_lo), (t_hi, t_lo), line = wave_tables(length)
    own = levels // n_gx
    steps = rows_y // 2
    few = own // CUTS
    tiles = length // LANES
    vmem = pl.BlockSpec(memory_space=pltpu.VMEM)
    smem = pl.BlockSpec(memory_space=pltpu.SMEM)
    hbm = pl.BlockSpec(memory_space=pl.ANY)
    dma = pltpu.SemaphoreType.DMA

    def buffer(*shape, dtype=F32):
        return pltpu.VMEM(shape, dtype)

    table = buffer(length, length, dtype=BF16)
    out = pl.pallas_call(
        functools.partial(field_kernel, n_gx, n_gy, (4, 8)),
        out_shape=jax.ShapeDtypeStruct((levels * rows_y, cols_x), F32),
        in_specs=[hbm, vmem, vmem, vmem, vmem, vmem, vmem, smem, hbm, hbm, hbm, hbm, vmem],
        out_specs=vmem,
        scratch_shapes=[
            buffer(levels * rows_y, LANES), table, table, table, table,
            buffer(devices, row_total, dtype=BF16),
            buffer(2 * LANES, row_total, dtype=BF16),
            buffer(CUTS, PAIRS, devices, LANES),
            buffer(CUTS, n_gy, PAIRS, n_gx, LANES),
            buffer(CUTS, n_gx, n_gx, 2, 2 * few, LANES),
            buffer(CUTS, n_gx, n_gx, 2, 2 * few, LANES),
            buffer(n_gy, 1, LANES),
            buffer(n_gy, 1, LANES),
            buffer(n_gx * QUADS, LANES),
            buffer(n_gx, n_gx * QUADS, LANES),
            buffer(n_gx, 2 * LANES, n_gx * QUADS * LANES, dtype=BF16),
            buffer(CUTS, steps, n_gx * 2 * few, LANES),
            buffer(CUTS, n_gx, steps, 2 * few, LANES),
            buffer(CUTS, steps, 2 * few, length),
            buffer(CUTS, steps, 2 * few, length),
            buffer(CUTS, tiles, 2 * few, LANES),
            buffer(CUTS, n_gy, 2 * few, LANES),
            buffer(CUTS, n_gy, 2 * few, LANES),
            buffer(CUTS, tiles, 2 * few, LANES),
            buffer(CUTS, n_gx, steps, 2 * few, LANES),
            buffer(CUTS, steps, n_gx * 2 * few, LANES),
            dma((5,)),
            dma(()), dma(()),
            dma(()), dma(()),
            dma((CUTS,)), dma((CUTS,)),
            dma((CUTS,)), dma((CUTS,)),
            dma((CUTS,)), dma((CUTS,)),
            dma((CUTS,)), dma((CUTS,)),
            dma((CUTS,)), dma((CUTS,)),
            dma((CUTS,)), dma((CUTS,)),
        ],
        compiler_params=pltpu.CompilerParams(
            collective_id=0, has_side_effects=True, vmem_limit_bytes=56 * 1024 * 1024
        ),
        name="field_solve",
    )(
        forcing_field.reshape(levels * rows_y, cols_x), innovations.T,
        owner_device.T, column_index.reshape(1, -1), obs_weight,
        vert_inverse, vert_basis, vert_eigen,
        t_hi, t_lo, c_hi, c_lo, line.reshape(1, -1),
    )
    return out.reshape(levels, rows_y, cols_x)


def solution(mesh):
    return jax.shard_map(
        per_device,
        mesh=mesh,
        in_specs=(
            P(None, "gy", "gx"),
            P(("gx", "gy"), None),
            P(("gx", "gy"), None),
            P(("gx", "gy")),
            P(),
            P(),
            P(),
            P(),
        ),
        out_specs=P(None, "gy", "gx"),
        check_vma=False,
    )
```

```python
import functools

import jax
import jax.numpy as jnp
import ml_dtypes
import numpy as np
from jax import lax
from jax.experimental import pallas as pl
from jax.experimental.pallas import tpu as pltpu
from jax.sharding import PartitionSpec as P

MESH = pl.DeviceIdType.MESH
F32 = jnp.float32
BF16 = jnp.bfloat16
LANES = 128
TILE = 256
CUTS = 2
SLOTS = 16
QUADS = 4
PAIRS = SLOTS // QUADS


def split_table(table):
    high = table.astype(np.float32).astype(ml_dtypes.bfloat16)
    low = (table - high.astype(np.float64)).astype(np.float32).astype(ml_dtypes.bfloat16)
    return high, low


def wave_tables(length):
    waves = np.arange(length, dtype=np.float64)
    scales = np.where(waves == 0, np.sqrt(1.0 / length), np.sqrt(2.0 / length))
    table = scales[:, None] * np.cos(np.pi * waves[:, None] * (2 * waves + 1) / (2 * length))
    line = 4.0 * np.sin(np.pi * waves / (2.0 * length)) ** 2
    return split_table(table), split_table(table.T), line.astype(np.float32)


def halves(value):
    high = value.astype(BF16)
    low = (value - high.astype(F32)).astype(BF16)
    return high, low


def dot(left, right):
    return jnp.dot(left, right, preferred_element_type=F32)


def dot_nt(left, right):
    return lax.dot_general(left, right, (((1,), (1,)), ((), ())), preferred_element_type=F32)


def wait_for(ref, sem):
    pltpu.make_async_copy(ref, ref, sem).wait()


def power(value, doublings):
    for _ in range(doublings):
        value = value * value
    return value


def decay(sigma):
    root = jnp.sqrt(sigma + 0.25 * sigma * sigma)
    return 1.0 / (1.0 + 0.5 * sigma + root), 0.5 / root


def field_kernel(
    n_gx, n_gy, gy_dims,
    field_hbm, innov, owner, column, weight, vinv, vbas, eigen,
    t_hi_hbm, t_lo_hbm, c_hi_hbm, c_lo_hbm, line,
    out,
    field, t_hi, t_lo, c_hi, c_lo,
    hots, expanded, slots, got, turned, rows_in, codes_out, codes_in, code_lines, codes, hot_x,
    vert, x_in, spec, run, edge_out, edge_in, flow_out, flow_in, z_out, phys,
    load_sem, cy_send, cy_recv, cx_send, cx_recv, ry_send, ry_recv, rx_send, rx_recv,
    xf_send, xf_recv, edge_send, edge_recv, flow_send, flow_recv, xb_send, xb_recv,
):
    gx = lax.axis_index("gx")
    gy = lax.axis_index("gy")
    n_hi, n_lo = gy_dims
    devices = n_gx * n_gy
    levels = vinv.shape[0]
    own = levels // n_gx
    few = own // CUTS
    steps = vert.shape[1]
    rows_y = 2 * steps
    length = t_hi.shape[0]
    chunks = owner.shape[1] // TILE
    tiles = length // LANES

    def iota(shape, axis):
        return lax.broadcasted_iota(jnp.int32, shape, axis)

    def gx_peer(step):
        return lax.rem(gx + step, n_gx)

    def gy_peer(step):
        high = lax.rem(gy // n_lo + step // n_lo, n_hi)
        low = lax.rem(gy + step, n_lo)
        return high * n_lo + low

    loads = [
        pltpu.make_async_copy(source, target, load_sem.at[i])
        for i, (source, target) in enumerate(
            [
                (field_hbm, field), (t_hi_hbm, t_hi), (t_lo_hbm, t_lo), (c_hi_hbm, c_hi),
                (c_lo_hbm, c_lo),
            ]
        )
    ]
    for load in loads:
        load.start()

    barrier = pltpu.get_barrier_semaphore()

    def greet_gx(step, carry):
        pl.semaphore_signal(barrier, inc=1, device_id=(gx_peer(step), gy), device_id_type=MESH)
        return carry

    def greet_gy(step, carry):
        pl.semaphore_signal(barrier, inc=1, device_id=(gx, gy_peer(step)), device_id_type=MESH)
        return carry

    lax.fori_loop(1, n_gy, greet_gy, 0)
    lax.fori_loop(1, n_gx, greet_gx, 0)

    def send_gx(source, target, send_sem, recv_sem):
        pltpu.make_async_copy(source(gx), target, recv_sem).start()

        def one(step, carry):
            peer = gx_peer(step)
            pltpu.make_async_remote_copy(
                src_ref=source(peer), dst_ref=target, send_sem=send_sem, recv_sem=recv_sem,
                device_id=(peer, gy), device_id_type=MESH,
            ).start()
            return carry

        lax.fori_loop(1, n_gx, one, 0)

    def send_gy(source, target, send_sem, recv_sem):
        pltpu.make_async_copy(source(gy), target, recv_sem).start()

        def one(step, carry):
            peer = gy_peer(step)
            pltpu.make_async_remote_copy(
                src_ref=source(peer), dst_ref=target, send_sem=send_sem, recv_sem=recv_sem,
                device_id=(gx, peer), device_id_type=MESH,
            ).start()
            return carry

        lax.fori_loop(1, n_gy, one, 0)

    def exact(left, right, dims):
        return lax.dot_general(
            left, right, (dims, ((), ())), precision=lax.Precision.HIGHEST,
            preferred_element_type=F32,
        )

    side = iota((devices, TILE), 0)

    def lanes_of(chunk):
        return slice(chunk * TILE, (chunk + 1) * TILE)

    def number_rows():
        before = jnp.where(iota((TILE, TILE), 0) < iota((TILE, TILE), 1), 1.0, 0.0).astype(BF16)
        seen = jnp.zeros((devices, 1), F32)
        ranks = []
        for chunk in range(chunks):
            name = owner[:, lanes_of(chunk)]
            peer = lax.rem(name, n_gy) * n_gx + name // n_gy
            hot = jnp.where(side == peer, 1.0, 0.0)
            narrow = hot.astype(BF16)
            hots[:, lanes_of(chunk)] = narrow
            earlier = dot(narrow, before) + seen
            ranks.append(jnp.sum(hot * earlier, axis=0, keepdims=True).astype(jnp.int32))
            seen = seen + jnp.sum(hot, axis=1, keepdims=True)
        return ranks

    def place_codes(ranks):
        lane_side = iota((LANES, TILE), 0)
        gy_side = iota((n_gy, TILE), 0)
        high = jnp.zeros((n_gy, LANES), F32)
        low = jnp.zeros((n_gy, LANES), F32)
        for chunk in range(chunks):
            name = owner[:, lanes_of(chunk)]
            rank = ranks[chunk]
            lane = (rank // QUADS * n_gx + name // n_gy) * QUADS + rank % QUADS
            code = column[:, lanes_of(chunk)] + 1
            here = lane_side == lane
            hot = jnp.where(gy_side == lax.rem(name, n_gy), 1.0, 0.0).astype(BF16)
            high += dot_nt(hot, jnp.where(here, (code >> 6).astype(F32), 0.0).astype(BF16))
            low += dot_nt(hot, jnp.where(here, (code & 63).astype(F32), 0.0).astype(BF16))
        codes_out[:, 0, :] = high * 64.0 + low

    def weigh_rows(ranks, c):
        place = iota((LANES, levels), 0)
        pick = place // (QUADS * few) * own + c * few + place % few
        chosen = jnp.where(iota((LANES, levels), 1) == pick, 1.0, 0.0)
        mixed = exact(vinv[...], weight[...], ((1,), (1,)))
        w_hi, w_lo = halves(exact(chosen, mixed, ((1,), (0,))))
        stack = jnp.concatenate([w_hi, w_hi, w_lo], axis=1)
        quad = iota((LANES, TILE), 0) // few % QUADS
        for chunk in range(chunks):
            hi, lo = halves(innov[:, lanes_of(chunk)])
            rows_m = dot(stack, jnp.concatenate([hi, lo, hi], axis=0))
            hi, lo = halves(jnp.where(quad == ranks[chunk] % QUADS, rows_m, 0.0))
            expanded[:LANES, lanes_of(chunk)] = hi
            expanded[LANES:, lanes_of(chunk)] = lo

    def place_rows(ranks, c, pair):
        total = jnp.zeros((devices, TILE), F32)
        for chunk in range(chunks):
            mask = jnp.where(ranks[chunk] // QUADS == pair, 1.0, 0.0).astype(BF16)
            total += dot_nt(hots[:, lanes_of(chunk)] * mask, expanded[:, lanes_of(chunk)])
        slots[c, pair] = total[:, :LANES] + total[:, LANES:]

    ranks = number_rows()
    place_codes(ranks)
    for c in range(CUTS):
        weigh_rows(ranks, c)
        for pair in range(PAIRS):
            place_rows(ranks, c, pair)
        if c == 0:
            pl.semaphore_wait(barrier, n_gx - 1 + n_gy - 1)
            send_gy(lambda b: codes_out.at[b], codes_in.at[gy], cy_send, cy_recv)
        send_gy(
            lambda b: slots.at[c, :, pl.ds(b * n_gx, n_gx), :],
            got.at[c, gy], ry_send.at[c], ry_recv.at[c],
        )

    width = 2 * levels
    place = iota((width, levels), 0)
    pick = place // (2 * few) % n_gx * own + place // (width // CUTS) * few + place % few
    chosen = jnp.where(iota((width, levels), 1) == pick, 1.0, 0.0)
    upper = (place // few) % 2

    def mix_lines(matrix, read, write):
        m_hi, m_lo = halves(matrix)
        stack = jnp.concatenate([m_hi, m_hi, m_lo], axis=1)
        for j in range(0, steps, 2):
            hi, lo = halves(jnp.concatenate([read(j), read(j + 1)], axis=1))
            mixed = dot(stack, jnp.concatenate([hi, lo, hi], axis=0))
            write(j, mixed[:, :LANES])
            write(j + 1, mixed[:, LANES:])

    def read_field(j):
        return jnp.concatenate(
            [field[pl.ds(half * steps + j, levels, stride=rows_y), :] for half in range(2)], axis=0
        )

    def write_vert(j, value):
        for c in range(CUTS):
            vert[c, j] = value[c * levels : (c + 1) * levels, :]

    into = exact(chosen, vinv[...], ((1,), (0,)))
    into = jnp.concatenate([jnp.where(upper == half, into, 0.0) for half in range(2)], axis=1)
    loads[0].wait()
    mix_lines(into, read_field, write_vert)
    for c in range(CUTS):
        send_gx(
            lambda a: vert.at[c, :, pl.ds(a * own, own), :],
            x_in.at[c, gx], xf_send.at[c], xf_recv.at[c],
        )

    wait_for(codes_in, cy_recv)
    turned_codes = codes_in[:, 0, :].T
    group = n_gx * QUADS
    code_lines[...] = jnp.concatenate(
        [turned_codes[pair * group : (pair + 1) * group, :] for pair in range(PAIRS)], axis=1
    )
    send_gx(lambda a: code_lines, codes.at[gx], cx_send, cx_recv)
    for load in loads[1:]:
        load.wait()
    wait_for(codes, cx_recv)
    wide = QUADS * LANES
    x_lane = iota((LANES, 2 * LANES), 1).astype(F32)

    def mark_x(a, carry):
        code = codes[a].astype(jnp.int32) - 1
        spot = code // (steps * LANES) * LANES + (code & (LANES - 1))
        spot = jnp.where(code < 0, -1, spot).astype(F32)
        for row in range(n_gx * QUADS):
            block, quad = divmod(row, QUADS)
            down = jnp.broadcast_to(spot[row : row + 1, :], (LANES, LANES)).T
            down = jnp.concatenate([down, down], axis=1)
            rows = pl.ds(pl.multiple_of(a * wide + quad * LANES, LANES), LANES)
            hot_x[block, rows, :] = jnp.where(down == x_lane, 1.0, 0.0).astype(BF16)
        return carry

    lax.fori_loop(0, n_gx, mark_x, 0)

    def turn(c):
        wait_for(got.at[c], ry_recv.at[c])
        lines = got.at[c].reshape(n_gy * PAIRS * n_gx, LANES)
        for block in range(n_gx):
            flat = jnp.concatenate(
                [
                    lines[pl.ds(pair * n_gx + block, n_gy, stride=PAIRS * n_gx), :]
                    for pair in range(PAIRS)
                ],
                axis=0,
            )
            turned[c, :, block] = flat.T.reshape(n_gx, 2, 2 * few, LANES)
        send_gx(lambda a: turned.at[c, a], rows_in.at[c, gx], rx_send.at[c], rx_recv.at[c])

    lower = iota((2 * few, LANES), 0) < few

    def add_rows(c):
        def one(block, carry):
            total = jnp.zeros((steps * 2 * few, 2 * LANES), F32)
            for a in range(n_gx):
                parts = []
                for quad in range(QUADS):
                    data = rows_in[c, a, block, quad // 2]
                    hi = data.astype(BF16).astype(F32)
                    lo = data - hi
                    if quad % 2 == 0:
                        both = jnp.where(lower, hi, pltpu.roll(lo, few, 0))
                    else:
                        both = jnp.where(lower, pltpu.roll(hi, few, 0), lo)
                    code = codes[a, pl.ds(block * QUADS + quad, 1), :].astype(jnp.int32) - 1
                    at = jnp.broadcast_to((code // LANES) & (steps - 1), (2 * few, LANES))
                    parts.append(
                        jnp.concatenate(
                            [jnp.where(at == j, both, 0.0) for j in range(steps)], axis=0
                        ).astype(BF16)
                    )
                total += dot(
                    jnp.concatenate(parts, axis=1), hot_x[block, a * wide : (a + 1) * wide, :]
                )
            for j in range(steps):
                both = total[j * 2 * few : (j + 1) * 2 * few, :]
                both = both + pltpu.roll(both, few, 0)
                x_in[c, block, j] += jnp.where(lower, both[:, :LANES], both[:, LANES:])
            return carry

        lax.fori_loop(0, n_gx, one, 0)

    def times_table(lines, hi_table, lo_table, write):
        hi, lo = halves(lines)
        for block in range(length // TILE):
            cols = pl.ds(block * TILE, TILE)
            write(
                block,
                dot(hi, hi_table[:, cols]) + dot(lo, hi_table[:, cols]) + dot(hi, lo_table[:, cols]),
            )

    def level_sigma(c, waves):
        row = iota((2 * few, waves.shape[1]), 0) % few
        sigma = jnp.broadcast_to(waves, row.shape)
        for i in range(few):
            sigma = sigma + jnp.where(row == i, eigen[gx * own + c * few + i], 0.0)
        return sigma

    first = iota((2 * few, length), 0) < few

    def swap(value):
        return pltpu.roll(value, few, 0)

    def solver(c, tile):
        return (tile + 2 * c) % n_hi * n_lo + tile

    def forward(c):
        lines = jnp.concatenate(
            [x_in[c, a].reshape(steps * 2 * few, LANES) for a in range(n_gx)], axis=1
        )

        def set_spec(block, value):
            spec[c, :, :, block * TILE : (block + 1) * TILE] = value.reshape(steps, 2 * few, TILE)

        times_table(lines, t_hi, t_lo, set_spec)
        ratio, scale = decay(level_sigma(c, line[...]))
        jump = power(ratio, steps.bit_length() - 1)
        ahead = jnp.zeros((2 * few, length), F32)
        for j in range(steps):
            ahead = spec[c, j] + ratio * ahead
            run[c, j] = ahead
        behind = jnp.zeros((2 * few, length), F32)
        for j in reversed(range(steps)):
            behind = ratio * behind
            run[c, j] += behind
            behind = spec[c, j] + behind
        edges = jnp.where(first, behind + jump * swap(behind), ahead + jump * swap(ahead))
        for tile in range(tiles):
            edge_out[c, tile] = edges[:, tile * LANES : (tile + 1) * LANES]
        for tile in range(tiles):
            target = solver(c, tile)

            @pl.when(gy == target)
            def _():
                pltpu.make_async_copy(edge_out.at[c, tile], edge_in.at[c, gy], edge_recv.at[c]).start()

            @pl.when(gy != target)
            def _():
                pltpu.make_async_remote_copy(
                    src_ref=edge_out.at[c, tile], dst_ref=edge_in.at[c, gy],
                    send_sem=edge_send.at[c], recv_sem=edge_recv.at[c],
                    device_id=(gx, target), device_id_type=MESH,
                ).start()

        return ratio, scale, jump, ahead, behind

    def solve_edges(c):
        tile = lax.rem(gy, n_lo)
        mine = gy // n_lo == lax.rem(tile + 2 * c, n_hi)

        @pl.when(mine)
        def _():
            part = pl.ds(pl.multiple_of(tile * LANES, LANES), LANES)
            ratio, _ = decay(level_sigma(c, line[:, part]))
            hop = power(ratio, rows_y.bit_length() - 1)
            across = power(hop, n_gy.bit_length() - 1)
            wait_for(edge_in.at[c], edge_recv.at[c])
            right = jnp.zeros((2 * few, LANES), F32)
            left = jnp.zeros((2 * few, LANES), F32)
            for b in range(n_gy):
                right = edge_in[c, b] + hop * right
                left = edge_in[c, n_gy - 1 - b] + hop * left
            mirror = 1.0 / (1.0 - across * across)
            right, left = (
                (swap(left) + across * right) * mirror, (swap(right) + across * left) * mirror
            )
            for b in range(n_gy):
                flow_out[c, b, few:, :] = right[few:, :]
                flow_out[c, n_gy - 1 - b, :few, :] = left[:few, :]
                right = edge_in[c, b] + hop * right
                left = edge_in[c, n_gy - 1 - b] + hop * left
            send_gy(
                lambda b: flow_out.at[c, b], flow_in.at[c, tile], flow_send.at[c], flow_recv.at[c]
            )

    def backward(c, ratio, scale, jump, ahead, behind):
        wait_for(flow_in.at[c], flow_recv.at[c])
        flow = jnp.concatenate([flow_in[c, tile] for tile in range(tiles)], axis=1)
        ahead, behind = (
            jnp.where(first, swap(flow), jump * flow + swap(ahead)),
            jnp.where(first, jump * flow + swap(behind), swap(flow)),
        )
        for j in range(steps):
            ahead = ratio * ahead
            run[c, j] += ahead
        for j in reversed(range(steps)):
            behind = ratio * behind
            run[c, j] = (run[c, j] + behind) * scale

        def set_lines(block, value):
            for i in range(TILE // LANES):
                z_out[c, block * 2 + i] = value[:, i * LANES : (i + 1) * LANES].reshape(
                    steps, 2 * few, LANES
                )

        times_table(run[c].reshape(steps * 2 * few, length), c_hi, c_lo, set_lines)
        send_gx(
            lambda a: z_out.at[c, a], phys.at[c, :, pl.ds(gx * own, own), :],
            xb_send.at[c], xb_recv.at[c],
        )

    for c in range(CUTS):
        turn(c)
    kept = []
    for c in range(CUTS):
        wait_for(x_in.at[c], xf_recv.at[c])
        wait_for(rows_in.at[c], rx_recv.at[c])
        add_rows(c)
        if c > 0:
            solve_edges(c - 1)
        kept.append(forward(c))
    for c in range(CUTS):
        if c == CUTS - 1:
            solve_edges(c)
        backward(c, *kept[c])

    out_of = exact(vbas[...], chosen, ((1,), (1,)))
    half_of = (iota((levels, width), 1) // few) % 2
    out_of = jnp.concatenate([jnp.where(half_of == half, out_of, 0.0) for half in range(2)], axis=0)

    def read_phys(j):
        return jnp.concatenate([phys[c, j] for c in range(CUTS)], axis=0)

    def write_out(j, value):
        for half in range(2):
            out[pl.ds(half * steps + j, levels, stride=rows_y), :] = value[
                half * levels : (half + 1) * levels, :
            ]

    for c in range(CUTS):
        wait_for(phys.at[c], xb_recv.at[c])
    mix_lines(out_of, read_phys, write_out)

    wait_for(codes_in.at[pl.ds(0, n_gy - 1)], cy_send)
    wait_for(codes.at[pl.ds(0, n_gx - 1)], cx_send)
    for c in range(CUTS):
        wait_for(got.at[c, pl.ds(0, n_gy - 1)], ry_send.at[c])
        wait_for(rows_in.at[c, pl.ds(0, n_gx - 1)], rx_send.at[c])
        wait_for(x_in.at[c, pl.ds(0, n_gx - 1)], xf_send.at[c])
        wait_for(z_out.at[c, pl.ds(0, n_gx - 1)], xb_send.at[c])
        mine = gy // n_lo == lax.rem(lax.rem(gy, n_lo) + 2 * c, n_hi)

        @pl.when(mine)
        def _():
            wait_for(edge_out.at[c, pl.ds(0, tiles - 1)], edge_send.at[c])
            wait_for(flow_out.at[c, pl.ds(0, n_gy - 1)], flow_send.at[c])

        @pl.when(jnp.logical_not(mine))
        def _():
            wait_for(edge_out.at[c], edge_send.at[c])


def per_device(
    forcing_field, innovations, owner_device, column_index, obs_weight, vert_inverse, vert_basis,
    vert_eigen,
):
    n_gx = lax.axis_size("gx")
    n_gy = lax.axis_size("gy")
    devices = n_gx * n_gy
    levels, rows_y, cols_x = forcing_field.shape
    row_total = innovations.shape[0]
    length = cols_x * n_gx
    (c_hi, c_lo), (t_hi, t_lo), line = wave_tables(length)
    own = levels // n_gx
    steps = rows_y // 2
    few = own // CUTS
    tiles = length // LANES
    vmem = pl.BlockSpec(memory_space=pltpu.VMEM)
    smem = pl.BlockSpec(memory_space=pltpu.SMEM)
    hbm = pl.BlockSpec(memory_space=pl.ANY)
    dma = pltpu.SemaphoreType.DMA

    def buffer(*shape, dtype=F32):
        return pltpu.VMEM(shape, dtype)

    table = buffer(length, length, dtype=BF16)
    out = pl.pallas_call(
        functools.partial(field_kernel, n_gx, n_gy, (4, 8)),
        out_shape=jax.ShapeDtypeStruct((levels * rows_y, cols_x), F32),
        in_specs=[hbm, vmem, vmem, vmem, vmem, vmem, vmem, smem, hbm, hbm, hbm, hbm, vmem],
        out_specs=vmem,
        scratch_shapes=[
            buffer(levels * rows_y, LANES), table, table, table, table,
            buffer(devices, row_total, dtype=BF16),
            buffer(2 * LANES, row_total, dtype=BF16),
            buffer(CUTS, PAIRS, devices, LANES),
            buffer(CUTS, n_gy, PAIRS, n_gx, LANES),
            buffer(CUTS, n_gx, n_gx, 2, 2 * few, LANES),
            buffer(CUTS, n_gx, n_gx, 2, 2 * few, LANES),
            buffer(n_gy, 1, LANES),
            buffer(n_gy, 1, LANES),
            buffer(n_gx * QUADS, LANES),
            buffer(n_gx, n_gx * QUADS, LANES),
            buffer(n_gx, n_gx * QUADS * LANES, 2 * LANES, dtype=BF16),
            buffer(CUTS, steps, n_gx * 2 * few, LANES),
            buffer(CUTS, n_gx, steps, 2 * few, LANES),
            buffer(CUTS, steps, 2 * few, length),
            buffer(CUTS, steps, 2 * few, length),
            buffer(CUTS, tiles, 2 * few, LANES),
            buffer(CUTS, n_gy, 2 * few, LANES),
            buffer(CUTS, n_gy, 2 * few, LANES),
            buffer(CUTS, tiles, 2 * few, LANES),
            buffer(CUTS, n_gx, steps, 2 * few, LANES),
            buffer(CUTS, steps, n_gx * 2 * few, LANES),
            dma((5,)),
            dma(()), dma(()),
            dma(()), dma(()),
            dma((CUTS,)), dma((CUTS,)),
            dma((CUTS,)), dma((CUTS,)),
            dma((CUTS,)), dma((CUTS,)),
            dma((CUTS,)), dma((CUTS,)),
            dma((CUTS,)), dma((CUTS,)),
            dma((CUTS,)), dma((CUTS,)),
        ],
        compiler_params=pltpu.CompilerParams(
            collective_id=0, has_side_effects=True, vmem_limit_bytes=56 * 1024 * 1024
        ),
        name="field_solve",
    )(
        forcing_field.reshape(levels * rows_y, cols_x), innovations.T,
        owner_device.T, column_index.reshape(1, -1), obs_weight,
        vert_inverse, vert_basis, vert_eigen,
        t_hi, t_lo, c_hi, c_lo, line.reshape(1, -1),
    )
    return out.reshape(levels, rows_y, cols_x)


def solution(mesh):
    return jax.shard_map(
        per_device,
        mesh=mesh,
        in_specs=(
            P(None, "gy", "gx"),
            P(("gx", "gy"), None),
            P(("gx", "gy"), None),
            P(("gx", "gy")),
            P(),
            P(),
            P(),
            P(),
        ),
        out_specs=P(None, "gy", "gx"),
        check_vma=False,
    )
```

```python
import functools

import jax
import jax.numpy as jnp
import ml_dtypes
import numpy as np
from jax import lax
from jax.experimental import pallas as pl
from jax.experimental.pallas import tpu as pltpu
from jax.sharding import PartitionSpec as P

MESH = pl.DeviceIdType.MESH
F32 = jnp.float32
BF16 = jnp.bfloat16
LANES = 128
TILE = 256
CUTS = 2
SLOTS = 16
BLOCK_CUTS = 2
QUADS = 4
PAIRS = SLOTS // QUADS


def split_table(table):
    high = table.astype(np.float32).astype(ml_dtypes.bfloat16)
    low = (table - high.astype(np.float64)).astype(np.float32).astype(ml_dtypes.bfloat16)
    return high, low


def wave_tables(length):
    waves = np.arange(length, dtype=np.float64)
    scales = np.where(waves == 0, np.sqrt(1.0 / length), np.sqrt(2.0 / length))
    table = scales[:, None] * np.cos(np.pi * waves[:, None] * (2 * waves + 1) / (2 * length))
    line = 4.0 * np.sin(np.pi * waves / (2.0 * length)) ** 2
    return split_table(table), split_table(table.T), line.astype(np.float32)


def halves(value):
    high = value.astype(BF16)
    low = (value - high.astype(F32)).astype(BF16)
    return high, low


def dot(left, right):
    return jnp.dot(left, right, preferred_element_type=F32)


def dot_nt(left, right):
    return lax.dot_general(left, right, (((1,), (1,)), ((), ())), preferred_element_type=F32)


def wait_for(ref, sem):
    pltpu.make_async_copy(ref, ref, sem).wait()


def power(value, doublings):
    for _ in range(doublings):
        value = value * value
    return value


def decay(sigma):
    root = jnp.sqrt(sigma + 0.25 * sigma * sigma)
    return 1.0 / (1.0 + 0.5 * sigma + root), 0.5 / root


def field_kernel(
    n_gx, n_gy, gy_dims,
    field_hbm, innov, owner, column, weight, vinv, vbas, eigen,
    t_hi_hbm, t_lo_hbm, c_hi_hbm, c_lo_hbm, line,
    out,
    field, t_hi, t_lo, c_hi, c_lo,
    masked, expanded, slots, got, turned, rows_in, codes_out, codes_in, code_lines, codes, hot_x,
    vert, x_in, spec, run, edge_out, edge_in, flow_out, flow_in, z_out, phys,
    load_sem, cy_send, cy_recv, cx_send, cx_recv, ry_send, ry_recv, rx_send, rx_recv,
    xf_send, xf_recv, edge_send, edge_recv, flow_send, flow_recv, xb_send, xb_recv,
):
    gx = lax.axis_index("gx")
    gy = lax.axis_index("gy")
    n_hi, n_lo = gy_dims
    devices = n_gx * n_gy
    levels = vinv.shape[0]
    own = levels // n_gx
    few = own // CUTS
    steps = vert.shape[1]
    rows_y = 2 * steps
    length = t_hi.shape[0]
    chunks = owner.shape[1] // TILE
    tiles = length // LANES

    def iota(shape, axis):
        return lax.broadcasted_iota(jnp.int32, shape, axis)

    def gx_peer(step):
        return lax.rem(gx + step, n_gx)

    def gy_peer(step):
        high = lax.rem(gy // n_lo + step // n_lo, n_hi)
        low = lax.rem(gy + step, n_lo)
        return high * n_lo + low

    loads = [
        pltpu.make_async_copy(source, target, load_sem.at[i])
        for i, (source, target) in enumerate(
            [
                (field_hbm, field), (t_hi_hbm, t_hi), (t_lo_hbm, t_lo), (c_hi_hbm, c_hi),
                (c_lo_hbm, c_lo),
            ]
        )
    ]
    for load in loads:
        load.start()

    barrier = pltpu.get_barrier_semaphore()

    def greet_gx(step, carry):
        pl.semaphore_signal(barrier, inc=1, device_id=(gx_peer(step), gy), device_id_type=MESH)
        return carry

    def greet_gy(step, carry):
        pl.semaphore_signal(barrier, inc=1, device_id=(gx, gy_peer(step)), device_id_type=MESH)
        return carry

    lax.fori_loop(1, n_gy, greet_gy, 0)
    lax.fori_loop(1, n_gx, greet_gx, 0)

    def send_gx(source, target, send_sem, recv_sem):
        pltpu.make_async_copy(source(gx), target, recv_sem).start()

        def one(step, carry):
            peer = gx_peer(step)
            pltpu.make_async_remote_copy(
                src_ref=source(peer), dst_ref=target, send_sem=send_sem, recv_sem=recv_sem,
                device_id=(peer, gy), device_id_type=MESH,
            ).start()
            return carry

        lax.fori_loop(1, n_gx, one, 0)

    def send_gy(source, target, send_sem, recv_sem):
        pltpu.make_async_copy(source(gy), target, recv_sem).start()

        def one(step, carry):
            peer = gy_peer(step)
            pltpu.make_async_remote_copy(
                src_ref=source(peer), dst_ref=target, send_sem=send_sem, recv_sem=recv_sem,
                device_id=(gx, peer), device_id_type=MESH,
            ).start()
            return carry

        lax.fori_loop(1, n_gy, one, 0)

    def exact(left, right, dims):
        return lax.dot_general(
            left, right, (dims, ((), ())), precision=lax.Precision.HIGHEST,
            preferred_element_type=F32,
        )

    side = iota((devices, TILE), 0)

    def lanes_of(chunk):
        return slice(chunk * TILE, (chunk + 1) * TILE)

    def number_rows():
        before = jnp.where(iota((TILE, TILE), 0) < iota((TILE, TILE), 1), 1.0, 0.0).astype(BF16)
        seen = jnp.zeros((devices, 1), F32)
        ranks = []
        for chunk in range(chunks):
            name = owner[:, lanes_of(chunk)]
            peer = lax.rem(name, n_gy) * n_gx + name // n_gy
            hot = jnp.where(side == peer, 1.0, 0.0)
            narrow = hot.astype(BF16)
            earlier = dot(narrow, before) + seen
            ranks.append(jnp.sum(hot * earlier, axis=0, keepdims=True).astype(jnp.int32))
            for pair in range(PAIRS):
                mask = jnp.where(ranks[chunk] // QUADS == pair, 1.0, 0.0).astype(BF16)
                masked[pair, :, lanes_of(chunk)] = narrow * mask
            seen = seen + jnp.sum(hot, axis=1, keepdims=True)
        return ranks

    def place_codes(ranks):
        lane_side = iota((LANES, TILE), 0)
        gy_side = iota((n_gy, TILE), 0)
        high = jnp.zeros((n_gy, LANES), F32)
        low = jnp.zeros((n_gy, LANES), F32)
        for chunk in range(chunks):
            name = owner[:, lanes_of(chunk)]
            rank = ranks[chunk]
            lane = (rank // QUADS * n_gx + name // n_gy) * QUADS + rank % QUADS
            code = column[:, lanes_of(chunk)] + 1
            here = lane_side == lane
            hot = jnp.where(gy_side == lax.rem(name, n_gy), 1.0, 0.0).astype(BF16)
            high += dot_nt(hot, jnp.where(here, (code >> 6).astype(F32), 0.0).astype(BF16))
            low += dot_nt(hot, jnp.where(here, (code & 63).astype(F32), 0.0).astype(BF16))
        codes_out[:, 0, :] = high * 64.0 + low

    def weigh_rows(ranks, c):
        place = iota((LANES, levels), 0)
        pick = place // (QUADS * few) * own + c * few + place % few
        chosen = jnp.where(iota((LANES, levels), 1) == pick, 1.0, 0.0)
        mixed = exact(vinv[...], weight[...], ((1,), (1,)))
        w_hi, w_lo = halves(exact(chosen, mixed, ((1,), (0,))))
        stack = jnp.concatenate([w_hi, w_hi, w_lo], axis=1)
        quad = iota((LANES, TILE), 0) // few % QUADS
        for chunk in range(chunks):
            hi, lo = halves(innov[:, lanes_of(chunk)])
            rows_m = dot(stack, jnp.concatenate([hi, lo, hi], axis=0))
            hi, lo = halves(jnp.where(quad == ranks[chunk] % QUADS, rows_m, 0.0))
            expanded[:LANES, lanes_of(chunk)] = hi
            expanded[LANES:, lanes_of(chunk)] = lo

    def place_rows(c):
        for pair in range(0, PAIRS, 2):
            total = dot_nt(
                masked[pair : pair + 2].reshape(2 * devices, chunks * TILE), expanded[...]
            )
            slots[c, pair : pair + 2] = (total[:, :LANES] + total[:, LANES:]).reshape(
                2, devices, LANES
            )

    ranks = number_rows()
    place_codes(ranks)
    for c in range(CUTS):
        weigh_rows(ranks, c)
        place_rows(c)
        if c == 0:
            pl.semaphore_wait(barrier, n_gx - 1 + n_gy - 1)
            send_gy(lambda b: codes_out.at[b], codes_in.at[gy], cy_send, cy_recv)
        send_gy(
            lambda b: slots.at[c, :, pl.ds(b * n_gx, n_gx), :],
            got.at[c, gy], ry_send.at[c], ry_recv.at[c],
        )

    wait_for(codes_in, cy_recv)
    turned_codes = codes_in[:, 0, :].T
    group = n_gx * QUADS
    code_lines[...] = jnp.concatenate(
        [turned_codes[pair * group : (pair + 1) * group, :] for pair in range(PAIRS)], axis=1
    )
    send_gx(lambda a: code_lines, codes.at[gx], cx_send, cx_recv)
    width = 2 * levels
    place = iota((width, levels), 0)
    pick = place // (2 * few) % n_gx * own + place // (width // CUTS) * few + place % few
    chosen = jnp.where(iota((width, levels), 1) == pick, 1.0, 0.0)
    upper = (place // few) % 2

    def mix_lines(matrix, read, write):
        m_hi, m_lo = halves(matrix)
        stack = jnp.concatenate([m_hi, m_hi, m_lo], axis=1)
        for j in range(0, steps, 2):
            hi, lo = halves(jnp.concatenate([read(j), read(j + 1)], axis=1))
            mixed = dot(stack, jnp.concatenate([hi, lo, hi], axis=0))
            write(j, mixed[:, :LANES])
            write(j + 1, mixed[:, LANES:])

    def read_field(j):
        return jnp.concatenate(
            [field[pl.ds(half * steps + j, levels, stride=rows_y), :] for half in range(2)], axis=0
        )

    def write_vert(j, value):
        for c in range(CUTS):
            vert[c, j] = value[c * levels : (c + 1) * levels, :]

    into = exact(chosen, vinv[...], ((1,), (0,)))
    into = jnp.concatenate([jnp.where(upper == half, into, 0.0) for half in range(2)], axis=1)
    loads[0].wait()
    mix_lines(into, read_field, write_vert)
    for c in range(CUTS):
        send_gx(
            lambda a: vert.at[c, :, pl.ds(a * own, own), :],
            x_in.at[c, gx], xf_send.at[c], xf_recv.at[c],
        )

    parts = n_gx // BLOCK_CUTS

    def turn(c):
        wait_for(got.at[c], ry_recv.at[c])
        lines = got.at[c].reshape(n_gy * PAIRS * n_gx, LANES)
        for h in range(BLOCK_CUTS):
            for block in range(h * parts, (h + 1) * parts):
                flat = jnp.concatenate(
                    [
                        lines[pl.ds(pair * n_gx + block, n_gy, stride=PAIRS * n_gx), :]
                        for pair in range(PAIRS)
                    ],
                    axis=0,
                )
                turned[c, :, block] = flat.T.reshape(n_gx, 2, 2 * few, LANES)
            send_gx(
                lambda a: turned.at[c, a, pl.ds(h * parts, parts)],
                rows_in.at[c, gx, pl.ds(h * parts, parts)],
                rx_send.at[c, h], rx_recv.at[c, h],
            )

    wide = QUADS * LANES
    x_lane = iota((LANES, 2 * LANES), 1).astype(F32)

    def mark_x(a, carry):
        code = codes[a].astype(jnp.int32) - 1
        spot = code // (steps * LANES) * LANES + (code & (LANES - 1))
        spot = jnp.where(code < 0, -1, spot).astype(F32)
        for row in range(n_gx * QUADS):
            block, quad = divmod(row, QUADS)
            down = jnp.broadcast_to(spot[row : row + 1, :], (LANES, LANES)).T
            down = jnp.concatenate([down, down], axis=1)
            rows = pl.ds(pl.multiple_of(a * wide + quad * LANES, LANES), LANES)
            hot_x[block, rows, :] = jnp.where(down == x_lane, 1.0, 0.0).astype(BF16)
        return carry

    turn(0)
    for load in loads[1:]:
        load.wait()
    wait_for(codes, cx_recv)
    lax.fori_loop(0, n_gx, mark_x, 0)
    for c in range(1, CUTS):
        turn(c)

    lower = iota((2 * few, LANES), 0) < few

    def add_rows(c, h):
        def one(block, carry):
            total = jnp.zeros((steps * 2 * few, 2 * LANES), F32)
            for a in range(n_gx):
                pieces = []
                for quad in range(QUADS):
                    data = rows_in[c, a, block, quad // 2]
                    hi = data.astype(BF16).astype(F32)
                    lo = data - hi
                    if quad % 2 == 0:
                        both = jnp.where(lower, hi, pltpu.roll(lo, few, 0))
                    else:
                        both = jnp.where(lower, pltpu.roll(hi, few, 0), lo)
                    code = codes[a, pl.ds(block * QUADS + quad, 1), :].astype(jnp.int32) - 1
                    at = jnp.broadcast_to((code // LANES) & (steps - 1), (2 * few, LANES))
                    pieces.append(
                        jnp.concatenate(
                            [jnp.where(at == j, both, 0.0) for j in range(steps)], axis=0
                        ).astype(BF16)
                    )
                total += dot(
                    jnp.concatenate(pieces, axis=1), hot_x[block, a * wide : (a + 1) * wide, :]
                )
            for j in range(steps):
                both = total[j * 2 * few : (j + 1) * 2 * few, :]
                both = both + pltpu.roll(both, few, 0)
                x_in[c, block, j] += jnp.where(lower, both[:, :LANES], both[:, LANES:])
            return carry

        lax.fori_loop(h * parts, (h + 1) * parts, one, 0)

    def times_table(lines, hi_table, lo_table, write):
        hi, lo = halves(lines)
        for block in range(length // TILE):
            cols = pl.ds(block * TILE, TILE)
            write(
                block,
                dot(hi, hi_table[:, cols]) + dot(lo, hi_table[:, cols]) + dot(hi, lo_table[:, cols]),
            )

    def level_sigma(c, waves):
        row = iota((2 * few, waves.shape[1]), 0) % few
        sigma = jnp.broadcast_to(waves, row.shape)
        for i in range(few):
            sigma = sigma + jnp.where(row == i, eigen[gx * own + c * few + i], 0.0)
        return sigma

    first = iota((2 * few, length), 0) < few

    def swap(value):
        return pltpu.roll(value, few, 0)

    def solver(c, tile):
        return (tile + 2 * c) % n_hi * n_lo + tile

    def forward(c):
        lines = jnp.concatenate(
            [x_in[c, a].reshape(steps * 2 * few, LANES) for a in range(n_gx)], axis=1
        )

        def set_spec(block, value):
            spec[c, :, :, block * TILE : (block + 1) * TILE] = value.reshape(steps, 2 * few, TILE)

        times_table(lines, t_hi, t_lo, set_spec)
        ratio, scale = decay(level_sigma(c, line[...]))
        jump = power(ratio, steps.bit_length() - 1)
        ahead = jnp.zeros((2 * few, length), F32)
        for j in range(steps):
            ahead = spec[c, j] + ratio * ahead
            run[c, j] = ahead
        behind = jnp.zeros((2 * few, length), F32)
        for j in reversed(range(steps)):
            behind = ratio * behind
            run[c, j] += behind
            behind = spec[c, j] + behind
        edges = jnp.where(first, behind + jump * swap(behind), ahead + jump * swap(ahead))
        for tile in range(tiles):
            edge_out[c, tile] = edges[:, tile * LANES : (tile + 1) * LANES]
        for tile in range(tiles):
            target = solver(c, tile)

            @pl.when(gy == target)
            def _():
                pltpu.make_async_copy(edge_out.at[c, tile], edge_in.at[c, gy], edge_recv.at[c]).start()

            @pl.when(gy != target)
            def _():
                pltpu.make_async_remote_copy(
                    src_ref=edge_out.at[c, tile], dst_ref=edge_in.at[c, gy],
                    send_sem=edge_send.at[c], recv_sem=edge_recv.at[c],
                    device_id=(gx, target), device_id_type=MESH,
                ).start()

        return ratio, scale, jump, ahead, behind

    def solve_edges(c):
        tile = lax.rem(gy, n_lo)
        mine = gy // n_lo == lax.rem(tile + 2 * c, n_hi)

        @pl.when(mine)
        def _():
            part = pl.ds(pl.multiple_of(tile * LANES, LANES), LANES)
            ratio, _ = decay(level_sigma(c, line[:, part]))
            hop = power(ratio, rows_y.bit_length() - 1)
            across = power(hop, n_gy.bit_length() - 1)
            wait_for(edge_in.at[c], edge_recv.at[c])
            right = jnp.zeros((2 * few, LANES), F32)
            left = jnp.zeros((2 * few, LANES), F32)
            for b in range(n_gy):
                right = edge_in[c, b] + hop * right
                left = edge_in[c, n_gy - 1 - b] + hop * left
            mirror = 1.0 / (1.0 - across * across)
            right, left = (
                (swap(left) + across * right) * mirror, (swap(right) + across * left) * mirror
            )
            for b in range(n_gy):
                flow_out[c, b, few:, :] = right[few:, :]
                flow_out[c, n_gy - 1 - b, :few, :] = left[:few, :]
                right = edge_in[c, b] + hop * right
                left = edge_in[c, n_gy - 1 - b] + hop * left
            send_gy(
                lambda b: flow_out.at[c, b], flow_in.at[c, tile], flow_send.at[c], flow_recv.at[c]
            )

    def backward(c, ratio, scale, jump, ahead, behind):
        wait_for(flow_in.at[c], flow_recv.at[c])
        flow = jnp.concatenate([flow_in[c, tile] for tile in range(tiles)], axis=1)
        ahead, behind = (
            jnp.where(first, swap(flow), jump * flow + swap(ahead)),
            jnp.where(first, jump * flow + swap(behind), swap(flow)),
        )
        for j in range(steps):
            ahead = ratio * ahead
            run[c, j] += ahead
        for j in reversed(range(steps)):
            behind = ratio * behind
            run[c, j] = (run[c, j] + behind) * scale

        hi, lo = halves(run[c].reshape(steps * 2 * few, length))
        pairs = n_gx // 2
        for step in range(pairs):
            pair = lax.rem(gx // 2 + 1 + step, pairs)
            cols = pl.ds(pl.multiple_of(pair * TILE, TILE), TILE)
            value = dot(hi, c_hi[:, cols]) + dot(lo, c_hi[:, cols]) + dot(hi, c_lo[:, cols])
            for i in range(2):
                z_out[c, pair * 2 + i] = value[:, i * LANES : (i + 1) * LANES].reshape(
                    steps, 2 * few, LANES
                )
            target = phys.at[c, :, pl.ds(gx * own, own), :]
            if step < pairs - 1:
                for i in range(2):
                    peer = pair * 2 + lax.rem(gx + i, 2)
                    pltpu.make_async_remote_copy(
                        src_ref=z_out.at[c, peer], dst_ref=target, send_sem=xb_send.at[c],
                        recv_sem=xb_recv.at[c], device_id=(peer, gy), device_id_type=MESH,
                    ).start()
            else:
                peer = pair * 2 + lax.rem(gx + 1, 2)
                pltpu.make_async_remote_copy(
                    src_ref=z_out.at[c, peer], dst_ref=target, send_sem=xb_send.at[c],
                    recv_sem=xb_recv.at[c], device_id=(peer, gy), device_id_type=MESH,
                ).start()
                pltpu.make_async_copy(z_out.at[c, gx], target, xb_recv.at[c]).start()

    kept = []
    for c in range(CUTS):
        wait_for(x_in.at[c], xf_recv.at[c])
        for h in range(BLOCK_CUTS):
            wait_for(rows_in.at[c, :, pl.ds(h * parts, parts)], rx_recv.at[c, h])
            add_rows(c, h)
        if c > 0:
            solve_edges(c - 1)
        kept.append(forward(c))
    for c in range(CUTS):
        if c == CUTS - 1:
            solve_edges(c)
        backward(c, *kept[c])

    out_of = exact(vbas[...], chosen, ((1,), (1,)))
    half_of = (iota((levels, width), 1) // few) % 2
    out_of = jnp.concatenate([jnp.where(half_of == half, out_of, 0.0) for half in range(2)], axis=0)

    def read_phys(j):
        return jnp.concatenate([phys[c, j] for c in range(CUTS)], axis=0)

    def write_out(j, value):
        for half in range(2):
            out[pl.ds(half * steps + j, levels, stride=rows_y), :] = value[
                half * levels : (half + 1) * levels, :
            ]

    for c in range(CUTS):
        wait_for(phys.at[c], xb_recv.at[c])
    mix_lines(out_of, read_phys, write_out)

    wait_for(codes_in.at[pl.ds(0, n_gy - 1)], cy_send)
    wait_for(codes.at[pl.ds(0, n_gx - 1)], cx_send)
    for c in range(CUTS):
        wait_for(got.at[c, pl.ds(0, n_gy - 1)], ry_send.at[c])
        for h in range(BLOCK_CUTS):
            wait_for(
                rows_in.at[c, pl.ds(0, n_gx - 1), pl.ds(h * parts, parts)], rx_send.at[c, h]
            )
        wait_for(x_in.at[c, pl.ds(0, n_gx - 1)], xf_send.at[c])
        wait_for(z_out.at[c, pl.ds(0, n_gx - 1)], xb_send.at[c])
        mine = gy // n_lo == lax.rem(lax.rem(gy, n_lo) + 2 * c, n_hi)

        @pl.when(mine)
        def _():
            wait_for(edge_out.at[c, pl.ds(0, tiles - 1)], edge_send.at[c])
            wait_for(flow_out.at[c, pl.ds(0, n_gy - 1)], flow_send.at[c])

        @pl.when(jnp.logical_not(mine))
        def _():
            wait_for(edge_out.at[c], edge_send.at[c])


def per_device(
    forcing_field, innovations, owner_device, column_index, obs_weight, vert_inverse, vert_basis,
    vert_eigen,
):
    n_gx = lax.axis_size("gx")
    n_gy = lax.axis_size("gy")
    devices = n_gx * n_gy
    levels, rows_y, cols_x = forcing_field.shape
    row_total = innovations.shape[0]
    length = cols_x * n_gx
    (c_hi, c_lo), (t_hi, t_lo), line = wave_tables(length)
    own = levels // n_gx
    steps = rows_y // 2
    few = own // CUTS
    tiles = length // LANES
    vmem = pl.BlockSpec(memory_space=pltpu.VMEM)
    smem = pl.BlockSpec(memory_space=pltpu.SMEM)
    hbm = pl.BlockSpec(memory_space=pl.ANY)
    dma = pltpu.SemaphoreType.DMA

    def buffer(*shape, dtype=F32):
        return pltpu.VMEM(shape, dtype)

    table = buffer(length, length, dtype=BF16)
    out = pl.pallas_call(
        functools.partial(field_kernel, n_gx, n_gy, (4, 8)),
        out_shape=jax.ShapeDtypeStruct((levels * rows_y, cols_x), F32),
        in_specs=[hbm, vmem, vmem, vmem, vmem, vmem, vmem, smem, hbm, hbm, hbm, hbm, vmem],
        out_specs=vmem,
        scratch_shapes=[
            buffer(levels * rows_y, LANES), table, table, table, table,
            buffer(PAIRS, devices, row_total, dtype=BF16),
            buffer(2 * LANES, row_total, dtype=BF16),
            buffer(CUTS, PAIRS, devices, LANES),
            buffer(CUTS, n_gy, PAIRS, n_gx, LANES),
            buffer(CUTS, n_gx, n_gx, 2, 2 * few, LANES),
            buffer(CUTS, n_gx, n_gx, 2, 2 * few, LANES),
            buffer(n_gy, 1, LANES),
            buffer(n_gy, 1, LANES),
            buffer(n_gx * QUADS, LANES),
            buffer(n_gx, n_gx * QUADS, LANES),
            buffer(n_gx, n_gx * QUADS * LANES, 2 * LANES, dtype=BF16),
            buffer(CUTS, steps, n_gx * 2 * few, LANES),
            buffer(CUTS, n_gx, steps, 2 * few, LANES),
            buffer(CUTS, steps, 2 * few, length),
            buffer(CUTS, steps, 2 * few, length),
            buffer(CUTS, tiles, 2 * few, LANES),
            buffer(CUTS, n_gy, 2 * few, LANES),
            buffer(CUTS, n_gy, 2 * few, LANES),
            buffer(CUTS, tiles, 2 * few, LANES),
            buffer(CUTS, n_gx, steps, 2 * few, LANES),
            buffer(CUTS, steps, n_gx * 2 * few, LANES),
            dma((5,)),
            dma(()), dma(()),
            dma(()), dma(()),
            dma((CUTS,)), dma((CUTS,)),
            dma((CUTS, BLOCK_CUTS)), dma((CUTS, BLOCK_CUTS)),
            dma((CUTS,)), dma((CUTS,)),
            dma((CUTS,)), dma((CUTS,)),
            dma((CUTS,)), dma((CUTS,)),
            dma((CUTS,)), dma((CUTS,)),
        ],
        compiler_params=pltpu.CompilerParams(
            collective_id=0, has_side_effects=True, vmem_limit_bytes=56 * 1024 * 1024
        ),
        name="field_solve",
    )(
        forcing_field.reshape(levels * rows_y, cols_x), innovations.T,
        owner_device.T, column_index.reshape(1, -1), obs_weight,
        vert_inverse, vert_basis, vert_eigen,
        t_hi, t_lo, c_hi, c_lo, line.reshape(1, -1),
    )
    return out.reshape(levels, rows_y, cols_x)


def solution(mesh):
    return jax.shard_map(
        per_device,
        mesh=mesh,
        in_specs=(
            P(None, "gy", "gx"),
            P(("gx", "gy"), None),
            P(("gx", "gy"), None),
            P(("gx", "gy")),
            P(),
            P(),
            P(),
            P(),
        ),
        out_specs=P(None, "gy", "gx"),
        check_vma=False,
    )
```

```python
import functools

import jax
import jax.numpy as jnp
import ml_dtypes
import numpy as np
from jax import lax
from jax.experimental import pallas as pl
from jax.experimental.pallas import tpu as pltpu
from jax.sharding import PartitionSpec as P

MESH = pl.DeviceIdType.MESH
F32 = jnp.float32
BF16 = jnp.bfloat16
LANES = 128
TILE = 256
CUTS = 2
SLOTS = 16
MIX_CUTS = 2
BLOCK_CUTS = 2
QUADS = 4
PAIRS = SLOTS // QUADS


def split_table(table):
    high = table.astype(np.float32).astype(ml_dtypes.bfloat16)
    low = (table - high.astype(np.float64)).astype(np.float32).astype(ml_dtypes.bfloat16)
    return high, low


def wave_tables(length):
    waves = np.arange(length, dtype=np.float64)
    scales = np.where(waves == 0, np.sqrt(1.0 / length), np.sqrt(2.0 / length))
    table = scales[:, None] * np.cos(np.pi * waves[:, None] * (2 * waves + 1) / (2 * length))
    line = 4.0 * np.sin(np.pi * waves / (2.0 * length)) ** 2
    return split_table(table), split_table(table.T), line.astype(np.float32)


def halves(value):
    high = value.astype(BF16)
    low = (value - high.astype(F32)).astype(BF16)
    return high, low


def dot(left, right):
    return jnp.dot(left, right, preferred_element_type=F32)


def dot_nt(left, right):
    return lax.dot_general(left, right, (((1,), (1,)), ((), ())), preferred_element_type=F32)


def wait_for(ref, sem):
    pltpu.make_async_copy(ref, ref, sem).wait()


def power(value, doublings):
    for _ in range(doublings):
        value = value * value
    return value


def decay(sigma):
    root = jnp.sqrt(sigma + 0.25 * sigma * sigma)
    return 1.0 / (1.0 + 0.5 * sigma + root), 0.5 / root


def exact(left, right, dims):
    return lax.dot_general(
        left, right, (dims, ((), ())), precision=lax.Precision.HIGHEST, preferred_element_type=F32
    )


def line_rows(levels, n_gx):
    own, width = levels // n_gx, 2 * levels
    few = own // CUTS
    place = lax.broadcasted_iota(jnp.int32, (width, levels), 0)
    pick = place // (2 * few) % n_gx * own + place // (width // CUTS) * few + place % few
    level = lax.broadcasted_iota(jnp.int32, (width, levels), 1)
    return jnp.where(level == pick, 1.0, 0.0), (place // few) % 2


def mix_lines(matrix, steps, read, write):
    m_hi, m_lo = halves(matrix)
    stack = jnp.concatenate([m_hi, m_hi, m_lo], axis=1)
    for j in range(0, steps, 2):
        hi, lo = halves(jnp.concatenate([read(j), read(j + 1)], axis=1))
        mixed = dot(stack, jnp.concatenate([hi, lo, hi], axis=0))
        write(j, mixed[:, :LANES])
        write(j + 1, mixed[:, LANES:])


def level_kernel(n_gx, vbas, phys, out):
    levels, _, steps, _ = out.shape
    width = 2 * levels
    few = levels // n_gx // CUTS
    chosen, _ = line_rows(levels, n_gx)
    back = exact(vbas[...], chosen, ((1,), (1,)))
    half_of = (lax.broadcasted_iota(jnp.int32, (levels, width), 1) // few) % 2
    back = jnp.concatenate([jnp.where(half_of == half, back, 0.0) for half in range(2)], axis=0)

    def read(j):
        return jnp.concatenate([phys[c, j] for c in range(CUTS)], axis=0)

    def write(j, value):
        for half in range(2):
            out[:, half, j, :] = value[half * levels : (half + 1) * levels, :]

    mix_lines(back, steps, read, write)


def field_kernel(
    n_gx, n_gy, gy_dims,
    field_hbm, innov, owner, column, weight, vinv, eigen,
    t_hi_hbm, t_lo_hbm, c_hi_hbm, c_lo_hbm, line,
    phys,
    field, t_hi, t_lo, c_hi, c_lo,
    masked, expanded, slots, got, turned, rows_in, codes_out, codes_in, code_lines, codes, hot_x,
    vert, x_in, spec, run, edge_out, edge_in, flow_out, flow_in, z_out,
    load_sem, cy_send, cy_recv, cx_send, cx_recv, ry_send, ry_recv, rx_send, rx_recv,
    xf_send, xf_recv, edge_send, edge_recv, flow_send, flow_recv, xb_send, xb_recv,
):
    gx = lax.axis_index("gx")
    gy = lax.axis_index("gy")
    n_hi, n_lo = gy_dims
    devices = n_gx * n_gy
    levels = vinv.shape[0]
    own = levels // n_gx
    few = own // CUTS
    steps = vert.shape[1]
    rows_y = 2 * steps
    length = t_hi.shape[0]
    chunks = owner.shape[1] // TILE
    tiles = length // LANES

    def iota(shape, axis):
        return lax.broadcasted_iota(jnp.int32, shape, axis)

    def gx_peer(step):
        return lax.rem(gx + step, n_gx)

    def gy_peer(step):
        high = lax.rem(gy // n_lo + step // n_lo, n_hi)
        low = lax.rem(gy + step, n_lo)
        return high * n_lo + low

    def hops(step):
        return min(step // n_lo, n_hi - step // n_lo) + min(step % n_lo, n_lo - step % n_lo)

    far_first = sorted(range(1, n_gy), key=hops, reverse=True)
    loads = [
        pltpu.make_async_copy(source, target, load_sem.at[i])
        for i, (source, target) in enumerate(
            [
                (field_hbm, field), (t_hi_hbm, t_hi), (t_lo_hbm, t_lo), (c_hi_hbm, c_hi),
                (c_lo_hbm, c_lo),
            ]
        )
    ]
    for load in loads:
        load.start()

    barrier = pltpu.get_barrier_semaphore()

    def greet_gx(step, carry):
        pl.semaphore_signal(barrier, inc=1, device_id=(gx_peer(step), gy), device_id_type=MESH)
        return carry

    def greet_gy(step, carry):
        pl.semaphore_signal(barrier, inc=1, device_id=(gx, gy_peer(step)), device_id_type=MESH)
        return carry

    lax.fori_loop(1, n_gy, greet_gy, 0)
    lax.fori_loop(1, n_gx, greet_gx, 0)

    def send_gx(source, target, send_sem, recv_sem):
        pltpu.make_async_copy(source(gx), target, recv_sem).start()

        def one(step, carry):
            peer = gx_peer(step)
            pltpu.make_async_remote_copy(
                src_ref=source(peer), dst_ref=target, send_sem=send_sem, recv_sem=recv_sem,
                device_id=(peer, gy), device_id_type=MESH,
            ).start()
            return carry

        lax.fori_loop(1, n_gx, one, 0)

    def send_gy(source, target, send_sem, recv_sem):
        pltpu.make_async_copy(source(gy), target, recv_sem).start()

        def one(step, carry):
            peer = gy_peer(step)
            pltpu.make_async_remote_copy(
                src_ref=source(peer), dst_ref=target, send_sem=send_sem, recv_sem=recv_sem,
                device_id=(gx, peer), device_id_type=MESH,
            ).start()
            return carry

        lax.fori_loop(1, n_gy, one, 0)

    side = iota((devices, TILE), 0)

    def lanes_of(chunk):
        return slice(chunk * TILE, (chunk + 1) * TILE)

    def number_rows():
        before = jnp.where(iota((TILE, TILE), 0) < iota((TILE, TILE), 1), 1.0, 0.0).astype(BF16)
        seen = jnp.zeros((devices, 1), F32)
        ranks = []
        for chunk in range(chunks):
            name = owner[:, lanes_of(chunk)]
            peer = lax.rem(name, n_gy) * n_gx + name // n_gy
            hot = jnp.where(side == peer, 1.0, 0.0)
            narrow = hot.astype(BF16)
            earlier = dot(narrow, before) + seen
            ranks.append(jnp.sum(hot * earlier, axis=0, keepdims=True).astype(jnp.int32))
            for pair in range(PAIRS):
                mask = jnp.where(ranks[chunk] // QUADS == pair, 1.0, 0.0).astype(BF16)
                masked[pair, :, lanes_of(chunk)] = narrow * mask
            seen = seen + jnp.sum(hot, axis=1, keepdims=True)
        return ranks

    def place_codes(ranks):
        lane_side = iota((LANES, TILE), 0)
        gy_side = iota((n_gy, TILE), 0)
        high = jnp.zeros((n_gy, LANES), F32)
        low = jnp.zeros((n_gy, LANES), F32)
        for chunk in range(chunks):
            name = owner[:, lanes_of(chunk)]
            rank = ranks[chunk]
            lane = (rank // QUADS * n_gx + name // n_gy) * QUADS + rank % QUADS
            code = column[:, lanes_of(chunk)] + 1
            here = lane_side == lane
            hot = jnp.where(gy_side == lax.rem(name, n_gy), 1.0, 0.0).astype(BF16)
            high += dot_nt(hot, jnp.where(here, (code >> 6).astype(F32), 0.0).astype(BF16))
            low += dot_nt(hot, jnp.where(here, (code & 63).astype(F32), 0.0).astype(BF16))
        codes_out[:, 0, :] = high * 64.0 + low

    def weigh_rows(ranks, c):
        place = iota((LANES, levels), 0)
        pick = place // (QUADS * few) * own + c * few + place % few
        chosen = jnp.where(iota((LANES, levels), 1) == pick, 1.0, 0.0)
        mixed = exact(vinv[...], weight[...], ((1,), (1,)))
        w_hi, w_lo = halves(exact(chosen, mixed, ((1,), (0,))))
        stack = jnp.concatenate([w_hi, w_hi, w_lo], axis=1)
        quad = iota((LANES, TILE), 0) // few % QUADS
        for chunk in range(chunks):
            hi, lo = halves(innov[:, lanes_of(chunk)])
            rows_m = dot(stack, jnp.concatenate([hi, lo, hi], axis=0))
            hi, lo = halves(jnp.where(quad == ranks[chunk] % QUADS, rows_m, 0.0))
            expanded[:LANES, lanes_of(chunk)] = hi
            expanded[LANES:, lanes_of(chunk)] = lo

    def place_rows(c):
        for pair in range(0, PAIRS, 2):
            total = dot_nt(
                masked[pair : pair + 2].reshape(2 * devices, chunks * TILE), expanded[...]
            )
            slots[c, pair : pair + 2] = (total[:, :LANES] + total[:, LANES:]).reshape(
                2, devices, LANES
            )

    ranks = number_rows()
    place_codes(ranks)
    for c in range(CUTS):
        weigh_rows(ranks, c)
        place_rows(c)
        if c == 0:
            pl.semaphore_wait(barrier, n_gx - 1 + n_gy - 1)
            send_gy(lambda b: codes_out.at[b], codes_in.at[gy], cy_send, cy_recv)
        send_gy(
            lambda b: slots.at[c, :, pl.ds(b * n_gx, n_gx), :],
            got.at[c, gy], ry_send.at[c], ry_recv.at[c],
        )

    wait_for(codes_in, cy_recv)
    turned_codes = codes_in[:, 0, :].T
    group = n_gx * QUADS
    code_lines[...] = jnp.concatenate(
        [turned_codes[pair * group : (pair + 1) * group, :] for pair in range(PAIRS)], axis=1
    )
    send_gx(lambda a: code_lines, codes.at[gx], cx_send, cx_recv)
    width = 2 * levels
    chosen, upper = line_rows(levels, n_gx)

    def read_field(j):
        return jnp.concatenate(
            [field[pl.ds(half * steps + j, levels, stride=rows_y), :] for half in range(2)], axis=0
        )

    def write_vert(j, value):
        for c in range(CUTS):
            vert[c, j] = value[c * levels : (c + 1) * levels, :]

    into = exact(chosen, vinv[...], ((1,), (0,)))
    into = jnp.concatenate([jnp.where(upper == half, into, 0.0) for half in range(2)], axis=1)
    loads[0].wait()
    mix_lines(into, steps, read_field, write_vert)
    for c in range(CUTS):
        send_gx(
            lambda a: vert.at[c, :, pl.ds(a * own, own), :],
            x_in.at[c, gx], xf_send.at[c], xf_recv.at[c],
        )

    parts = n_gx // BLOCK_CUTS

    def turn(c):
        wait_for(got.at[c], ry_recv.at[c])
        lines = got.at[c].reshape(n_gy * PAIRS * n_gx, LANES)
        for h in range(BLOCK_CUTS):
            for block in range(h * parts, (h + 1) * parts):
                flat = jnp.concatenate(
                    [
                        lines[pl.ds(pair * n_gx + block, n_gy, stride=PAIRS * n_gx), :]
                        for pair in range(PAIRS)
                    ],
                    axis=0,
                )
                turned[c, :, block] = flat.T.reshape(n_gx, 2, 2 * few, LANES)
            send_gx(
                lambda a: turned.at[c, a, pl.ds(h * parts, parts)],
                rows_in.at[c, gx, pl.ds(h * parts, parts)],
                rx_send.at[c, h], rx_recv.at[c, h],
            )

    wide = QUADS * LANES
    x_lane = iota((LANES, 2 * LANES), 1).astype(F32)

    def mark_x(a, carry):
        code = codes[a].astype(jnp.int32) - 1
        spot = code // (steps * LANES) * LANES + (code & (LANES - 1))
        spot = jnp.where(code < 0, -1, spot).astype(F32)
        for row in range(n_gx * QUADS):
            block, quad = divmod(row, QUADS)
            down = jnp.broadcast_to(spot[row : row + 1, :], (LANES, LANES)).T
            down = jnp.concatenate([down, down], axis=1)
            rows = pl.ds(pl.multiple_of(a * wide + quad * LANES, LANES), LANES)
            hot_x[block, rows, :] = jnp.where(down == x_lane, 1.0, 0.0).astype(BF16)
        return carry

    turn(0)
    for load in loads[1:]:
        load.wait()
    wait_for(codes, cx_recv)
    lax.fori_loop(0, n_gx, mark_x, 0)
    for c in range(1, CUTS):
        turn(c)

    lower = iota((2 * few, LANES), 0) < few

    def add_rows(c, h):
        def one(block, carry):
            total = jnp.zeros((steps * 2 * few, 2 * LANES), F32)
            for a in range(n_gx):
                pieces = []
                for quad in range(QUADS):
                    data = rows_in[c, a, block, quad // 2]
                    hi = data.astype(BF16).astype(F32)
                    lo = data - hi
                    if quad % 2 == 0:
                        both = jnp.where(lower, hi, pltpu.roll(lo, few, 0))
                    else:
                        both = jnp.where(lower, pltpu.roll(hi, few, 0), lo)
                    code = codes[a, pl.ds(block * QUADS + quad, 1), :].astype(jnp.int32) - 1
                    at = jnp.broadcast_to((code // LANES) & (steps - 1), (2 * few, LANES))
                    pieces.append(
                        jnp.concatenate(
                            [jnp.where(at == j, both, 0.0) for j in range(steps)], axis=0
                        ).astype(BF16)
                    )
                total += dot(
                    jnp.concatenate(pieces, axis=1), hot_x[block, a * wide : (a + 1) * wide, :]
                )
            for j in range(steps):
                both = total[j * 2 * few : (j + 1) * 2 * few, :]
                both = both + pltpu.roll(both, few, 0)
                x_in[c, block, j] += jnp.where(lower, both[:, :LANES], both[:, LANES:])
            return carry

        lax.fori_loop(h * parts, (h + 1) * parts, one, 0)

    def times_table(lines, hi_table, lo_table, write):
        hi, lo = halves(lines)
        for block in range(length // TILE):
            cols = pl.ds(block * TILE, TILE)
            write(
                block,
                dot(hi, hi_table[:, cols]) + dot(lo, hi_table[:, cols]) + dot(hi, lo_table[:, cols]),
            )

    def level_sigma(c, waves):
        row = iota((2 * few, waves.shape[1]), 0) % few
        sigma = jnp.broadcast_to(waves, row.shape)
        for i in range(few):
            sigma = sigma + jnp.where(row == i, eigen[gx * own + c * few + i], 0.0)
        return sigma

    first = iota((2 * few, length), 0) < few

    def swap(value):
        return pltpu.roll(value, few, 0)

    def solver(c, tile):
        return (tile + 2 * c) % n_hi * n_lo + tile

    def forward(c):
        lines = jnp.concatenate(
            [x_in[c, a].reshape(steps * 2 * few, LANES) for a in range(n_gx)], axis=1
        )

        def set_spec(block, value):
            spec[c, :, :, block * TILE : (block + 1) * TILE] = value.reshape(steps, 2 * few, TILE)

        times_table(lines, t_hi, t_lo, set_spec)
        ratio, scale = decay(level_sigma(c, line[...]))
        jump = power(ratio, steps.bit_length() - 1)
        ahead = jnp.zeros((2 * few, length), F32)
        for j in range(steps):
            ahead = spec[c, j] + ratio * ahead
            run[c, j] = ahead
        behind = jnp.zeros((2 * few, length), F32)
        for j in reversed(range(steps)):
            behind = ratio * behind
            run[c, j] += behind
            behind = spec[c, j] + behind
        edges = jnp.where(first, behind + jump * swap(behind), ahead + jump * swap(ahead))
        for tile in range(tiles):
            edge_out[c, tile] = edges[:, tile * LANES : (tile + 1) * LANES]
        for tile in range(tiles):
            target = solver(c, tile)

            @pl.when(gy == target)
            def _():
                pltpu.make_async_copy(edge_out.at[c, tile], edge_in.at[c, gy], edge_recv.at[c]).start()

            @pl.when(gy != target)
            def _():
                pltpu.make_async_remote_copy(
                    src_ref=edge_out.at[c, tile], dst_ref=edge_in.at[c, gy],
                    send_sem=edge_send.at[c], recv_sem=edge_recv.at[c],
                    device_id=(gx, target), device_id_type=MESH,
                ).start()

        return ratio, scale, jump, ahead, behind

    def solve_edges(c):
        tile = lax.rem(gy, n_lo)
        mine = gy // n_lo == lax.rem(tile + 2 * c, n_hi)

        @pl.when(mine)
        def _():
            part = pl.ds(pl.multiple_of(tile * LANES, LANES), LANES)
            ratio, _ = decay(level_sigma(c, line[:, part]))
            hop = power(ratio, rows_y.bit_length() - 1)
            across = power(hop, n_gy.bit_length() - 1)
            wait_for(edge_in.at[c], edge_recv.at[c])
            right = jnp.zeros((2 * few, LANES), F32)
            left = jnp.zeros((2 * few, LANES), F32)
            for b in range(n_gy):
                right = edge_in[c, b] + hop * right
                left = edge_in[c, n_gy - 1 - b] + hop * left
            mirror = 1.0 / (1.0 - across * across)
            right, left = (
                (swap(left) + across * right) * mirror, (swap(right) + across * left) * mirror
            )
            for b in range(n_gy):
                flow_out[c, b, few:, :] = right[few:, :]
                flow_out[c, n_gy - 1 - b, :few, :] = left[:few, :]
                right = edge_in[c, b] + hop * right
                left = edge_in[c, n_gy - 1 - b] + hop * left
            target = flow_in.at[c, tile]
            pltpu.make_async_copy(flow_out.at[c, gy], target, flow_recv.at[c]).start()
            for step in far_first:
                peer = gy_peer(step)
                pltpu.make_async_remote_copy(
                    src_ref=flow_out.at[c, peer], dst_ref=target, send_sem=flow_send.at[c],
                    recv_sem=flow_recv.at[c], device_id=(gx, peer), device_id_type=MESH,
                ).start()

    def backward(c, ratio, scale, jump, ahead, behind):
        wait_for(flow_in.at[c], flow_recv.at[c])
        flow = jnp.concatenate([flow_in[c, tile] for tile in range(tiles)], axis=1)
        ahead, behind = (
            jnp.where(first, swap(flow), jump * flow + swap(ahead)),
            jnp.where(first, jump * flow + swap(behind), swap(flow)),
        )
        for j in range(steps):
            ahead = ratio * ahead
            run[c, j] += ahead
        for j in reversed(range(steps)):
            behind = ratio * behind
            run[c, j] = (run[c, j] + behind) * scale

        hi, lo = halves(run[c].reshape(steps * 2 * few, length))
        pairs = n_gx // 2
        for step in range(pairs):
            pair = lax.rem(gx // 2 + 1 + step, pairs)
            cols = pl.ds(pl.multiple_of(pair * TILE, TILE), TILE)
            value = dot(hi, c_hi[:, cols]) + dot(lo, c_hi[:, cols]) + dot(hi, c_lo[:, cols])
            for i in range(2):
                z_out[c, pair * 2 + i] = value[:, i * LANES : (i + 1) * LANES].reshape(
                    steps, 2 * few, LANES
                )
            target = phys.at[c, :, pl.ds(gx * own, own), :]
            if step < pairs - 1:
                for i in range(2):
                    peer = pair * 2 + lax.rem(gx + i, 2)
                    pltpu.make_async_remote_copy(
                        src_ref=z_out.at[c, peer], dst_ref=target, send_sem=xb_send.at[c],
                        recv_sem=xb_recv.at[c], device_id=(peer, gy), device_id_type=MESH,
                    ).start()
            else:
                peer = pair * 2 + lax.rem(gx + 1, 2)
                pltpu.make_async_remote_copy(
                    src_ref=z_out.at[c, peer], dst_ref=target, send_sem=xb_send.at[c],
                    recv_sem=xb_recv.at[c], device_id=(peer, gy), device_id_type=MESH,
                ).start()
                pltpu.make_async_copy(z_out.at[c, gx], target, xb_recv.at[c]).start()

    kept = []
    for c in range(CUTS):
        wait_for(x_in.at[c], xf_recv.at[c])
        for h in range(BLOCK_CUTS):
            wait_for(rows_in.at[c, :, pl.ds(h * parts, parts)], rx_recv.at[c, h])
            add_rows(c, h)
        kept.append(forward(c))
    for c in range(CUTS):
        solve_edges(c)
    for c in range(CUTS):
        backward(c, *kept[c])

    for c in range(CUTS):
        wait_for(phys.at[c], xb_recv.at[c])

    wait_for(codes_in.at[pl.ds(0, n_gy - 1)], cy_send)
    wait_for(codes.at[pl.ds(0, n_gx - 1)], cx_send)
    for c in range(CUTS):
        wait_for(got.at[c, pl.ds(0, n_gy - 1)], ry_send.at[c])
        for h in range(BLOCK_CUTS):
            wait_for(
                rows_in.at[c, pl.ds(0, n_gx - 1), pl.ds(h * parts, parts)], rx_send.at[c, h]
            )
        wait_for(x_in.at[c, pl.ds(0, n_gx - 1)], xf_send.at[c])
        wait_for(z_out.at[c, pl.ds(0, n_gx - 1)], xb_send.at[c])
        mine = gy // n_lo == lax.rem(lax.rem(gy, n_lo) + 2 * c, n_hi)

        @pl.when(mine)
        def _():
            wait_for(edge_out.at[c, pl.ds(0, tiles - 1)], edge_send.at[c])
            wait_for(flow_out.at[c, pl.ds(0, n_gy - 1)], flow_send.at[c])

        @pl.when(jnp.logical_not(mine))
        def _():
            wait_for(edge_out.at[c], edge_send.at[c])


def per_device(
    forcing_field, innovations, owner_device, column_index, obs_weight, vert_inverse, vert_basis,
    vert_eigen,
):
    n_gx = lax.axis_size("gx")
    n_gy = lax.axis_size("gy")
    devices = n_gx * n_gy
    levels, rows_y, cols_x = forcing_field.shape
    row_total = innovations.shape[0]
    length = cols_x * n_gx
    (c_hi, c_lo), (t_hi, t_lo), line = wave_tables(length)
    own = levels // n_gx
    steps = rows_y // 2
    few = own // CUTS
    tiles = length // LANES
    vmem = pl.BlockSpec(memory_space=pltpu.VMEM)
    smem = pl.BlockSpec(memory_space=pltpu.SMEM)
    hbm = pl.BlockSpec(memory_space=pl.ANY)
    dma = pltpu.SemaphoreType.DMA

    def buffer(*shape, dtype=F32):
        return pltpu.VMEM(shape, dtype)

    table = buffer(length, length, dtype=BF16)
    phys = pl.pallas_call(
        functools.partial(field_kernel, n_gx, n_gy, (4, 8)),
        out_shape=jax.ShapeDtypeStruct((CUTS, steps, n_gx * 2 * few, LANES), F32),
        in_specs=[hbm, vmem, vmem, vmem, vmem, vmem, smem, hbm, hbm, hbm, hbm, vmem],
        out_specs=hbm,
        scratch_shapes=[
            buffer(levels * rows_y, LANES), table, table, table, table,
            buffer(PAIRS, devices, row_total, dtype=BF16),
            buffer(2 * LANES, row_total, dtype=BF16),
            buffer(CUTS, PAIRS, devices, LANES),
            buffer(CUTS, n_gy, PAIRS, n_gx, LANES),
            buffer(CUTS, n_gx, n_gx, 2, 2 * few, LANES),
            buffer(CUTS, n_gx, n_gx, 2, 2 * few, LANES),
            buffer(n_gy, 1, LANES),
            buffer(n_gy, 1, LANES),
            buffer(n_gx * QUADS, LANES),
            buffer(n_gx, n_gx * QUADS, LANES),
            buffer(n_gx, n_gx * QUADS * LANES, 2 * LANES, dtype=BF16),
            buffer(CUTS, steps, n_gx * 2 * few, LANES),
            buffer(CUTS, n_gx, steps, 2 * few, LANES),
            buffer(CUTS, steps, 2 * few, length),
            buffer(CUTS, steps, 2 * few, length),
            buffer(CUTS, tiles, 2 * few, LANES),
            buffer(CUTS, n_gy, 2 * few, LANES),
            buffer(CUTS, n_gy, 2 * few, LANES),
            buffer(CUTS, tiles, 2 * few, LANES),
            buffer(CUTS, n_gx, steps, 2 * few, LANES),
            dma((5,)),
            dma(()), dma(()),
            dma(()), dma(()),
            dma((CUTS,)), dma((CUTS,)),
            dma((CUTS, BLOCK_CUTS)), dma((CUTS, BLOCK_CUTS)),
            dma((CUTS,)), dma((CUTS,)),
            dma((CUTS,)), dma((CUTS,)),
            dma((CUTS,)), dma((CUTS,)),
            dma((CUTS,)), dma((CUTS,)),
        ],
        compiler_params=pltpu.CompilerParams(
            collective_id=0, has_side_effects=True, vmem_limit_bytes=56 * 1024 * 1024
        ),
        name="field_solve",
    )(
        forcing_field.reshape(levels * rows_y, cols_x), innovations.T,
        owner_device.T, column_index.reshape(1, -1), obs_weight,
        vert_inverse, vert_eigen,
        t_hi, t_lo, c_hi, c_lo, line.reshape(1, -1),
    )
    part = steps // MIX_CUTS
    out = pl.pallas_call(
        functools.partial(level_kernel, n_gx),
        grid=(MIX_CUTS,),
        out_shape=jax.ShapeDtypeStruct((levels, 2, steps, cols_x), F32),
        in_specs=[
            pl.BlockSpec((levels, levels), lambda i: (0, 0)),
            pl.BlockSpec((CUTS, part, n_gx * 2 * few, LANES), lambda i: (0, i, 0, 0)),
        ],
        out_specs=pl.BlockSpec((levels, 2, part, cols_x), lambda i: (0, 0, i, 0)),
        compiler_params=pltpu.CompilerParams(vmem_limit_bytes=56 * 1024 * 1024),
        name="levels_back",
    )(vert_basis, phys)
    return out.reshape(levels, rows_y, cols_x)


def solution(mesh):
    return jax.shard_map(
        per_device,
        mesh=mesh,
        in_specs=(
            P(None, "gy", "gx"),
            P(("gx", "gy"), None),
            P(("gx", "gy"), None),
            P(("gx", "gy")),
            P(),
            P(),
            P(),
            P(),
        ),
        out_specs=P(None, "gy", "gx"),
        check_vma=False,
    )
```

```python
import functools

import jax
import jax.numpy as jnp
import ml_dtypes
import numpy as np
from jax import lax
from jax.experimental import pallas as pl
from jax.experimental.pallas import tpu as pltpu
from jax.sharding import PartitionSpec as P

MESH = pl.DeviceIdType.MESH
F32 = jnp.float32
BF16 = jnp.bfloat16
LANES = 128
TILE = 256
CUTS = 2
SLOTS = 16
MIX_CUTS = 2
BLOCK_CUTS = 2
QUADS = 4
PAIRS = SLOTS // QUADS


def split_table(table):
    high = table.astype(np.float32).astype(ml_dtypes.bfloat16)
    low = (table - high.astype(np.float64)).astype(np.float32).astype(ml_dtypes.bfloat16)
    return high, low


def wave_tables(length):
    waves = np.arange(length, dtype=np.float64)
    scales = np.where(waves == 0, np.sqrt(1.0 / length), np.sqrt(2.0 / length))
    table = scales[:, None] * np.cos(np.pi * waves[:, None] * (2 * waves + 1) / (2 * length))
    line = 4.0 * np.sin(np.pi * waves / (2.0 * length)) ** 2
    return split_table(table), split_table(table.T), line.astype(np.float32)


def halves(value):
    high = value.astype(BF16)
    low = (value - high.astype(F32)).astype(BF16)
    return high, low


def dot(left, right):
    return jnp.dot(left, right, preferred_element_type=F32)


def dot_nt(left, right):
    return lax.dot_general(left, right, (((1,), (1,)), ((), ())), preferred_element_type=F32)


def wait_for(ref, sem):
    pltpu.make_async_copy(ref, ref, sem).wait()


def power(value, doublings):
    for _ in range(doublings):
        value = value * value
    return value


def decay(sigma):
    root = jnp.sqrt(sigma + 0.25 * sigma * sigma)
    return 1.0 / (1.0 + 0.5 * sigma + root), 0.5 / root


def exact(left, right, dims):
    return lax.dot_general(
        left, right, (dims, ((), ())), precision=lax.Precision.HIGHEST, preferred_element_type=F32
    )


def line_rows(levels, n_gx):
    own, width = levels // n_gx, 2 * levels
    few = own // CUTS
    place = lax.broadcasted_iota(jnp.int32, (width, levels), 0)
    pick = place // (2 * few) % n_gx * own + place // (width // CUTS) * few + place % few
    level = lax.broadcasted_iota(jnp.int32, (width, levels), 1)
    return jnp.where(level == pick, 1.0, 0.0), (place // few) % 2


def mix_stack(matrix):
    m_hi, m_lo = halves(matrix)
    return jnp.concatenate([m_hi, m_hi, m_lo], axis=1)


def mix_lines(stack, steps, read, write):
    for j in range(0, steps, 2):
        hi, lo = halves(jnp.concatenate([read(j), read(j + 1)], axis=1))
        mixed = dot(stack, jnp.concatenate([hi, lo, hi], axis=0))
        write(j, mixed[:, :LANES])
        write(j + 1, mixed[:, LANES:])


def level_kernel(back, phys, out):
    levels, _, steps, _ = out.shape

    def read(j):
        return jnp.concatenate([phys[c, j] for c in range(CUTS)], axis=0)

    def write(j, value):
        for half in range(2):
            out[:, half, j, :] = value[half * levels : (half + 1) * levels, :]

    mix_lines(back[...], steps, read, write)


def field_kernel(
    n_gx, n_gy, gy_dims,
    field_hbm, innov, owner, column, weight, vinv, vbas, eigen,
    t_hi_hbm, t_lo_hbm, c_hi_hbm, c_lo_hbm, line,
    phys, back,
    field, t_hi, t_lo, c_hi, c_lo,
    masked, expanded, slots, got, turned, rows_in, codes_out, codes_in, code_lines, codes, hot_x,
    vert, x_in, spec, run, edge_out, edge_in, flow_out, flow_in, z_out,
    load_sem, cy_send, cy_recv, cx_send, cx_recv, ry_send, ry_recv, rx_send, rx_recv,
    xf_send, xf_recv, edge_send, edge_recv, flow_send, flow_recv, xb_send, xb_recv,
):
    gx = lax.axis_index("gx")
    gy = lax.axis_index("gy")
    n_hi, n_lo = gy_dims
    devices = n_gx * n_gy
    levels = vinv.shape[0]
    own = levels // n_gx
    few = own // CUTS
    steps = vert.shape[1]
    rows_y = 2 * steps
    length = t_hi.shape[0]
    chunks = owner.shape[1] // TILE
    tiles = length // LANES

    def iota(shape, axis):
        return lax.broadcasted_iota(jnp.int32, shape, axis)

    def gx_peer(step):
        return lax.rem(gx + step, n_gx)

    def gy_peer(step):
        high = lax.rem(gy // n_lo + step // n_lo, n_hi)
        low = lax.rem(gy + step, n_lo)
        return high * n_lo + low

    def hops(step):
        return min(step // n_lo, n_hi - step // n_lo) + min(step % n_lo, n_lo - step % n_lo)

    far_first = sorted(range(1, n_gy), key=hops, reverse=True)
    loads = [
        pltpu.make_async_copy(source, target, load_sem.at[i])
        for i, (source, target) in enumerate(
            [
                (field_hbm, field), (t_hi_hbm, t_hi), (t_lo_hbm, t_lo), (c_hi_hbm, c_hi),
                (c_lo_hbm, c_lo),
            ]
        )
    ]
    for load in loads:
        load.start()

    barrier = pltpu.get_barrier_semaphore()

    for step in far_first:
        pl.semaphore_signal(barrier, inc=1, device_id=(gx, gy_peer(step)), device_id_type=MESH)
    for step in range(1, n_gx):
        pl.semaphore_signal(barrier, inc=1, device_id=(gx_peer(step), gy), device_id_type=MESH)

    def send_gx(source, target, send_sem, recv_sem):
        for chip, core in ((2, 0), (2, 1), (1, 0), (3, 0), (1, 1), (3, 1), (0, 1)):
            peer = lax.rem(gx // 2 + chip, n_gx // 2) * 2 + lax.rem(gx + core, 2)
            pltpu.make_async_remote_copy(
                src_ref=source(peer), dst_ref=target, send_sem=send_sem, recv_sem=recv_sem,
                device_id=(peer, gy), device_id_type=MESH,
            ).start()
        pltpu.make_async_copy(source(gx), target, recv_sem).start()

    def send_gy(source, target, send_sem, recv_sem):
        pltpu.make_async_copy(source(gy), target, recv_sem).start()

        def one(step, carry):
            peer = gy_peer(step)
            pltpu.make_async_remote_copy(
                src_ref=source(peer), dst_ref=target, send_sem=send_sem, recv_sem=recv_sem,
                device_id=(gx, peer), device_id_type=MESH,
            ).start()
            return carry

        lax.fori_loop(1, n_gy, one, 0)

    side = iota((devices, TILE), 0)

    def lanes_of(chunk):
        return slice(chunk * TILE, (chunk + 1) * TILE)

    def number_rows():
        before = jnp.where(iota((TILE, TILE), 0) < iota((TILE, TILE), 1), 1.0, 0.0).astype(BF16)
        seen = jnp.zeros((devices, 1), F32)
        ranks = []
        for chunk in range(chunks):
            name = owner[:, lanes_of(chunk)]
            peer = lax.rem(name, n_gy) * n_gx + name // n_gy
            hot = jnp.where(side == peer, 1.0, 0.0)
            narrow = hot.astype(BF16)
            earlier = dot(narrow, before) + seen
            ranks.append(jnp.sum(hot * earlier, axis=0, keepdims=True).astype(jnp.int32))
            for pair in range(PAIRS):
                mask = jnp.where(ranks[chunk] // QUADS == pair, 1.0, 0.0).astype(BF16)
                masked[pair, :, lanes_of(chunk)] = narrow * mask
            seen = seen + jnp.sum(hot, axis=1, keepdims=True)
        return ranks

    def place_codes(ranks):
        lane_side = iota((LANES, TILE), 0)
        gy_side = iota((n_gy, TILE), 0)
        high = jnp.zeros((n_gy, LANES), F32)
        low = jnp.zeros((n_gy, LANES), F32)
        for chunk in range(chunks):
            name = owner[:, lanes_of(chunk)]
            rank = ranks[chunk]
            lane = (rank // QUADS * n_gx + name // n_gy) * QUADS + rank % QUADS
            code = column[:, lanes_of(chunk)] + 1
            here = lane_side == lane
            hot = jnp.where(gy_side == lax.rem(name, n_gy), 1.0, 0.0).astype(BF16)
            high += dot_nt(hot, jnp.where(here, (code >> 6).astype(F32), 0.0).astype(BF16))
            low += dot_nt(hot, jnp.where(here, (code & 63).astype(F32), 0.0).astype(BF16))
        codes_out[:, 0, :] = high * 64.0 + low

    def weigh_rows(ranks, c):
        place = iota((LANES, levels), 0)
        pick = place // (QUADS * few) * own + c * few + place % few
        chosen = jnp.where(iota((LANES, levels), 1) == pick, 1.0, 0.0)
        mixed = exact(vinv[...], weight[...], ((1,), (1,)))
        w_hi, w_lo = halves(exact(chosen, mixed, ((1,), (0,))))
        stack = jnp.concatenate([w_hi, w_hi, w_lo], axis=1)
        quad = iota((LANES, TILE), 0) // few % QUADS
        for chunk in range(chunks):
            hi, lo = halves(innov[:, lanes_of(chunk)])
            rows_m = dot(stack, jnp.concatenate([hi, lo, hi], axis=0))
            hi, lo = halves(jnp.where(quad == ranks[chunk] % QUADS, rows_m, 0.0))
            expanded[:LANES, lanes_of(chunk)] = hi
            expanded[LANES:, lanes_of(chunk)] = lo

    def place_rows(c):
        for pair in range(0, PAIRS, 2):
            total = dot_nt(
                masked[pair : pair + 2].reshape(2 * devices, chunks * TILE), expanded[...]
            )
            slots[c, pair : pair + 2] = (total[:, :LANES] + total[:, LANES:]).reshape(
                2, devices, LANES
            )

    ranks = number_rows()
    place_codes(ranks)
    for c in range(CUTS):
        weigh_rows(ranks, c)
        place_rows(c)
        if c == 0:
            pl.semaphore_wait(barrier, n_gx - 1 + n_gy - 1)
            send_gy(lambda b: codes_out.at[b], codes_in.at[gy], cy_send, cy_recv)
        send_gy(
            lambda b: slots.at[c, :, pl.ds(b * n_gx, n_gx), :],
            got.at[c, gy], ry_send.at[c], ry_recv.at[c],
        )

    wait_for(codes_in, cy_recv)
    turned_codes = codes_in[:, 0, :].T
    group = n_gx * QUADS
    code_lines[...] = jnp.concatenate(
        [turned_codes[pair * group : (pair + 1) * group, :] for pair in range(PAIRS)], axis=1
    )
    send_gx(lambda a: code_lines, codes.at[gx], cx_send, cx_recv)
    width = 2 * levels
    chosen, upper = line_rows(levels, n_gx)

    def read_field(j):
        return jnp.concatenate(
            [field[pl.ds(half * steps + j, levels, stride=rows_y), :] for half in range(2)], axis=0
        )

    def write_vert(j, value):
        for c in range(CUTS):
            vert[c, j] = value[c * levels : (c + 1) * levels, :]

    into = exact(chosen, vinv[...], ((1,), (0,)))
    into = jnp.concatenate([jnp.where(upper == half, into, 0.0) for half in range(2)], axis=1)
    loads[0].wait()
    mix_lines(mix_stack(into), steps, read_field, write_vert)
    for c in range(CUTS):
        send_gx(
            lambda a: vert.at[c, :, pl.ds(a * own, own), :],
            x_in.at[c, gx], xf_send.at[c], xf_recv.at[c],
        )

    back_to = exact(vbas[...], chosen, ((1,), (1,)))
    half_of = (iota((levels, width), 1) // few) % 2
    back[...] = mix_stack(
        jnp.concatenate([jnp.where(half_of == half, back_to, 0.0) for half in range(2)], axis=0)
    )

    parts = n_gx // BLOCK_CUTS

    def turn(c):
        wait_for(got.at[c], ry_recv.at[c])
        lines = got.at[c].reshape(n_gy * PAIRS * n_gx, LANES)
        for h in range(BLOCK_CUTS):
            for block in range(h * parts, (h + 1) * parts):
                flat = jnp.concatenate(
                    [
                        lines[pl.ds(pair * n_gx + block, n_gy, stride=PAIRS * n_gx), :]
                        for pair in range(PAIRS)
                    ],
                    axis=0,
                )
                turned[c, :, block] = flat.T.reshape(n_gx, 2, 2 * few, LANES)
            send_gx(
                lambda a: turned.at[c, a, pl.ds(h * parts, parts)],
                rows_in.at[c, gx, pl.ds(h * parts, parts)],
                rx_send.at[c, h], rx_recv.at[c, h],
            )

    wide = QUADS * LANES
    x_lane = iota((LANES, 2 * LANES), 1).astype(F32)

    def mark_x(a, carry):
        code = codes[a].astype(jnp.int32) - 1
        spot = code // (steps * LANES) * LANES + (code & (LANES - 1))
        spot = jnp.where(code < 0, -1, spot).astype(F32)
        for row in range(n_gx * QUADS):
            block, quad = divmod(row, QUADS)
            down = jnp.broadcast_to(spot[row : row + 1, :], (LANES, LANES)).T
            down = jnp.concatenate([down, down], axis=1)
            rows = pl.ds(pl.multiple_of(a * wide + quad * LANES, LANES), LANES)
            hot_x[block, rows, :] = jnp.where(down == x_lane, 1.0, 0.0).astype(BF16)
        return carry

    turn(0)
    for load in loads[1:]:
        load.wait()
    wait_for(codes, cx_recv)
    lax.fori_loop(0, n_gx, mark_x, 0)
    for c in range(1, CUTS):
        turn(c)

    lower = iota((2 * few, LANES), 0) < few

    def add_rows(c, h):
        def one(block, carry):
            total = jnp.zeros((steps * 2 * few, 2 * LANES), F32)
            for a in range(n_gx):
                pieces = []
                for quad in range(QUADS):
                    data = rows_in[c, a, block, quad // 2]
                    hi = data.astype(BF16).astype(F32)
                    lo = data - hi
                    if quad % 2 == 0:
                        both = jnp.where(lower, hi, pltpu.roll(lo, few, 0))
                    else:
                        both = jnp.where(lower, pltpu.roll(hi, few, 0), lo)
                    code = codes[a, pl.ds(block * QUADS + quad, 1), :].astype(jnp.int32) - 1
                    at = jnp.broadcast_to((code // LANES) & (steps - 1), (2 * few, LANES))
                    pieces.append(
                        jnp.concatenate(
                            [jnp.where(at == j, both, 0.0) for j in range(steps)], axis=0
                        ).astype(BF16)
                    )
                total += dot(
                    jnp.concatenate(pieces, axis=1), hot_x[block, a * wide : (a + 1) * wide, :]
                )
            for j in range(steps):
                both = total[j * 2 * few : (j + 1) * 2 * few, :]
                both = both + pltpu.roll(both, few, 0)
                x_in[c, block, j] += jnp.where(lower, both[:, :LANES], both[:, LANES:])
            return carry

        lax.fori_loop(h * parts, (h + 1) * parts, one, 0)

    def times_columns(both, hi_table, lo_table, cols):
        count = both.shape[0] // 2
        value = dot(both, hi_table[:, cols])
        return value[:count] + value[count:] + dot(both[:count], lo_table[:, cols])

    def times_table(lines, hi_table, lo_table, write):
        both = jnp.concatenate(halves(lines), axis=0)
        for block in range(length // TILE):
            write(block, times_columns(both, hi_table, lo_table, pl.ds(block * TILE, TILE)))

    def level_sigma(c, waves):
        row = iota((2 * few, waves.shape[1]), 0) % few
        sigma = jnp.broadcast_to(waves, row.shape)
        for i in range(few):
            sigma = sigma + jnp.where(row == i, eigen[gx * own + c * few + i], 0.0)
        return sigma

    first = iota((2 * few, length), 0) < few

    def swap(value):
        return pltpu.roll(value, few, 0)

    def solver(c, tile):
        return (tile + 2 * c) % n_hi * n_lo + tile

    def forward(c):
        lines = jnp.concatenate(
            [x_in[c, a].reshape(steps * 2 * few, LANES) for a in range(n_gx)], axis=1
        )

        def set_spec(block, value):
            spec[c, :, :, block * TILE : (block + 1) * TILE] = value.reshape(steps, 2 * few, TILE)

        times_table(lines, t_hi, t_lo, set_spec)
        ratio, scale = decay(level_sigma(c, line[...]))
        jump = power(ratio, steps.bit_length() - 1)
        ahead = jnp.zeros((2 * few, length), F32)
        for j in range(steps):
            ahead = spec[c, j] + ratio * ahead
            run[c, j] = ahead
        behind = jnp.zeros((2 * few, length), F32)
        for j in reversed(range(steps)):
            behind = ratio * behind
            run[c, j] += behind
            behind = spec[c, j] + behind
        edges = jnp.where(first, behind + jump * swap(behind), ahead + jump * swap(ahead))
        for tile in range(tiles):
            edge_out[c, tile] = edges[:, tile * LANES : (tile + 1) * LANES]
        for tile in range(tiles):
            target = solver(c, tile)

            @pl.when(gy == target)
            def _():
                pltpu.make_async_copy(edge_out.at[c, tile], edge_in.at[c, gy], edge_recv.at[c]).start()

            @pl.when(gy != target)
            def _():
                pltpu.make_async_remote_copy(
                    src_ref=edge_out.at[c, tile], dst_ref=edge_in.at[c, gy],
                    send_sem=edge_send.at[c], recv_sem=edge_recv.at[c],
                    device_id=(gx, target), device_id_type=MESH,
                ).start()

        return ratio, scale, jump, ahead, behind

    def solve_edges(c):
        tile = lax.rem(gy, n_lo)
        mine = gy // n_lo == lax.rem(tile + 2 * c, n_hi)

        @pl.when(mine)
        def _():
            part = pl.ds(pl.multiple_of(tile * LANES, LANES), LANES)
            ratio, _ = decay(level_sigma(c, line[:, part]))
            hop = power(ratio, rows_y.bit_length() - 1)
            across = power(hop, n_gy.bit_length() - 1)
            wait_for(edge_in.at[c], edge_recv.at[c])
            right = jnp.zeros((2 * few, LANES), F32)
            left = jnp.zeros((2 * few, LANES), F32)
            for b in range(n_gy):
                right = edge_in[c, b] + hop * right
                left = edge_in[c, n_gy - 1 - b] + hop * left
            mirror = 1.0 / (1.0 - across * across)
            right, left = (
                (swap(left) + across * right) * mirror, (swap(right) + across * left) * mirror
            )
            for b in range(n_gy):
                flow_out[c, b, few:, :] = right[few:, :]
                flow_out[c, n_gy - 1 - b, :few, :] = left[:few, :]
                right = edge_in[c, b] + hop * right
                left = edge_in[c, n_gy - 1 - b] + hop * left
            target = flow_in.at[c, tile]
            pltpu.make_async_copy(flow_out.at[c, gy], target, flow_recv.at[c]).start()
            for step in far_first:
                peer = gy_peer(step)
                pltpu.make_async_remote_copy(
                    src_ref=flow_out.at[c, peer], dst_ref=target, send_sem=flow_send.at[c],
                    recv_sem=flow_recv.at[c], device_id=(gx, peer), device_id_type=MESH,
                ).start()

    def backward(c, ratio, scale, jump, ahead, behind):
        wait_for(flow_in.at[c], flow_recv.at[c])
        flow = jnp.concatenate([flow_in[c, tile] for tile in range(tiles)], axis=1)
        ahead, behind = (
            jnp.where(first, swap(flow), jump * flow + swap(ahead)),
            jnp.where(first, jump * flow + swap(behind), swap(flow)),
        )
        for j in range(steps):
            ahead = ratio * ahead
            run[c, j] += ahead
        for j in reversed(range(steps)):
            behind = ratio * behind
            run[c, j] = (run[c, j] + behind) * scale

        both = jnp.concatenate(halves(run[c].reshape(steps * 2 * few, length)), axis=0)
        pairs = n_gx // 2
        for step in range(pairs):
            pair = lax.rem(gx // 2 + 1 + step, pairs)
            cols = pl.ds(pl.multiple_of(pair * TILE, TILE), TILE)
            value = times_columns(both, c_hi, c_lo, cols)
            for i in range(2):
                z_out[c, pair * 2 + i] = value[:, i * LANES : (i + 1) * LANES].reshape(
                    steps, 2 * few, LANES
                )
            target = phys.at[c, :, pl.ds(gx * own, own), :]
            if step < pairs - 1:
                for i in range(2):
                    peer = pair * 2 + lax.rem(gx + i, 2)
                    pltpu.make_async_remote_copy(
                        src_ref=z_out.at[c, peer], dst_ref=target, send_sem=xb_send.at[c],
                        recv_sem=xb_recv.at[c], device_id=(peer, gy), device_id_type=MESH,
                    ).start()
            else:
                peer = pair * 2 + lax.rem(gx + 1, 2)
                pltpu.make_async_remote_copy(
                    src_ref=z_out.at[c, peer], dst_ref=target, send_sem=xb_send.at[c],
                    recv_sem=xb_recv.at[c], device_id=(peer, gy), device_id_type=MESH,
                ).start()
                pltpu.make_async_copy(z_out.at[c, gx], target, xb_recv.at[c]).start()

    kept = []
    for c in range(CUTS):
        wait_for(x_in.at[c], xf_recv.at[c])
        for h in range(BLOCK_CUTS):
            wait_for(rows_in.at[c, :, pl.ds(h * parts, parts)], rx_recv.at[c, h])
            add_rows(c, h)
        kept.append(forward(c))
    for c in range(CUTS):
        solve_edges(c)
    for c in range(CUTS):
        backward(c, *kept[c])

    for c in range(CUTS):
        wait_for(phys.at[c], xb_recv.at[c])

    wait_for(codes_in.at[pl.ds(0, n_gy - 1)], cy_send)
    wait_for(codes.at[pl.ds(0, n_gx - 1)], cx_send)
    for c in range(CUTS):
        wait_for(got.at[c, pl.ds(0, n_gy - 1)], ry_send.at[c])
        for h in range(BLOCK_CUTS):
            wait_for(
                rows_in.at[c, pl.ds(0, n_gx - 1), pl.ds(h * parts, parts)], rx_send.at[c, h]
            )
        wait_for(x_in.at[c, pl.ds(0, n_gx - 1)], xf_send.at[c])
        wait_for(z_out.at[c, pl.ds(0, n_gx - 1)], xb_send.at[c])
        mine = gy // n_lo == lax.rem(lax.rem(gy, n_lo) + 2 * c, n_hi)

        @pl.when(mine)
        def _():
            wait_for(edge_out.at[c, pl.ds(0, tiles - 1)], edge_send.at[c])
            wait_for(flow_out.at[c, pl.ds(0, n_gy - 1)], flow_send.at[c])

        @pl.when(jnp.logical_not(mine))
        def _():
            wait_for(edge_out.at[c], edge_send.at[c])


def per_device(
    forcing_field, innovations, owner_device, column_index, obs_weight, vert_inverse, vert_basis,
    vert_eigen,
):
    n_gx = lax.axis_size("gx")
    n_gy = lax.axis_size("gy")
    devices = n_gx * n_gy
    levels, rows_y, cols_x = forcing_field.shape
    row_total = innovations.shape[0]
    length = cols_x * n_gx
    (c_hi, c_lo), (t_hi, t_lo), line = wave_tables(length)
    own = levels // n_gx
    steps = rows_y // 2
    few = own // CUTS
    tiles = length // LANES
    vmem = pl.BlockSpec(memory_space=pltpu.VMEM)
    smem = pl.BlockSpec(memory_space=pltpu.SMEM)
    hbm = pl.BlockSpec(memory_space=pl.ANY)
    dma = pltpu.SemaphoreType.DMA

    def buffer(*shape, dtype=F32):
        return pltpu.VMEM(shape, dtype)

    table = buffer(length, length, dtype=BF16)
    phys, back = pl.pallas_call(
        functools.partial(field_kernel, n_gx, n_gy, (4, 8)),
        out_shape=(
            jax.ShapeDtypeStruct((CUTS, steps, n_gx * 2 * few, LANES), F32),
            jax.ShapeDtypeStruct((2 * levels, 6 * levels), BF16),
        ),
        in_specs=[hbm, vmem, vmem, vmem, vmem, vmem, vmem, smem, hbm, hbm, hbm, hbm, vmem],
        out_specs=(hbm, vmem),
        scratch_shapes=[
            buffer(levels * rows_y, LANES), table, table, table, table,
            buffer(PAIRS, devices, row_total, dtype=BF16),
            buffer(2 * LANES, row_total, dtype=BF16),
            buffer(CUTS, PAIRS, devices, LANES),
            buffer(CUTS, n_gy, PAIRS, n_gx, LANES),
            buffer(CUTS, n_gx, n_gx, 2, 2 * few, LANES),
            buffer(CUTS, n_gx, n_gx, 2, 2 * few, LANES),
            buffer(n_gy, 1, LANES),
            buffer(n_gy, 1, LANES),
            buffer(n_gx * QUADS, LANES),
            buffer(n_gx, n_gx * QUADS, LANES),
            buffer(n_gx, n_gx * QUADS * LANES, 2 * LANES, dtype=BF16),
            buffer(CUTS, steps, n_gx * 2 * few, LANES),
            buffer(CUTS, n_gx, steps, 2 * few, LANES),
            buffer(CUTS, steps, 2 * few, length),
            buffer(CUTS, steps, 2 * few, length),
            buffer(CUTS, tiles, 2 * few, LANES),
            buffer(CUTS, n_gy, 2 * few, LANES),
            buffer(CUTS, n_gy, 2 * few, LANES),
            buffer(CUTS, tiles, 2 * few, LANES),
            buffer(CUTS, n_gx, steps, 2 * few, LANES),
            dma((5,)),
            dma(()), dma(()),
            dma(()), dma(()),
            dma((CUTS,)), dma((CUTS,)),
            dma((CUTS, BLOCK_CUTS)), dma((CUTS, BLOCK_CUTS)),
            dma((CUTS,)), dma((CUTS,)),
            dma((CUTS,)), dma((CUTS,)),
            dma((CUTS,)), dma((CUTS,)),
            dma((CUTS,)), dma((CUTS,)),
        ],
        compiler_params=pltpu.CompilerParams(
            collective_id=0, has_side_effects=True, vmem_limit_bytes=56 * 1024 * 1024
        ),
        name="field_solve",
    )(
        forcing_field.reshape(levels * rows_y, cols_x), innovations.T,
        owner_device.T, column_index.reshape(1, -1), obs_weight,
        vert_inverse, vert_basis, vert_eigen,
        t_hi, t_lo, c_hi, c_lo, line.reshape(1, -1),
    )
    part = steps // MIX_CUTS
    out = pl.pallas_call(
        level_kernel,
        grid=(MIX_CUTS,),
        out_shape=jax.ShapeDtypeStruct((levels, 2, steps, cols_x), F32),
        in_specs=[
            pl.BlockSpec((2 * levels, 6 * levels), lambda i: (0, 0)),
            pl.BlockSpec((CUTS, part, n_gx * 2 * few, LANES), lambda i: (0, i, 0, 0)),
        ],
        out_specs=pl.BlockSpec((levels, 2, part, cols_x), lambda i: (0, 0, i, 0)),
        compiler_params=pltpu.CompilerParams(vmem_limit_bytes=56 * 1024 * 1024),
        name="levels_back",
    )(back, phys)
    return out.reshape(levels, rows_y, cols_x)


def solution(mesh):
    return jax.shard_map(
        per_device,
        mesh=mesh,
        in_specs=(
            P(None, "gy", "gx"),
            P(("gx", "gy"), None),
            P(("gx", "gy"), None),
            P(("gx", "gy")),
            P(),
            P(),
            P(),
            P(),
        ),
        out_specs=P(None, "gy", "gx"),
        check_vma=False,
    )
```

```python
import functools

import jax
import jax.numpy as jnp
import ml_dtypes
import numpy as np
from jax import lax
from jax.experimental import pallas as pl
from jax.experimental.pallas import tpu as pltpu
from jax.sharding import PartitionSpec as P

MESH = pl.DeviceIdType.MESH
F32 = jnp.float32
BF16 = jnp.bfloat16
LANES = 128
TILE = 256
CUTS = 2
SLOTS = 16
MIX_CUTS = 2
BLOCK_CUTS = 4
QUADS = 4
PAIRS = SLOTS // QUADS


def split_table(table):
    high = table.astype(np.float32).astype(ml_dtypes.bfloat16)
    low = (table - high.astype(np.float64)).astype(np.float32).astype(ml_dtypes.bfloat16)
    return high, low


def wave_tables(length):
    waves = np.arange(length, dtype=np.float64)
    scales = np.where(waves == 0, np.sqrt(1.0 / length), np.sqrt(2.0 / length))
    table = scales[:, None] * np.cos(np.pi * waves[:, None] * (2 * waves + 1) / (2 * length))
    line = 4.0 * np.sin(np.pi * waves / (2.0 * length)) ** 2
    return split_table(table), split_table(table.T), line.astype(np.float32)


def halves(value):
    high = value.astype(BF16)
    low = (value - high.astype(F32)).astype(BF16)
    return high, low


def dot(left, right):
    return jnp.dot(left, right, preferred_element_type=F32)


def dot_nt(left, right):
    return lax.dot_general(left, right, (((1,), (1,)), ((), ())), preferred_element_type=F32)


def wait_for(ref, sem):
    pltpu.make_async_copy(ref, ref, sem).wait()


def power(value, doublings):
    for _ in range(doublings):
        value = value * value
    return value


def decay(sigma):
    root = jnp.sqrt(sigma + 0.25 * sigma * sigma)
    return 1.0 / (1.0 + 0.5 * sigma + root), 0.5 / root


def exact(left, right, dims):
    return lax.dot_general(
        left, right, (dims, ((), ())), precision=lax.Precision.HIGHEST, preferred_element_type=F32
    )


def line_rows(levels, n_gx):
    own, width = levels // n_gx, 2 * levels
    few = own // CUTS
    place = lax.broadcasted_iota(jnp.int32, (width, levels), 0)
    pick = place // (2 * few) % n_gx * own + place // (width // CUTS) * few + place % few
    level = lax.broadcasted_iota(jnp.int32, (width, levels), 1)
    return jnp.where(level == pick, 1.0, 0.0), (place // few) % 2


def mix_stack(matrix):
    m_hi, m_lo = halves(matrix)
    return jnp.concatenate([m_hi, m_hi, m_lo], axis=1)


def mix_lines(stack, steps, read, write):
    for j in range(0, steps, 2):
        hi, lo = halves(jnp.concatenate([read(j), read(j + 1)], axis=1))
        mixed = dot(stack, jnp.concatenate([hi, lo, hi], axis=0))
        write(j, mixed[:, :LANES])
        write(j + 1, mixed[:, LANES:])


def level_kernel(back, phys, out):
    levels, _, steps, _ = out.shape

    def read(j):
        return jnp.concatenate([phys[c, j] for c in range(CUTS)], axis=0)

    def write(j, value):
        for half in range(2):
            out[:, half, j, :] = value[half * levels : (half + 1) * levels, :]

    mix_lines(back[...], steps, read, write)


def field_kernel(
    n_gx, n_gy, gy_dims,
    field_hbm, innov, owner, column, weight, vinv, vbas, eigen,
    t_hi_hbm, t_lo_hbm, c_hi_hbm, c_lo_hbm, line,
    phys, back,
    field, t_hi, t_lo, c_hi, c_lo,
    masked, expanded, slots, got, turned, rows_in, codes_out, codes_in, code_lines, codes, hot_x,
    vert, x_in, spec, run, edge_out, edge_in, flow_out, flow_in, z_out,
    load_sem, cy_send, cy_recv, cx_send, cx_recv, ry_send, ry_recv, rx_send, rx_recv,
    xf_send, xf_recv, edge_send, edge_recv, flow_send, flow_recv, xb_send, xb_recv,
):
    gx = lax.axis_index("gx")
    gy = lax.axis_index("gy")
    n_hi, n_lo = gy_dims
    devices = n_gx * n_gy
    levels = vinv.shape[0]
    own = levels // n_gx
    few = own // CUTS
    steps = vert.shape[1]
    rows_y = 2 * steps
    length = t_hi.shape[0]
    chunks = owner.shape[1] // TILE
    tiles = length // LANES

    def iota(shape, axis):
        return lax.broadcasted_iota(jnp.int32, shape, axis)

    def gx_peer(step):
        return lax.rem(gx + step, n_gx)

    def gy_peer(step):
        high = lax.rem(gy // n_lo + step // n_lo, n_hi)
        low = lax.rem(gy + step, n_lo)
        return high * n_lo + low

    def hops(step):
        high, low = step // n_lo, step % n_lo
        return min(low, n_lo - low), min(high, n_hi - high)

    far_first = sorted(range(1, n_gy), key=hops, reverse=True)
    loads = [
        pltpu.make_async_copy(source, target, load_sem.at[i])
        for i, (source, target) in enumerate(
            [
                (field_hbm, field), (t_hi_hbm, t_hi), (t_lo_hbm, t_lo), (c_hi_hbm, c_hi),
                (c_lo_hbm, c_lo),
            ]
        )
    ]
    for load in loads:
        load.start()

    barrier = pltpu.get_barrier_semaphore()

    for step in far_first:
        pl.semaphore_signal(barrier, inc=1, device_id=(gx, gy_peer(step)), device_id_type=MESH)
    for step in range(1, n_gx):
        pl.semaphore_signal(barrier, inc=1, device_id=(gx_peer(step), gy), device_id_type=MESH)

    def send_gx(source, target, send_sem, recv_sem):
        pltpu.make_async_copy(source(gx), target, recv_sem).start()

        def one(step, carry):
            peer = gx_peer(step)
            pltpu.make_async_remote_copy(
                src_ref=source(peer), dst_ref=target, send_sem=send_sem, recv_sem=recv_sem,
                device_id=(peer, gy), device_id_type=MESH,
            ).start()
            return carry

        lax.fori_loop(1, n_gx, one, 0)

    def send_gy(source, target, send_sem, recv_sem):
        for step in far_first:
            peer = gy_peer(step)
            pltpu.make_async_remote_copy(
                src_ref=source(peer), dst_ref=target, send_sem=send_sem, recv_sem=recv_sem,
                device_id=(gx, peer), device_id_type=MESH,
            ).start()
        pltpu.make_async_copy(source(gy), target, recv_sem).start()

    side = iota((devices, TILE), 0)

    def lanes_of(chunk):
        return slice(chunk * TILE, (chunk + 1) * TILE)

    def number_rows():
        before = jnp.where(iota((TILE, TILE), 0) < iota((TILE, TILE), 1), 1.0, 0.0).astype(BF16)
        seen = jnp.zeros((devices, 1), F32)
        ranks = []
        for chunk in range(chunks):
            name = owner[:, lanes_of(chunk)]
            peer = lax.rem(name, n_gy) * n_gx + name // n_gy
            hot = jnp.where(side == peer, 1.0, 0.0)
            narrow = hot.astype(BF16)
            earlier = dot(narrow, before) + seen
            ranks.append(jnp.sum(hot * earlier, axis=0, keepdims=True).astype(jnp.int32))
            for pair in range(PAIRS):
                mask = jnp.where(ranks[chunk] // QUADS == pair, 1.0, 0.0).astype(BF16)
                masked[pair, :, lanes_of(chunk)] = narrow * mask
            seen = seen + jnp.sum(hot, axis=1, keepdims=True)
        return ranks

    def place_codes(ranks):
        lane_side = iota((LANES, TILE), 0)
        gy_side = iota((n_gy, TILE), 0)
        high = jnp.zeros((n_gy, LANES), F32)
        low = jnp.zeros((n_gy, LANES), F32)
        for chunk in range(chunks):
            name = owner[:, lanes_of(chunk)]
            rank = ranks[chunk]
            lane = (rank // QUADS * n_gx + name // n_gy) * QUADS + rank % QUADS
            code = column[:, lanes_of(chunk)] + 1
            here = lane_side == lane
            hot = jnp.where(gy_side == lax.rem(name, n_gy), 1.0, 0.0).astype(BF16)
            high += dot_nt(hot, jnp.where(here, (code >> 6).astype(F32), 0.0).astype(BF16))
            low += dot_nt(hot, jnp.where(here, (code & 63).astype(F32), 0.0).astype(BF16))
        codes_out[:, 0, :] = high * 64.0 + low

    def weigh_rows(ranks, c):
        place = iota((LANES, levels), 0)
        pick = place // (QUADS * few) * own + c * few + place % few
        chosen = jnp.where(iota((LANES, levels), 1) == pick, 1.0, 0.0)
        mixed = exact(vinv[...], weight[...], ((1,), (1,)))
        w_hi, w_lo = halves(exact(chosen, mixed, ((1,), (0,))))
        stack = jnp.concatenate([w_hi, w_hi, w_lo], axis=1)
        quad = iota((LANES, TILE), 0) // few % QUADS
        for chunk in range(chunks):
            hi, lo = halves(innov[:, lanes_of(chunk)])
            rows_m = dot(stack, jnp.concatenate([hi, lo, hi], axis=0))
            hi, lo = halves(jnp.where(quad == ranks[chunk] % QUADS, rows_m, 0.0))
            expanded[:LANES, lanes_of(chunk)] = hi
            expanded[LANES:, lanes_of(chunk)] = lo

    def place_rows(c):
        for pair in range(0, PAIRS, 2):
            total = dot_nt(
                masked[pair : pair + 2].reshape(2 * devices, chunks * TILE), expanded[...]
            )
            slots[c, pair : pair + 2] = (total[:, :LANES] + total[:, LANES:]).reshape(
                2, devices, LANES
            )

    ranks = number_rows()
    place_codes(ranks)
    for c in range(CUTS):
        weigh_rows(ranks, c)
        place_rows(c)
        if c == 0:
            pl.semaphore_wait(barrier, n_gx - 1 + n_gy - 1)
            send_gy(lambda b: codes_out.at[b], codes_in.at[gy], cy_send, cy_recv)
        send_gy(
            lambda b: slots.at[c, :, pl.ds(b * n_gx, n_gx), :],
            got.at[c, gy], ry_send.at[c], ry_recv.at[c],
        )

    wait_for(codes_in, cy_recv)
    turned_codes = codes_in[:, 0, :].T
    group = n_gx * QUADS
    code_lines[...] = jnp.concatenate(
        [turned_codes[pair * group : (pair + 1) * group, :] for pair in range(PAIRS)], axis=1
    )
    send_gx(lambda a: code_lines, codes.at[gx], cx_send, cx_recv)
    width = 2 * levels
    chosen, upper = line_rows(levels, n_gx)

    def read_field(j):
        return jnp.concatenate(
            [field[pl.ds(half * steps + j, levels, stride=rows_y), :] for half in range(2)], axis=0
        )

    def write_vert(j, value):
        for c in range(CUTS):
            vert[c, j] = value[c * levels : (c + 1) * levels, :]

    into = exact(chosen, vinv[...], ((1,), (0,)))
    into = jnp.concatenate([jnp.where(upper == half, into, 0.0) for half in range(2)], axis=1)
    loads[0].wait()
    mix_lines(mix_stack(into), steps, read_field, write_vert)
    for c in range(CUTS):
        send_gx(
            lambda a: vert.at[c, :, pl.ds(a * own, own), :],
            x_in.at[c, gx], xf_send.at[c], xf_recv.at[c],
        )

    back_to = exact(vbas[...], chosen, ((1,), (1,)))
    half_of = (iota((levels, width), 1) // few) % 2
    back[...] = mix_stack(
        jnp.concatenate([jnp.where(half_of == half, back_to, 0.0) for half in range(2)], axis=0)
    )

    parts = n_gx // BLOCK_CUTS

    def turn(c):
        wait_for(got.at[c], ry_recv.at[c])
        lines = got.at[c].reshape(n_gy * PAIRS * n_gx, LANES)
        for h in range(BLOCK_CUTS):
            for block in range(h * parts, (h + 1) * parts):
                flat = jnp.concatenate(
                    [
                        lines[pl.ds(pair * n_gx + block, n_gy, stride=PAIRS * n_gx), :]
                        for pair in range(PAIRS)
                    ],
                    axis=0,
                )
                turned[c, :, block] = flat.T.reshape(n_gx, 2, 2 * few, LANES)
            send_gx(
                lambda a: turned.at[c, a, pl.ds(h * parts, parts)],
                rows_in.at[c, gx, pl.ds(h * parts, parts)],
                rx_send.at[c, h], rx_recv.at[c, h],
            )

    wide = QUADS * LANES
    x_lane = iota((LANES, 2 * LANES), 1).astype(F32)

    def mark_x(a, carry):
        code = codes[a].astype(jnp.int32) - 1
        spot = code // (steps * LANES) * LANES + (code & (LANES - 1))
        spot = jnp.where(code < 0, -1, spot).astype(F32)
        for row in range(n_gx * QUADS):
            block, quad = divmod(row, QUADS)
            down = jnp.broadcast_to(spot[row : row + 1, :], (LANES, LANES)).T
            down = jnp.concatenate([down, down], axis=1)
            rows = pl.ds(pl.multiple_of(a * wide + quad * LANES, LANES), LANES)
            hot_x[block, rows, :] = jnp.where(down == x_lane, 1.0, 0.0).astype(BF16)
        return carry

    turn(0)
    for load in loads[1:]:
        load.wait()
    wait_for(codes, cx_recv)
    lax.fori_loop(0, n_gx, mark_x, 0)
    for c in range(1, CUTS):
        turn(c)

    lower = iota((2 * few, LANES), 0) < few

    def add_rows(c, h):
        def one(block, carry):
            total = jnp.zeros((steps * 2 * few, 2 * LANES), F32)
            for a in range(n_gx):
                pieces = []
                for quad in range(QUADS):
                    data = rows_in[c, a, block, quad // 2]
                    hi = data.astype(BF16).astype(F32)
                    lo = data - hi
                    if quad % 2 == 0:
                        both = jnp.where(lower, hi, pltpu.roll(lo, few, 0))
                    else:
                        both = jnp.where(lower, pltpu.roll(hi, few, 0), lo)
                    code = codes[a, pl.ds(block * QUADS + quad, 1), :].astype(jnp.int32) - 1
                    at = jnp.broadcast_to((code // LANES) & (steps - 1), (2 * few, LANES))
                    pieces.append(
                        jnp.concatenate(
                            [jnp.where(at == j, both, 0.0) for j in range(steps)], axis=0
                        ).astype(BF16)
                    )
                total += dot(
                    jnp.concatenate(pieces, axis=1), hot_x[block, a * wide : (a + 1) * wide, :]
                )
            for j in range(steps):
                both = total[j * 2 * few : (j + 1) * 2 * few, :]
                both = both + pltpu.roll(both, few, 0)
                x_in[c, block, j] += jnp.where(lower, both[:, :LANES], both[:, LANES:])
            return carry

        lax.fori_loop(h * parts, (h + 1) * parts, one, 0)

    def times_columns(both, hi_table, lo_table, cols):
        count = both.shape[0] // 2
        value = dot(both, hi_table[:, cols])
        return value[:count] + value[count:] + dot(both[:count], lo_table[:, cols])

    def times_table(lines, hi_table, lo_table, write):
        both = jnp.concatenate(halves(lines), axis=0)
        for block in range(length // TILE):
            write(block, times_columns(both, hi_table, lo_table, pl.ds(block * TILE, TILE)))

    def level_sigma(c, waves):
        row = iota((2 * few, waves.shape[1]), 0) % few
        sigma = jnp.broadcast_to(waves, row.shape)
        for i in range(few):
            sigma = sigma + jnp.where(row == i, eigen[gx * own + c * few + i], 0.0)
        return sigma

    first = iota((2 * few, length), 0) < few

    def swap(value):
        return pltpu.roll(value, few, 0)

    def solver(c, tile):
        return (tile + 2 * c) % n_hi * n_lo + tile

    def forward(c):
        lines = jnp.concatenate(
            [x_in[c, a].reshape(steps * 2 * few, LANES) for a in range(n_gx)], axis=1
        )

        def set_spec(block, value):
            spec[c, :, :, block * TILE : (block + 1) * TILE] = value.reshape(steps, 2 * few, TILE)

        times_table(lines, t_hi, t_lo, set_spec)
        ratio, scale = decay(level_sigma(c, line[...]))
        jump = power(ratio, steps.bit_length() - 1)
        ahead = jnp.zeros((2 * few, length), F32)
        for j in range(steps):
            ahead = spec[c, j] + ratio * ahead
            run[c, j] = ahead
        behind = jnp.zeros((2 * few, length), F32)
        for j in reversed(range(steps)):
            behind = ratio * behind
            run[c, j] += behind
            behind = spec[c, j] + behind
        edges = jnp.where(first, behind + jump * swap(behind), ahead + jump * swap(ahead))
        for tile in range(tiles):
            edge_out[c, tile] = edges[:, tile * LANES : (tile + 1) * LANES]
        for tile in range(tiles):
            target = solver(c, tile)

            @pl.when(gy == target)
            def _():
                pltpu.make_async_copy(edge_out.at[c, tile], edge_in.at[c, gy], edge_recv.at[c]).start()

            @pl.when(gy != target)
            def _():
                pltpu.make_async_remote_copy(
                    src_ref=edge_out.at[c, tile], dst_ref=edge_in.at[c, gy],
                    send_sem=edge_send.at[c], recv_sem=edge_recv.at[c],
                    device_id=(gx, target), device_id_type=MESH,
                ).start()

        return ratio, scale, jump, ahead, behind

    def solve_edges(c):
        tile = lax.rem(gy, n_lo)
        mine = gy // n_lo == lax.rem(tile + 2 * c, n_hi)

        @pl.when(mine)
        def _():
            part = pl.ds(pl.multiple_of(tile * LANES, LANES), LANES)
            ratio, _ = decay(level_sigma(c, line[:, part]))
            hop = power(ratio, rows_y.bit_length() - 1)
            across = power(hop, n_gy.bit_length() - 1)
            wait_for(edge_in.at[c], edge_recv.at[c])
            right = jnp.zeros((2 * few, LANES), F32)
            left = jnp.zeros((2 * few, LANES), F32)
            for b in range(n_gy):
                right = edge_in[c, b] + hop * right
                left = edge_in[c, n_gy - 1 - b] + hop * left
            mirror = 1.0 / (1.0 - across * across)
            right, left = (
                (swap(left) + across * right) * mirror, (swap(right) + across * left) * mirror
            )
            for b in range(n_gy):
                flow_out[c, b, few:, :] = right[few:, :]
                flow_out[c, n_gy - 1 - b, :few, :] = left[:few, :]
                right = edge_in[c, b] + hop * right
                left = edge_in[c, n_gy - 1 - b] + hop * left
            send_gy(
                lambda b: flow_out.at[c, b], flow_in.at[c, tile], flow_send.at[c], flow_recv.at[c]
            )

    def backward(c, ratio, scale, jump, ahead, behind):
        wait_for(flow_in.at[c], flow_recv.at[c])
        flow = jnp.concatenate([flow_in[c, tile] for tile in range(tiles)], axis=1)
        ahead, behind = (
            jnp.where(first, swap(flow), jump * flow + swap(ahead)),
            jnp.where(first, jump * flow + swap(behind), swap(flow)),
        )
        for j in range(steps):
            ahead = ratio * ahead
            run[c, j] += ahead
        for j in reversed(range(steps)):
            behind = ratio * behind
            run[c, j] = (run[c, j] + behind) * scale

        both = jnp.concatenate(halves(run[c].reshape(steps * 2 * few, length)), axis=0)
        pairs = n_gx // 2
        for step in range(pairs):
            pair = lax.rem(gx // 2 + 1 + step, pairs)
            cols = pl.ds(pl.multiple_of(pair * TILE, TILE), TILE)
            value = times_columns(both, c_hi, c_lo, cols)
            for i in range(2):
                z_out[c, pair * 2 + i] = value[:, i * LANES : (i + 1) * LANES].reshape(
                    steps, 2 * few, LANES
                )
            target = phys.at[c, :, pl.ds(gx * own, own), :]
            if step < pairs - 1:
                for i in range(2):
                    peer = pair * 2 + lax.rem(gx + i, 2)
                    pltpu.make_async_remote_copy(
                        src_ref=z_out.at[c, peer], dst_ref=target, send_sem=xb_send.at[c],
                        recv_sem=xb_recv.at[c], device_id=(peer, gy), device_id_type=MESH,
                    ).start()
            else:
                peer = pair * 2 + lax.rem(gx + 1, 2)
                pltpu.make_async_remote_copy(
                    src_ref=z_out.at[c, peer], dst_ref=target, send_sem=xb_send.at[c],
                    recv_sem=xb_recv.at[c], device_id=(peer, gy), device_id_type=MESH,
                ).start()
                pltpu.make_async_copy(z_out.at[c, gx], target, xb_recv.at[c]).start()

    kept = []
    for c in range(CUTS):
        wait_for(x_in.at[c], xf_recv.at[c])
        for h in range(BLOCK_CUTS):
            wait_for(rows_in.at[c, :, pl.ds(h * parts, parts)], rx_recv.at[c, h])
            add_rows(c, h)
        kept.append(forward(c))
    for c in range(CUTS):
        solve_edges(c)
    for c in range(CUTS):
        backward(c, *kept[c])

    for c in range(CUTS):
        wait_for(phys.at[c], xb_recv.at[c])

    wait_for(codes_in.at[pl.ds(0, n_gy - 1)], cy_send)
    wait_for(codes.at[pl.ds(0, n_gx - 1)], cx_send)
    for c in range(CUTS):
        wait_for(got.at[c, pl.ds(0, n_gy - 1)], ry_send.at[c])
        for h in range(BLOCK_CUTS):
            wait_for(
                rows_in.at[c, pl.ds(0, n_gx - 1), pl.ds(h * parts, parts)], rx_send.at[c, h]
            )
        wait_for(x_in.at[c, pl.ds(0, n_gx - 1)], xf_send.at[c])
        wait_for(z_out.at[c, pl.ds(0, n_gx - 1)], xb_send.at[c])
        mine = gy // n_lo == lax.rem(lax.rem(gy, n_lo) + 2 * c, n_hi)

        @pl.when(mine)
        def _():
            wait_for(edge_out.at[c, pl.ds(0, tiles - 1)], edge_send.at[c])
            wait_for(flow_out.at[c, pl.ds(0, n_gy - 1)], flow_send.at[c])

        @pl.when(jnp.logical_not(mine))
        def _():
            wait_for(edge_out.at[c], edge_send.at[c])


def per_device(
    forcing_field, innovations, owner_device, column_index, obs_weight, vert_inverse, vert_basis,
    vert_eigen,
):
    n_gx = lax.axis_size("gx")
    n_gy = lax.axis_size("gy")
    devices = n_gx * n_gy
    levels, rows_y, cols_x = forcing_field.shape
    row_total = innovations.shape[0]
    length = cols_x * n_gx
    (c_hi, c_lo), (t_hi, t_lo), line = wave_tables(length)
    own = levels // n_gx
    steps = rows_y // 2
    few = own // CUTS
    tiles = length // LANES
    vmem = pl.BlockSpec(memory_space=pltpu.VMEM)
    smem = pl.BlockSpec(memory_space=pltpu.SMEM)
    hbm = pl.BlockSpec(memory_space=pl.ANY)
    dma = pltpu.SemaphoreType.DMA

    def buffer(*shape, dtype=F32):
        return pltpu.VMEM(shape, dtype)

    table = buffer(length, length, dtype=BF16)
    phys, back = pl.pallas_call(
        functools.partial(field_kernel, n_gx, n_gy, (4, 8)),
        out_shape=(
            jax.ShapeDtypeStruct((CUTS, steps, n_gx * 2 * few, LANES), F32),
            jax.ShapeDtypeStruct((2 * levels, 6 * levels), BF16),
        ),
        in_specs=[hbm, vmem, vmem, vmem, vmem, vmem, vmem, smem, hbm, hbm, hbm, hbm, vmem],
        out_specs=(hbm, vmem),
        scratch_shapes=[
            buffer(levels * rows_y, LANES), table, table, table, table,
            buffer(PAIRS, devices, row_total, dtype=BF16),
            buffer(2 * LANES, row_total, dtype=BF16),
            buffer(CUTS, PAIRS, devices, LANES),
            buffer(CUTS, n_gy, PAIRS, n_gx, LANES),
            buffer(CUTS, n_gx, n_gx, 2, 2 * few, LANES),
            buffer(CUTS, n_gx, n_gx, 2, 2 * few, LANES),
            buffer(n_gy, 1, LANES),
            buffer(n_gy, 1, LANES),
            buffer(n_gx * QUADS, LANES),
            buffer(n_gx, n_gx * QUADS, LANES),
            buffer(n_gx, n_gx * QUADS * LANES, 2 * LANES, dtype=BF16),
            buffer(CUTS, steps, n_gx * 2 * few, LANES),
            buffer(CUTS, n_gx, steps, 2 * few, LANES),
            buffer(CUTS, steps, 2 * few, length),
            buffer(CUTS, steps, 2 * few, length),
            buffer(CUTS, tiles, 2 * few, LANES),
            buffer(CUTS, n_gy, 2 * few, LANES),
            buffer(CUTS, n_gy, 2 * few, LANES),
            buffer(CUTS, tiles, 2 * few, LANES),
            buffer(CUTS, n_gx, steps, 2 * few, LANES),
            dma((5,)),
            dma(()), dma(()),
            dma(()), dma(()),
            dma((CUTS,)), dma((CUTS,)),
            dma((CUTS, BLOCK_CUTS)), dma((CUTS, BLOCK_CUTS)),
            dma((CUTS,)), dma((CUTS,)),
            dma((CUTS,)), dma((CUTS,)),
            dma((CUTS,)), dma((CUTS,)),
            dma((CUTS,)), dma((CUTS,)),
        ],
        compiler_params=pltpu.CompilerParams(
            collective_id=0, has_side_effects=True, vmem_limit_bytes=56 * 1024 * 1024
        ),
        name="field_solve",
    )(
        forcing_field.reshape(levels * rows_y, cols_x), innovations.T,
        owner_device.T, column_index.reshape(1, -1), obs_weight,
        vert_inverse, vert_basis, vert_eigen,
        t_hi, t_lo, c_hi, c_lo, line.reshape(1, -1),
    )
    part = steps // MIX_CUTS
    out = pl.pallas_call(
        level_kernel,
        grid=(MIX_CUTS,),
        out_shape=jax.ShapeDtypeStruct((levels, 2, steps, cols_x), F32),
        in_specs=[
            pl.BlockSpec((2 * levels, 6 * levels), lambda i: (0, 0)),
            pl.BlockSpec((CUTS, part, n_gx * 2 * few, LANES), lambda i: (0, i, 0, 0)),
        ],
        out_specs=pl.BlockSpec((levels, 2, part, cols_x), lambda i: (0, 0, i, 0)),
        compiler_params=pltpu.CompilerParams(vmem_limit_bytes=56 * 1024 * 1024),
        name="levels_back",
    )(back, phys)
    return out.reshape(levels, rows_y, cols_x)


def solution(mesh):
    return jax.shard_map(
        per_device,
        mesh=mesh,
        in_specs=(
            P(None, "gy", "gx"),
            P(("gx", "gy"), None),
            P(("gx", "gy"), None),
            P(("gx", "gy")),
            P(),
            P(),
            P(),
            P(),
        ),
        out_specs=P(None, "gy", "gx"),
        check_vma=False,
    )
```

```python
import functools

import jax
import jax.numpy as jnp
import ml_dtypes
import numpy as np
from jax import lax
from jax.experimental import pallas as pl
from jax.experimental.pallas import tpu as pltpu
from jax.sharding import PartitionSpec as P

MESH = pl.DeviceIdType.MESH
F32 = jnp.float32
BF16 = jnp.bfloat16
LANES = 128
TILE = 256
CUTS = 2
SLOTS = 16
MIX_CUTS = 2
BLOCK_CUTS = 4
QUADS = 4
PAIRS = SLOTS // QUADS


def split_table(table):
    high = table.astype(np.float32).astype(ml_dtypes.bfloat16)
    low = (table - high.astype(np.float64)).astype(np.float32).astype(ml_dtypes.bfloat16)
    return high, low


def wave_tables(length):
    waves = np.arange(length, dtype=np.float64)
    scales = np.where(waves == 0, np.sqrt(1.0 / length), np.sqrt(2.0 / length))
    table = scales[:, None] * np.cos(np.pi * waves[:, None] * (2 * waves + 1) / (2 * length))
    line = 4.0 * np.sin(np.pi * waves / (2.0 * length)) ** 2
    return split_table(table), split_table(table.T), line.astype(np.float32)


def halves(value):
    high = value.astype(BF16)
    low = (value - high.astype(F32)).astype(BF16)
    return high, low


def dot(left, right):
    return jnp.dot(left, right, preferred_element_type=F32)


def dot_nt(left, right):
    return lax.dot_general(left, right, (((1,), (1,)), ((), ())), preferred_element_type=F32)


def wait_for(ref, sem):
    pltpu.make_async_copy(ref, ref, sem).wait()


def power(value, doublings):
    for _ in range(doublings):
        value = value * value
    return value


def decay(sigma):
    root = jnp.sqrt(sigma + 0.25 * sigma * sigma)
    return 1.0 / (1.0 + 0.5 * sigma + root), 0.5 / root


def exact(left, right, dims):
    return lax.dot_general(
        left, right, (dims, ((), ())), precision=lax.Precision.HIGHEST, preferred_element_type=F32
    )


def line_rows(levels, n_gx):
    own, width = levels // n_gx, 2 * levels
    few = own // CUTS
    place = lax.broadcasted_iota(jnp.int32, (width, levels), 0)
    pick = place // (2 * few) % n_gx * own + place // (width // CUTS) * few + place % few
    level = lax.broadcasted_iota(jnp.int32, (width, levels), 1)
    return jnp.where(level == pick, 1.0, 0.0), (place // few) % 2


def mix_stack(matrix):
    m_hi, m_lo = halves(matrix)
    return jnp.concatenate([m_hi, m_hi, m_lo], axis=1)


def mix_lines(stack, steps, read, write):
    for j in range(0, steps, 2):
        hi, lo = halves(jnp.concatenate([read(j), read(j + 1)], axis=1))
        mixed = dot(stack, jnp.concatenate([hi, lo, hi], axis=0))
        write(j, mixed[:, :LANES])
        write(j + 1, mixed[:, LANES:])


def level_kernel(back, phys, out):
    levels, _, steps, _ = out.shape

    def read(j):
        return jnp.concatenate([phys[c, j] for c in range(CUTS)], axis=0)

    def write(j, value):
        for half in range(2):
            out[:, half, j, :] = value[half * levels : (half + 1) * levels, :]

    mix_lines(back[...], steps, read, write)


def field_kernel(
    n_gx, n_gy, gy_dims,
    field_hbm, innov, owner, column, weight, vinv, vbas, eigen,
    t_hi_hbm, t_lo_hbm, c_hi_hbm, c_lo_hbm, line,
    phys, back,
    field, t_hi, t_lo, c_hi, c_lo,
    masked, expanded, slots, got, turned, rows_in, codes_out, codes_in, code_lines, codes, hot_x,
    vert, x_in, spec, run, edge_out, edge_in, flow_out, flow_in, z_out,
    load_sem, cy_send, cy_recv, cx_send, cx_recv, ry_send, ry_recv, rx_send, rx_recv,
    xf_send, xf_recv, edge_send, edge_recv, flow_send, flow_recv, xb_send, xb_recv,
):
    gx = lax.axis_index("gx")
    gy = lax.axis_index("gy")
    n_hi, n_lo = gy_dims
    devices = n_gx * n_gy
    levels = vinv.shape[0]
    own = levels // n_gx
    few = own // CUTS
    steps = vert.shape[1]
    rows_y = 2 * steps
    length = t_hi.shape[0]
    chunks = owner.shape[1] // TILE
    tiles = length // LANES

    def iota(shape, axis):
        return lax.broadcasted_iota(jnp.int32, shape, axis)

    def gx_peer(step):
        return lax.rem(gx + step, n_gx)

    def gy_peer(step):
        high = lax.rem(gy // n_lo + step // n_lo, n_hi)
        low = lax.rem(gy + step, n_lo)
        return high * n_lo + low

    def hops(step):
        high, low = step // n_lo, step % n_lo
        return min(low, n_lo - low), min(high, n_hi - high)

    far_first = sorted(range(1, n_gy), key=hops, reverse=True)
    loads = [
        pltpu.make_async_copy(source, target, load_sem.at[i])
        for i, (source, target) in enumerate(
            [
                (field_hbm, field), (t_hi_hbm, t_hi), (t_lo_hbm, t_lo), (c_hi_hbm, c_hi),
                (c_lo_hbm, c_lo),
            ]
        )
    ]
    for load in loads:
        load.start()

    barrier = pltpu.get_barrier_semaphore()

    for step in far_first:
        pl.semaphore_signal(barrier, inc=1, device_id=(gx, gy_peer(step)), device_id_type=MESH)
    for step in range(1, n_gx):
        pl.semaphore_signal(barrier, inc=1, device_id=(gx_peer(step), gy), device_id_type=MESH)

    def send_gx(source, target, send_sem, recv_sem):
        pltpu.make_async_copy(source(gx), target, recv_sem).start()

        def one(step, carry):
            peer = gx_peer(step)
            pltpu.make_async_remote_copy(
                src_ref=source(peer), dst_ref=target, send_sem=send_sem, recv_sem=recv_sem,
                device_id=(peer, gy), device_id_type=MESH,
            ).start()
            return carry

        lax.fori_loop(1, n_gx, one, 0)

    def send_gy(source, target, send_sem, recv_sem):
        for step in far_first:
            peer = gy_peer(step)
            pltpu.make_async_remote_copy(
                src_ref=source(peer), dst_ref=target, send_sem=send_sem, recv_sem=recv_sem,
                device_id=(gx, peer), device_id_type=MESH,
            ).start()
        pltpu.make_async_copy(source(gy), target, recv_sem).start()

    side = iota((devices, TILE), 0)

    def lanes_of(chunk):
        return slice(chunk * TILE, (chunk + 1) * TILE)

    def number_rows():
        before = jnp.where(iota((TILE, TILE), 0) < iota((TILE, TILE), 1), 1.0, 0.0).astype(BF16)
        seen = jnp.zeros((devices, 1), F32)
        ranks = []
        for chunk in range(chunks):
            name = owner[:, lanes_of(chunk)]
            peer = lax.rem(name, n_gy) * n_gx + name // n_gy
            hot = jnp.where(side == peer, 1.0, 0.0)
            narrow = hot.astype(BF16)
            earlier = dot(narrow, before) + seen
            ranks.append(jnp.sum(hot * earlier, axis=0, keepdims=True).astype(jnp.int32))
            for pair in range(PAIRS):
                mask = jnp.where(ranks[chunk] // QUADS == pair, 1.0, 0.0).astype(BF16)
                masked[pair, :, lanes_of(chunk)] = narrow * mask
            seen = seen + jnp.sum(hot, axis=1, keepdims=True)
        return ranks

    def place_codes(ranks):
        lane_side = iota((LANES, TILE), 0)
        gy_side = iota((n_gy, TILE), 0)
        high = jnp.zeros((n_gy, LANES), F32)
        low = jnp.zeros((n_gy, LANES), F32)
        for chunk in range(chunks):
            name = owner[:, lanes_of(chunk)]
            rank = ranks[chunk]
            lane = (rank // QUADS * n_gx + name // n_gy) * QUADS + rank % QUADS
            code = column[:, lanes_of(chunk)] + 1
            here = lane_side == lane
            hot = jnp.where(gy_side == lax.rem(name, n_gy), 1.0, 0.0).astype(BF16)
            high += dot_nt(hot, jnp.where(here, (code >> 6).astype(F32), 0.0).astype(BF16))
            low += dot_nt(hot, jnp.where(here, (code & 63).astype(F32), 0.0).astype(BF16))
        codes_out[:, 0, :] = high * 64.0 + low

    def weigh_rows(ranks, c):
        place = iota((LANES, levels), 0)
        pick = place // (QUADS * few) * own + c * few + place % few
        chosen = jnp.where(iota((LANES, levels), 1) == pick, 1.0, 0.0)
        mixed = exact(vinv[...], weight[...], ((1,), (1,)))
        w_hi, w_lo = halves(exact(chosen, mixed, ((1,), (0,))))
        stack = jnp.concatenate([w_hi, w_hi, w_lo], axis=1)
        quad = iota((LANES, TILE), 0) // few % QUADS
        for chunk in range(chunks):
            hi, lo = halves(innov[:, lanes_of(chunk)])
            rows_m = dot(stack, jnp.concatenate([hi, lo, hi], axis=0))
            hi, lo = halves(jnp.where(quad == ranks[chunk] % QUADS, rows_m, 0.0))
            expanded[:LANES, lanes_of(chunk)] = hi
            expanded[LANES:, lanes_of(chunk)] = lo

    def place_rows(c):
        for pair in range(0, PAIRS, 2):
            total = dot_nt(
                masked[pair : pair + 2].reshape(2 * devices, chunks * TILE), expanded[...]
            )
            slots[c, pair : pair + 2] = (total[:, :LANES] + total[:, LANES:]).reshape(
                2, devices, LANES
            )

    ranks = number_rows()
    place_codes(ranks)
    for c in range(CUTS):
        weigh_rows(ranks, c)
        place_rows(c)
        if c == 0:
            pl.semaphore_wait(barrier, n_gx - 1 + n_gy - 1)
            send_gy(lambda b: codes_out.at[b], codes_in.at[gy], cy_send, cy_recv)
        send_gy(
            lambda b: slots.at[c, :, pl.ds(b * n_gx, n_gx), :],
            got.at[c, gy], ry_send.at[c], ry_recv.at[c],
        )

    wait_for(codes_in, cy_recv)
    turned_codes = codes_in[:, 0, :].T
    group = n_gx * QUADS
    code_lines[...] = jnp.concatenate(
        [turned_codes[pair * group : (pair + 1) * group, :] for pair in range(PAIRS)], axis=1
    )
    send_gx(lambda a: code_lines, codes.at[gx], cx_send, cx_recv)
    width = 2 * levels
    chosen, upper = line_rows(levels, n_gx)

    def read_field(j):
        return jnp.concatenate(
            [field[pl.ds(half * steps + j, levels, stride=rows_y), :] for half in range(2)], axis=0
        )

    def write_vert(j, value):
        for c in range(CUTS):
            vert[c, j] = value[c * levels : (c + 1) * levels, :]

    into = exact(chosen, vinv[...], ((1,), (0,)))
    into = jnp.concatenate([jnp.where(upper == half, into, 0.0) for half in range(2)], axis=1)
    loads[0].wait()
    mix_lines(mix_stack(into), steps, read_field, write_vert)
    for c in range(CUTS):
        send_gx(
            lambda a: vert.at[c, :, pl.ds(a * own, own), :],
            x_in.at[c, gx], xf_send.at[c], xf_recv.at[c],
        )

    back_to = exact(vbas[...], chosen, ((1,), (1,)))
    half_of = (iota((levels, width), 1) // few) % 2
    back[...] = mix_stack(
        jnp.concatenate([jnp.where(half_of == half, back_to, 0.0) for half in range(2)], axis=0)
    )

    parts = n_gx // BLOCK_CUTS

    def turn(c):
        wait_for(got.at[c], ry_recv.at[c])
        lines = got.at[c].reshape(n_gy * PAIRS * n_gx, LANES)
        for h in range(BLOCK_CUTS):
            for block in range(h * parts, (h + 1) * parts):
                flat = jnp.concatenate(
                    [
                        lines[pl.ds(pair * n_gx + block, n_gy, stride=PAIRS * n_gx), :]
                        for pair in range(PAIRS)
                    ],
                    axis=0,
                )
                turned[c, :, block] = flat.T.reshape(n_gx, 2, 2 * few, LANES)
            send_gx(
                lambda a: turned.at[c, a, pl.ds(h * parts, parts)],
                rows_in.at[c, gx, pl.ds(h * parts, parts)],
                rx_send.at[c, h], rx_recv.at[c, h],
            )

    wide = QUADS * LANES
    x_lane = iota((LANES, 2 * LANES), 1).astype(F32)

    def mark_x(a, carry):
        code = codes[a].astype(jnp.int32) - 1
        spot = code // (steps * LANES) * LANES + (code & (LANES - 1))
        spot = jnp.where(code < 0, -1, spot).astype(F32)
        for row in range(n_gx * QUADS):
            block, quad = divmod(row, QUADS)
            down = jnp.broadcast_to(spot[row : row + 1, :], (LANES, LANES)).T
            down = jnp.concatenate([down, down], axis=1)
            rows = pl.ds(pl.multiple_of(a * wide + quad * LANES, LANES), LANES)
            hot_x[block, rows, :] = jnp.where(down == x_lane, 1.0, 0.0).astype(BF16)
        return carry

    turn(0)
    for load in loads[1:]:
        load.wait()
    wait_for(codes, cx_recv)
    lax.fori_loop(0, n_gx, mark_x, 0)
    for c in range(1, CUTS):
        turn(c)

    lower = iota((2 * few, LANES), 0) < few

    def add_rows(c, h):
        def one(block, carry):
            total = jnp.zeros((steps * 2 * few, 2 * LANES), F32)
            for a in range(n_gx):
                pieces = []
                for quad in range(QUADS):
                    data = rows_in[c, a, block, quad // 2]
                    hi = data.astype(BF16).astype(F32)
                    lo = data - hi
                    if quad % 2 == 0:
                        both = jnp.where(lower, hi, pltpu.roll(lo, few, 0))
                    else:
                        both = jnp.where(lower, pltpu.roll(hi, few, 0), lo)
                    code = codes[a, pl.ds(block * QUADS + quad, 1), :].astype(jnp.int32) - 1
                    at = jnp.broadcast_to((code // LANES) & (steps - 1), (2 * few, LANES))
                    pieces.append(
                        jnp.concatenate(
                            [jnp.where(at == j, both, 0.0) for j in range(steps)], axis=0
                        ).astype(BF16)
                    )
                total += dot(
                    jnp.concatenate(pieces, axis=1), hot_x[block, a * wide : (a + 1) * wide, :]
                )
            for j in range(steps):
                both = total[j * 2 * few : (j + 1) * 2 * few, :]
                both = both + pltpu.roll(both, few, 0)
                x_in[c, block, j] += jnp.where(lower, both[:, :LANES], both[:, LANES:])
            return carry

        lax.fori_loop(h * parts, (h + 1) * parts, one, 0)

    def times_columns(both, hi_table, lo_table, cols):
        count = both.shape[0] // 2
        value = dot(both, hi_table[:, cols])
        return value[:count] + value[count:] + dot(both[:count], lo_table[:, cols])

    def level_sigma(c, waves):
        row = iota((2 * few, waves.shape[1]), 0) % few
        sigma = jnp.broadcast_to(waves, row.shape)
        for i in range(few):
            sigma = sigma + jnp.where(row == i, eigen[gx * own + c * few + i], 0.0)
        return sigma

    first = iota((2 * few, length), 0) < few

    def swap(value):
        return pltpu.roll(value, few, 0)

    def solver(c, tile):
        return (tile + 2 * c) % n_hi * n_lo + tile

    def forward(c):
        lines = jnp.concatenate(
            [x_in[c, a].reshape(steps * 2 * few, LANES) for a in range(n_gx)], axis=1
        )

        both = jnp.concatenate(halves(lines), axis=0)
        ratio, scale = decay(level_sigma(c, line[...]))
        jump = power(ratio, steps.bit_length() - 1)
        ends = []
        for block in range(length // TILE):
            cols = slice(block * TILE, (block + 1) * TILE)
            rate, skip, low = ratio[:, cols], jump[:, cols], first[:, cols]
            spec[c, :, :, cols] = times_columns(both, t_hi, t_lo, cols).reshape(
                steps, 2 * few, TILE
            )
            ahead = jnp.zeros((2 * few, TILE), F32)
            for j in range(steps):
                ahead = spec[c, j, :, cols] + rate * ahead
                run[c, j, :, cols] = ahead
            behind = jnp.zeros((2 * few, TILE), F32)
            for j in reversed(range(steps)):
                behind = rate * behind
                run[c, j, :, cols] += behind
                behind = spec[c, j, :, cols] + behind
            ends.append((ahead, behind))
            edges = jnp.where(low, behind + skip * swap(behind), ahead + skip * swap(ahead))
            for i in range(TILE // LANES):
                edge_out[c, block * 2 + i] = edges[:, i * LANES : (i + 1) * LANES]
            for tile in range(block * 2, block * 2 + 2):
                target = solver(c, tile)

                @pl.when(gy == target)
                def _():
                    pltpu.make_async_copy(edge_out.at[c, tile], edge_in.at[c, gy], edge_recv.at[c]).start()

                @pl.when(gy != target)
                def _():
                    pltpu.make_async_remote_copy(
                        src_ref=edge_out.at[c, tile], dst_ref=edge_in.at[c, gy],
                        send_sem=edge_send.at[c], recv_sem=edge_recv.at[c],
                        device_id=(gx, target), device_id_type=MESH,
                    ).start()

        ahead, behind = (jnp.concatenate(part, axis=1) for part in zip(*ends))
        return ratio, scale, jump, ahead, behind

    def solve_edges(c):
        tile = lax.rem(gy, n_lo)
        mine = gy // n_lo == lax.rem(tile + 2 * c, n_hi)

        @pl.when(mine)
        def _():
            part = pl.ds(pl.multiple_of(tile * LANES, LANES), LANES)
            ratio, _ = decay(level_sigma(c, line[:, part]))
            hop = power(ratio, rows_y.bit_length() - 1)
            across = power(hop, n_gy.bit_length() - 1)
            wait_for(edge_in.at[c], edge_recv.at[c])
            right = jnp.zeros((2 * few, LANES), F32)
            left = jnp.zeros((2 * few, LANES), F32)
            for b in range(n_gy):
                right = edge_in[c, b] + hop * right
                left = edge_in[c, n_gy - 1 - b] + hop * left
            mirror = 1.0 / (1.0 - across * across)
            right, left = (
                (swap(left) + across * right) * mirror, (swap(right) + across * left) * mirror
            )
            for b in range(n_gy):
                flow_out[c, b, few:, :] = right[few:, :]
                flow_out[c, n_gy - 1 - b, :few, :] = left[:few, :]
                right = edge_in[c, b] + hop * right
                left = edge_in[c, n_gy - 1 - b] + hop * left
            send_gy(
                lambda b: flow_out.at[c, b], flow_in.at[c, tile], flow_send.at[c], flow_recv.at[c]
            )

    def backward(c, ratio, scale, jump, ahead, behind):
        wait_for(flow_in.at[c], flow_recv.at[c])
        flow = jnp.concatenate([flow_in[c, tile] for tile in range(tiles)], axis=1)
        ahead, behind = (
            jnp.where(first, swap(flow), jump * flow + swap(ahead)),
            jnp.where(first, jump * flow + swap(behind), swap(flow)),
        )
        for j in range(steps):
            ahead = ratio * ahead
            run[c, j] += ahead
        for j in reversed(range(steps)):
            behind = ratio * behind
            run[c, j] = (run[c, j] + behind) * scale

        both = jnp.concatenate(halves(run[c].reshape(steps * 2 * few, length)), axis=0)
        pairs = n_gx // 2
        for step in range(pairs):
            pair = lax.rem(gx // 2 + 1 + step, pairs)
            cols = pl.ds(pl.multiple_of(pair * TILE, TILE), TILE)
            value = times_columns(both, c_hi, c_lo, cols)
            for i in range(2):
                z_out[c, pair * 2 + i] = value[:, i * LANES : (i + 1) * LANES].reshape(
                    steps, 2 * few, LANES
                )
            target = phys.at[c, :, pl.ds(gx * own, own), :]
            if step < pairs - 1:
                for i in range(2):
                    peer = pair * 2 + lax.rem(gx + i, 2)
                    pltpu.make_async_remote_copy(
                        src_ref=z_out.at[c, peer], dst_ref=target, send_sem=xb_send.at[c],
                        recv_sem=xb_recv.at[c], device_id=(peer, gy), device_id_type=MESH,
                    ).start()
            else:
                peer = pair * 2 + lax.rem(gx + 1, 2)
                pltpu.make_async_remote_copy(
                    src_ref=z_out.at[c, peer], dst_ref=target, send_sem=xb_send.at[c],
                    recv_sem=xb_recv.at[c], device_id=(peer, gy), device_id_type=MESH,
                ).start()
                pltpu.make_async_copy(z_out.at[c, gx], target, xb_recv.at[c]).start()

    kept = []
    for c in range(CUTS):
        wait_for(x_in.at[c], xf_recv.at[c])
        for h in range(BLOCK_CUTS):
            wait_for(rows_in.at[c, :, pl.ds(h * parts, parts)], rx_recv.at[c, h])
            add_rows(c, h)
        kept.append(forward(c))
    for c in range(CUTS):
        solve_edges(c)
    for c in range(CUTS):
        backward(c, *kept[c])

    for c in range(CUTS):
        wait_for(phys.at[c], xb_recv.at[c])

    wait_for(codes_in.at[pl.ds(0, n_gy - 1)], cy_send)
    wait_for(codes.at[pl.ds(0, n_gx - 1)], cx_send)
    for c in range(CUTS):
        wait_for(got.at[c, pl.ds(0, n_gy - 1)], ry_send.at[c])
        for h in range(BLOCK_CUTS):
            wait_for(
                rows_in.at[c, pl.ds(0, n_gx - 1), pl.ds(h * parts, parts)], rx_send.at[c, h]
            )
        wait_for(x_in.at[c, pl.ds(0, n_gx - 1)], xf_send.at[c])
        wait_for(z_out.at[c, pl.ds(0, n_gx - 1)], xb_send.at[c])
        mine = gy // n_lo == lax.rem(lax.rem(gy, n_lo) + 2 * c, n_hi)

        @pl.when(mine)
        def _():
            wait_for(edge_out.at[c, pl.ds(0, tiles - 1)], edge_send.at[c])
            wait_for(flow_out.at[c, pl.ds(0, n_gy - 1)], flow_send.at[c])

        @pl.when(jnp.logical_not(mine))
        def _():
            wait_for(edge_out.at[c], edge_send.at[c])


def per_device(
    forcing_field, innovations, owner_device, column_index, obs_weight, vert_inverse, vert_basis,
    vert_eigen,
):
    n_gx = lax.axis_size("gx")
    n_gy = lax.axis_size("gy")
    devices = n_gx * n_gy
    levels, rows_y, cols_x = forcing_field.shape
    row_total = innovations.shape[0]
    length = cols_x * n_gx
    (c_hi, c_lo), (t_hi, t_lo), line = wave_tables(length)
    own = levels // n_gx
    steps = rows_y // 2
    few = own // CUTS
    tiles = length // LANES
    vmem = pl.BlockSpec(memory_space=pltpu.VMEM)
    smem = pl.BlockSpec(memory_space=pltpu.SMEM)
    hbm = pl.BlockSpec(memory_space=pl.ANY)
    dma = pltpu.SemaphoreType.DMA

    def buffer(*shape, dtype=F32):
        return pltpu.VMEM(shape, dtype)

    table = buffer(length, length, dtype=BF16)
    phys, back = pl.pallas_call(
        functools.partial(field_kernel, n_gx, n_gy, (4, 8)),
        out_shape=(
            jax.ShapeDtypeStruct((CUTS, steps, n_gx * 2 * few, LANES), F32),
            jax.ShapeDtypeStruct((2 * levels, 6 * levels), BF16),
        ),
        in_specs=[hbm, vmem, vmem, vmem, vmem, vmem, vmem, smem, hbm, hbm, hbm, hbm, vmem],
        out_specs=(hbm, vmem),
        scratch_shapes=[
            buffer(levels * rows_y, LANES), table, table, table, table,
            buffer(PAIRS, devices, row_total, dtype=BF16),
            buffer(2 * LANES, row_total, dtype=BF16),
            buffer(CUTS, PAIRS, devices, LANES),
            buffer(CUTS, n_gy, PAIRS, n_gx, LANES),
            buffer(CUTS, n_gx, n_gx, 2, 2 * few, LANES),
            buffer(CUTS, n_gx, n_gx, 2, 2 * few, LANES),
            buffer(n_gy, 1, LANES),
            buffer(n_gy, 1, LANES),
            buffer(n_gx * QUADS, LANES),
            buffer(n_gx, n_gx * QUADS, LANES),
            buffer(n_gx, n_gx * QUADS * LANES, 2 * LANES, dtype=BF16),
            buffer(CUTS, steps, n_gx * 2 * few, LANES),
            buffer(CUTS, n_gx, steps, 2 * few, LANES),
            buffer(CUTS, steps, 2 * few, length),
            buffer(CUTS, steps, 2 * few, length),
            buffer(CUTS, tiles, 2 * few, LANES),
            buffer(CUTS, n_gy, 2 * few, LANES),
            buffer(CUTS, n_gy, 2 * few, LANES),
            buffer(CUTS, tiles, 2 * few, LANES),
            buffer(CUTS, n_gx, steps, 2 * few, LANES),
            dma((5,)),
            dma(()), dma(()),
            dma(()), dma(()),
            dma((CUTS,)), dma((CUTS,)),
            dma((CUTS, BLOCK_CUTS)), dma((CUTS, BLOCK_CUTS)),
            dma((CUTS,)), dma((CUTS,)),
            dma((CUTS,)), dma((CUTS,)),
            dma((CUTS,)), dma((CUTS,)),
            dma((CUTS,)), dma((CUTS,)),
        ],
        compiler_params=pltpu.CompilerParams(
            collective_id=0, has_side_effects=True, vmem_limit_bytes=56 * 1024 * 1024
        ),
        name="field_solve",
    )(
        forcing_field.reshape(levels * rows_y, cols_x), innovations.T,
        owner_device.T, column_index.reshape(1, -1), obs_weight,
        vert_inverse, vert_basis, vert_eigen,
        t_hi, t_lo, c_hi, c_lo, line.reshape(1, -1),
    )
    part = steps // MIX_CUTS
    out = pl.pallas_call(
        level_kernel,
        grid=(MIX_CUTS,),
        out_shape=jax.ShapeDtypeStruct((levels, 2, steps, cols_x), F32),
        in_specs=[
            pl.BlockSpec((2 * levels, 6 * levels), lambda i: (0, 0)),
            pl.BlockSpec((CUTS, part, n_gx * 2 * few, LANES), lambda i: (0, i, 0, 0)),
        ],
        out_specs=pl.BlockSpec((levels, 2, part, cols_x), lambda i: (0, 0, i, 0)),
        compiler_params=pltpu.CompilerParams(vmem_limit_bytes=56 * 1024 * 1024),
        name="levels_back",
    )(back, phys)
    return out.reshape(levels, rows_y, cols_x)


def solution(mesh):
    return jax.shard_map(
        per_device,
        mesh=mesh,
        in_specs=(
            P(None, "gy", "gx"),
            P(("gx", "gy"), None),
            P(("gx", "gy"), None),
            P(("gx", "gy")),
            P(),
            P(),
            P(),
            P(),
        ),
        out_specs=P(None, "gy", "gx"),
        check_vma=False,
    )
```
